128 devices in a mesh: lon: 64 (over x_hi, z, y, core), lat: 2 (over x_lo).
Axes of the slice: x: 4 (x_hi: 2, x_lo: 2; x = x_hi * 2 + x_lo), y: 4, z: 4, core: 2. Of those that a mesh axis runs over, the one named last changes fastest.
Arguments:
- state_field: bfloat16 [77, 128, 8192], P(None, 'lat', 'lon'), may hold values from -6 to 6
- cotangent: bfloat16 [77, 128, 8192], P(None, 'lat', 'lon'), may hold values from -6 to 6
- land_mask: int32 [128, 8192], P('lat', 'lon'), may hold values 0 or 1
- ocean_slots: int32 [2, 64, 2], P('lat', 'lon'), may hold values from 0 to 1, as said below
- ocean_count: int32 [2, 64], P('lat', 'lon'), may hold values from 0 to 2, as said below
- kernel: bfloat16 [77, 49], replicated, may hold values from -0.875 to 0.875
- norm_gain: bfloat16 [77], replicated, may hold values from 0.5 to 1.5
- norm_bias: bfloat16 [77], replicated, may hold values from -3 to 3
- up_weight: bfloat16 [308, 77], replicated, may hold values from -0.625 to 0.625
- up_bias: bfloat16 [308], replicated, may hold values from -3 to 3
- down_weight: bfloat16 [77, 308], replicated, may hold values from -0.3125 to 0.3125
Outputs:
- field_grad: float32 [77, 128, 8192], P(None, 'lat', 'lon')
- kernel_grad: float32 [77, 49], replicated
- up_grad: float32 [308, 77], replicated
- down_grad: float32 [77, 308], replicated
The draws below stay inside these ranges and needn't reach their ends.
Inputs may be any that keep to these rules, and one draw needn't show every extreme that they name: `ocean_slots`: each tile's row of 2 entries holds every slot once: first its ocean patches in ascending order, then its land patches in ascending order. `ocean_count`: some tile has all 2 patches ocean and some tile none.
All inputs are finite; a program needn't handle non-finite values. No bound on the sum of `land_mask` on one device may be relied on, other than what follows from the above.
Results may differ from the reference program's by a relative error of at most 0.0017.
Values may be sent and summed in bfloat16 or wider, within the bound.
A program may use at most 448 MiB of HBM per device.

```python
import math
import jax
import jax.numpy as jnp
from jax import lax

C = 77
HID = 308
KTAPS = 49
STRIDE = 64
MARGIN = 16
PATCH = 96
PD = 2
LAT_TILES = 2
LON_TILES = 64
NH = 128
NW = 8192


def ocean_lists(key):
    folded = jax.random.fold_in(key, 11)
    draws = jax.random.randint(folded, (LAT_TILES, LON_TILES, PD), 0, 4)
    lon_index = jnp.arange(LON_TILES)[None, :, None]
    slot_index = jnp.arange(PD)[None, None, :]
    limit = jnp.where(lon_index < LON_TILES // 2, 3, 1)
    flags = (draws < limit).astype(jnp.int32)
    flags = jnp.where(lon_index == 0, 1, flags)
    flags = jnp.where((lon_index == LON_TILES - 1) & (slot_index == PD - 1), 1, flags)
    flags = jnp.where((lon_index == 1) & (slot_index == 0), 1, flags)
    flags = jnp.where(lon_index == LON_TILES // 2 + 1, 0, flags)
    counted = jnp.sum(flags, axis=-1).astype(jnp.int32)
    score = (1 - flags) * PD + jnp.arange(PD, dtype=jnp.int32)[None, None, :]
    slots = jnp.argsort(score, axis=-1).astype(jnp.int32)
    return (slots, counted)


def draw_ocean_slots(key, part):
    return ocean_lists(key)[0]


def draw_ocean_count(key, part):
    return ocean_lists(key)[1]


def touch_ends(result, stream_key, smallest, top_value):
    longest = result.shape.index(max(result.shape))
    spots = []
    for shift in (0, 1):
        where = [jax.random.randint(jax.random.fold_in(stream_key, axis), (), 0, length) for axis, length in enumerate(result.shape)]
        where[longest] = (where[longest] + shift) % result.shape[longest]
        spots.append(tuple(where))
    return result.at[spots[0]].set(smallest).at[spots[1]].set(top_value)


def block_scale(stream_key, shape, split, smallest, high):
    def one(dim, shards_of):
        steps = jax.random.uniform(jax.random.fold_in(jax.random.fold_in(stream_key, 6), dim), (shards_of,), jnp.float32, smallest / len(split), high / len(split))
        return jnp.repeat(jnp.exp(steps), shape[dim] // shards_of).reshape((-1,) + (1,) * (len(shape) - dim - 1))

    loudness = one(*split[0])
    for cut in split[1:]:
        loudness = loudness * one(*cut)
    return loudness


def scatter_about(stream_key, shape, deviation, bound, shards=(), kind=jnp.bfloat16):
    gain = block_scale(stream_key, shape, shards, -0.22, 0.18) if shards else 1.0
    drawn = jax.random.normal(stream_key, shape, jnp.float32) * deviation * gain
    return jnp.minimum(jnp.maximum(drawn, -bound), bound).astype(kind)


def setup_inputs(seed: int = 0) -> dict:
    seeds = jax.random.split(jax.random.key(seed), 12)
    return {
        "state_field": scatter_about(seeds[0], (C, NH, NW), 1.0, 6.0, ((1, 2), (2, 64))),
        "cotangent": scatter_about(seeds[1], (C, NH, NW), 1.0, 6.0, ((1, 2), (2, 64))),
        "land_mask": touch_ends((jax.random.randint(seeds[2], (NH, NW), 0, 4) < 3).astype(jnp.int32), jax.random.fold_in(seeds[2], 1), 0, 1),
        "ocean_slots": draw_ocean_slots(jax.random.fold_in(seeds[11], 71), 0),
        "ocean_count": draw_ocean_count(jax.random.fold_in(seeds[11], 71), 0),
        "kernel": scatter_about(seeds[5], (C, KTAPS), KTAPS ** -0.5, 0.875),
        "norm_gain": jnp.clip(1.0 + 0.1 * jax.random.normal(seeds[6], (C,), jnp.float32), 0.5, 1.5).astype(jnp.bfloat16),
        "norm_bias": scatter_about(seeds[7], (C,), 0.5, 3.0),
        "up_weight": scatter_about(seeds[8], (HID, C), C ** -0.5, 0.625),
        "up_bias": scatter_about(seeds[9], (HID,), 0.5, 3.0),
        "down_weight": scatter_about(seeds[10], (C, HID), HID ** -0.5, 0.3125),
    }


def ramp_table(length, margin):
    offsets = jnp.arange(length, dtype=jnp.float32) + 0.5
    return jnp.minimum(1.0, jnp.minimum(offsets / (2.0 * margin), (length - offsets) / (2.0 * margin)))

def depthwise(values, kernel):
    taps = kernel.shape[1]
    extent = math.isqrt(taps)
    radius = extent // 2
    side = values.shape[1]
    padded = jnp.pad(values, ((0, 0), (radius, radius), (radius, radius)))
    summed = jnp.zeros_like(values)
    for row_tap in range(extent):
        for col_tap in range(extent):
            summed = summed + kernel[:, row_tap * extent + col_tap][:, None, None] * padded[:, row_tap:row_tap + side, col_tap:col_tap + side]
    return summed

def convnext(values, kernel, norm_gain, norm_bias, up_weight, up_bias, down_weight):
    channels, side, _ = values.shape
    convolved = depthwise(values, kernel)
    average = lax.optimization_barrier(jnp.mean(convolved, axis=0, keepdims=True))
    centred = convolved - average
    spread = lax.optimization_barrier(jnp.mean(centred * centred, axis=0, keepdims=True))
    normed = centred * lax.rsqrt(spread + 1e-06) * norm_gain[:, None, None] + norm_bias[:, None, None]
    flattened = normed.reshape(channels, side * side)
    hidden = jnp.dot(up_weight, flattened, precision=lax.Precision.HIGHEST) + up_bias[:, None]
    activated = jax.nn.gelu(hidden, approximate=False)
    projected = jnp.dot(down_weight, activated, precision=lax.Precision.HIGHEST)
    return values + projected.reshape(channels, side, side)

def patch_grads(values, patch_cot, parameters):
    _, pullback = jax.vjp(convnext, values, *parameters)
    grads = pullback(patch_cot)
    return (grads[0], grads[1], grads[4], grads[6])

def reference(state_field, cotangent, land_mask, ocean_slots, ocean_count, kernel, norm_gain, norm_bias, up_weight, up_bias, down_weight):
    channels, height, breadth = state_field.shape
    lat_tiles, lon_tiles, per_tile = ocean_slots.shape
    parameters = tuple((weight_arr.astype(jnp.float32) for weight_arr in (kernel, norm_gain, norm_bias, up_weight, up_bias, down_weight)))
    masked = cotangent.astype(jnp.float32) * land_mask.astype(jnp.float32)[None]

    def widen_band(array):
        array = jnp.concatenate([array[:, :, breadth - MARGIN:], array, array[:, :, :MARGIN]], axis=2)
        return jnp.pad(array, ((0, 0), (MARGIN, MARGIN), (0, 0)))
    state_wide = widen_band(state_field.astype(jnp.float32))
    cot_wide = widen_band(masked)
    offsets = jnp.arange(per_tile, dtype=jnp.int32)
    listed = (ocean_slots[..., :, None] == offsets) & (offsets[:, None] < ocean_count[..., None, None])
    active = lax.optimization_barrier(jnp.sum(listed.astype(jnp.float32), axis=-2))
    ramp = ramp_table(PATCH, MARGIN)
    blending = ramp[:, None] * ramp[None, :]
    tile_breadth = per_tile * STRIDE
    anchor = jnp.int32(0)

    def patch_step(carry, index):
        collected, grad_kernel, grad_up, grad_down = carry
        lat_tile = index // (lon_tiles * per_tile)
        lon_tile = index // per_tile % lon_tiles
        tile_slot = index % per_tile
        row_start = (lat_tile * STRIDE).astype(jnp.int32)
        col_start = (lon_tile * tile_breadth + tile_slot * STRIDE).astype(jnp.int32)
        starts = (anchor, row_start, col_start)
        values = lax.dynamic_slice(state_wide, starts, (channels, PATCH, PATCH))
        patch_cot = lax.dynamic_slice(cot_wide, starts, (channels, PATCH, PATCH)) * blending * active[lat_tile, lon_tile, tile_slot]
        grad_field, grad_k, grad_u, grad_d = patch_grads(values, patch_cot, parameters)
        before = lax.dynamic_slice(collected, starts, (channels, PATCH, PATCH))
        collected = lax.dynamic_update_slice(collected, before + grad_field, starts)
        return ((collected, grad_kernel + grad_k, grad_up + grad_u, grad_down + grad_d), None)
    init = (jnp.zeros(state_wide.shape, jnp.float32), jnp.zeros(kernel.shape, jnp.float32), jnp.zeros(up_weight.shape, jnp.float32), jnp.zeros(down_weight.shape, jnp.float32))
    indices = jnp.arange(lat_tiles * lon_tiles * per_tile, dtype=jnp.int32)
    (collected, grad_kernel, grad_up, grad_down), _ = lax.scan(patch_step, init, indices)
    rows_band = collected[:, MARGIN:MARGIN + height, :]
    interior = rows_band[:, :, MARGIN:MARGIN + breadth]
    interior = interior.at[:, :, :MARGIN].add(rows_band[:, :, MARGIN + breadth:])
    interior = interior.at[:, :, breadth - MARGIN:].add(rows_band[:, :, :MARGIN])
    scale = 1.0 / math.sqrt(height * breadth)
    return (interior, grad_kernel * scale, grad_up * scale, grad_down * scale)
```

```python
import functools
import math

import jax
import jax.numpy as jnp
import numpy as np
from jax import lax
from jax.experimental import pallas as pl
from jax.experimental.pallas import tpu as pltpu
from jax.sharding import PartitionSpec as P

STRIDE = 64
MARGIN = 16
SIDE = 96
ROWS = 80
CH = 80
HP = 320
LANES = 128
RB = 8
CELLS = RB * SIDE
CR = 8
F32 = jnp.float32
BF16 = jnp.bfloat16

NT = (((1,), (1,)), ((), ()))

ERF_P = 0.3275911 / math.sqrt(2.0)
ERF_C = [0.5 * c for c in (0.254829592, -0.284496736, 1.421413741, -1.453152027, 1.061405429)]


def gelu_parts(h):
    a = jnp.abs(h)
    d = 1.0 + ERF_P * a
    t = pl.reciprocal(d, approx=True)
    t = t * (2.0 - d * t)
    e = jnp.exp(h * h * (-0.5))
    q = ERF_C[4] * t + ERF_C[3]
    q = q * t + ERF_C[2]
    q = q * t + ERF_C[1]
    q = q * t + ERF_C[0]
    q = q * (t * e)
    cdf = jnp.where(h > 0, 1.0 - q, q)
    act = h * cdf
    slope = cdf + h * (e * (1.0 / math.sqrt(2.0 * math.pi)))
    return act, slope


def halves(v):
    hi = v.astype(BF16)
    lo = (v - hi.astype(F32)).astype(BF16)
    return hi, lo


def pack_rows(rows, lane):
    r1 = pltpu.roll(rows[1], 96, 1)
    r2 = pltpu.roll(rows[2], 64, 1)
    r3 = pltpu.roll(rows[3], 32, 1)
    return (
        jnp.where(lane < 96, rows[0], r1),
        jnp.where(lane < 64, r1, r2),
        jnp.where(lane < 32, r2, r3),
    )


def unpack_rows(packed, lane):
    live = lane < 96
    v0, v1, v2 = packed
    zero = jnp.zeros_like(v0)
    r1 = pltpu.roll(jnp.where(lane < 96, v1, v0), 32, 1)
    r2 = pltpu.roll(jnp.where(lane < 32, v2, v1), 64, 1)
    r3 = pltpu.roll(v2, 96, 1)
    return tuple(jnp.where(live, r, zero) for r in (v0, r1, r2, r3))


def patch_kernel(
    count_ref, slots_ref, x_ref, c_ref, blend_ref, taps_ref, gain_ref, bias_ref, upk_ref, dnk_ref,
    upt_ref,
    field_ref, kg_ref, up_ref, dn_ref,
    xf, conv, cbf, dpad, nk, cbk, xhat, rstd, hid, dact, ahl, dhl,
):
    field_ref[...] = jnp.zeros(field_ref.shape, F32)
    kg_ref[...] = jnp.zeros(kg_ref.shape, F32)
    up_ref[...] = jnp.zeros(up_ref.shape, F32)
    dn_ref[...] = jnp.zeros(dn_ref.shape, F32)
    for ref in (xf, dpad):
        ref[0:3] = jnp.zeros((3, CH, LANES), F32)
        ref[ROWS + 3 : ROWS + 6] = jnp.zeros((3, CH, LANES), F32)
    nk[160:176, :] = (lax.broadcasted_iota(jnp.int32, (16, CELLS), 0) == 0).astype(F32).astype(BF16)

    def lanes(n):
        return lax.broadcasted_iota(jnp.int32, (n, LANES), 1)

    def one_patch(pos, carry):
        s = slots_ref[pos]

        def widen(r, carry):
            xf[r + 3] = x_ref[s, r].astype(F32)
            cbf[r] = c_ref[s, r].astype(F32) * blend_ref[r][0:1]
            return carry

        lax.fori_loop(0, ROWS, widen, 0)

        def conv_block(index, carry):
            g = pl.multiple_of((index // (ROWS // CR)) * 8, 8)
            r0 = (index % (ROWS // CR)) * CR
            acc = [None] * CR
            for b in range(7):
                rolled = []
                for i in range(CR + 6):
                    v = xf[r0 + i, pl.ds(g, 8), :]
                    rolled.append(v if b == 3 else pltpu.roll(v, (3 - b) % LANES, 1))
                for a in range(7):
                    tap = taps_ref[a * 7 + b, pl.ds(g, 8), :]
                    for r in range(CR):
                        term = tap * rolled[r + a]
                        acc[r] = term if acc[r] is None else acc[r] + term
            for r in range(CR):
                conv[r0 + r, pl.ds(g, 8), :] = acc[r]
            return carry

        lax.fori_loop(0, (CH // 8) * (ROWS // CR), conv_block, 0)

        def pointwise(block, carry):
            r0 = block * RB
            lane = lanes(CH)
            real = lax.broadcasted_iota(jnp.int32, (CH, LANES), 0) < 77
            gain = gain_ref[...]
            bias = bias_ref[...]
            for half in range(RB // 4):
                rows = [conv[r0 + half * 4 + i] for i in range(4)]
                for k, v in enumerate(pack_rows(rows, lane)):
                    at = pl.ds((half * 3 + k) * LANES, LANES)
                    mean = jnp.sum(v, axis=0, keepdims=True) * (1.0 / 77.0)
                    cen = jnp.where(real, v - mean, 0.0)
                    var = jnp.sum(cen * cen, axis=0, keepdims=True) * (1.0 / 77.0)
                    rs = lax.rsqrt(var + 1e-06)
                    xh = cen * rs
                    xhat[:, at] = xh
                    rstd[:, at] = jnp.broadcast_to(rs, (8, LANES))
                    hi, lo = halves(xh * gain + bias)
                    nk[0:CH, at] = hi
                    nk[CH : 2 * CH, at] = lo
                rows = [cbf[r0 + half * 4 + i] for i in range(4)]
                for k, v in enumerate(pack_rows(rows, lane)):
                    at = pl.ds((half * 3 + k) * LANES, LANES)
                    hi, lo = halves(v)
                    cbk[0:CH, at] = hi
                    cbk[CH : 2 * CH, at] = lo
            hid[...] = jnp.dot(upk_ref[...], nk[...], preferred_element_type=F32)
            dact[...] = jnp.dot(dnk_ref[...], cbk[...], preferred_element_type=F32)

            def hidden_chunk(i, carry):
                base = pl.multiple_of(i * 16, 16)
                for k in range(CELLS // 256):
                    at = pl.ds(k * 256, 256)
                    act, slope = gelu_parts(hid[pl.ds(base, 16), at])
                    hi, lo = halves(act)
                    ahl[pl.ds(base, 16), at] = hi
                    ahl[pl.ds(pl.multiple_of(HP + base, 16), 16), at] = lo
                    hi, lo = halves(slope * dact[pl.ds(base, 16), at])
                    dhl[pl.ds(base, 16), at] = hi
                    dhl[pl.ds(pl.multiple_of(HP + base, 16), 16), at] = lo
                return carry

            lax.fori_loop(0, HP // 16, hidden_chunk, 0)
            dn_ref[...] += lax.dot_general(ahl[...], cbk[...], NT, preferred_element_type=F32)
            up_ref[...] += lax.dot_general(dhl[...], nk[0 : 2 * CH], NT, preferred_element_type=F32)
            dnorm = jnp.dot(upt_ref[...], dhl[...], preferred_element_type=F32)
            for half in range(RB // 4):
                packed = []
                for k in range(3):
                    first = (half * 3 + k) * LANES
                    at = pl.ds(first, LANES)
                    xh = xhat[:, at]
                    dxh = dnorm[:, first : first + LANES] * gain
                    m1 = jnp.sum(dxh, axis=0, keepdims=True) * (1.0 / 77.0)
                    m2 = jnp.sum(dxh * xh, axis=0, keepdims=True) * (1.0 / 77.0)
                    v = (dxh - m1 - xh * m2) * rstd[0:1, at]
                    packed.append(jnp.where(real, v, 0.0))
                for i, row in enumerate(unpack_rows(packed, lane)):
                    dpad[r0 + half * 4 + i + 3] = row
            return carry

        lax.fori_loop(0, ROWS // RB, pointwise, 0)

        def back_block(index, carry):
            g = pl.multiple_of((index // (ROWS // CR)) * 8, 8)
            r0 = (index % (ROWS // CR)) * CR
            at = pl.ds(g, 8)
            acc = [cbf[r0 + r, at, :] for r in range(CR)]
            vals = [xf[r0 + r + 3, at, :] for r in range(CR)]
            for b in range(7):
                rolled = []
                for i in range(CR + 6):
                    v = dpad[r0 + i, at, :]
                    rolled.append(v if b == 3 else pltpu.roll(v, (b - 3) % LANES, 1))
                for a in range(7):
                    tap = taps_ref[a * 7 + b, at, :]
                    part = None
                    for r in range(CR):
                        d = rolled[r + 6 - a]
                        acc[r] = acc[r] + tap * d
                        term = vals[r] * d
                        part = term if part is None else part + term
                    kg_ref[a * 7 + b, at, :] += part
            lane = lanes(8)
            first = s == 0
            m0 = jnp.logical_and(lane < 96, first)
            m1 = jnp.logical_and(lane >= 64, jnp.logical_not(first))
            m2 = jnp.logical_and(lane < 32, jnp.logical_not(first))
            for r in range(CR):
                moved = pltpu.roll(acc[r], 64, 1)
                field_ref[r0 + r, at, 0:LANES] += jnp.where(m0, acc[r], jnp.where(m1, moved, 0.0))
                field_ref[r0 + r, at, LANES : 2 * LANES] += jnp.where(m2, moved, 0.0)
            return carry

        lax.fori_loop(0, (CH // 8) * (ROWS // CR), back_block, 0)
        return carry

    lax.fori_loop(0, count_ref[0], one_patch, 0)


def patches(count, slots, x, c, blend, taps, gain, bias, upk, dnk, upt):
    smem = pl.BlockSpec(memory_space=pltpu.SMEM)
    vmem = pl.BlockSpec(memory_space=pltpu.VMEM)
    return pl.pallas_call(
        patch_kernel,
        out_shape=(
            jax.ShapeDtypeStruct((ROWS, CH, 2 * LANES), F32),
            jax.ShapeDtypeStruct((49, CH, LANES), F32),
            jax.ShapeDtypeStruct((2 * HP, 2 * CH), F32),
            jax.ShapeDtypeStruct((2 * HP, 2 * CH), F32),
        ),
        in_specs=[smem, smem] + [vmem] * 9,
        out_specs=(vmem,) * 4,
        scratch_shapes=[
            pltpu.VMEM((ROWS + 6, CH, LANES), F32),
            pltpu.VMEM((ROWS, CH, LANES), F32),
            pltpu.VMEM((ROWS, CH, LANES), F32),
            pltpu.VMEM((ROWS + 6, CH, LANES), F32),
            pltpu.VMEM((176, CELLS), BF16),
            pltpu.VMEM((2 * CH, CELLS), BF16),
            pltpu.VMEM((CH, CELLS), F32),
            pltpu.VMEM((8, CELLS), F32),
            pltpu.VMEM((HP, CELLS), F32),
            pltpu.VMEM((HP, CELLS), F32),
            pltpu.VMEM((2 * HP, CELLS), BF16),
            pltpu.VMEM((2 * HP, CELLS), BF16),
        ],
        compiler_params=pltpu.CompilerParams(vmem_limit_bytes=60 * 1024 * 1024),
    )(count, slots, x, c, blend, taps, gain, bias, upk, dnk, upt)


def ramp_table(length, margin):
    offsets = jnp.arange(length, dtype=F32) + 0.5
    return jnp.minimum(1.0, jnp.minimum(offsets / (2.0 * margin), (length - offsets) / (2.0 * margin)))


def padded(array, shape):
    return jnp.pad(array, [(0, want - have) for want, have in zip(shape, array.shape)])


def prepare_weights(kernel, norm_gain, norm_bias, up_weight, up_bias, down_weight):
    taps = jnp.broadcast_to(
        padded(kernel.astype(F32).T, (49, CH))[:, :, None], (49, CH, LANES)
    )
    gain = jnp.broadcast_to(padded(norm_gain.astype(F32), (CH,))[:, None], (CH, LANES))
    bias = jnp.broadcast_to(padded(norm_bias.astype(F32), (CH,))[:, None], (CH, LANES))
    up = padded(up_weight, (HP, CH))
    upk = jnp.concatenate([up, up, padded(up_bias[:, None], (HP, 16))], axis=1)
    dn = padded(down_weight.T, (HP, CH))
    dnk = jnp.concatenate([dn, dn], axis=1)
    upt = jnp.concatenate([up.T, up.T], axis=1)
    return taps, gain, bias, upk, dnk, upt


def blend_rows(lat):
    ramp = ramp_table(SIDE, MARGIN)
    rows = lax.dynamic_slice(ramp, (jnp.where(lat == 0, MARGIN, 0),), (ROWS,))
    cols = padded(ramp, (LANES,))
    return jnp.broadcast_to((rows[:, None] * cols[None, :])[:, None, :], (ROWS, 8, LANES))


def ring(value, axis, steps):
    count = lax.axis_size(axis)
    return lax.ppermute(value, axis, [(i, (i + steps) % count) for i in range(count)])


def body(
    state_field, cotangent, land_mask, ocean_slots, ocean_count,
    kernel, norm_gain, norm_bias, up_weight, up_bias, down_weight,
):
    channels, height, breadth = state_field.shape
    lat = lax.axis_index("lat")
    masked = jnp.where(land_mask[None] > 0, cotangent, jnp.zeros_like(cotangent))
    own = jnp.stack([state_field, masked])
    own = jnp.pad(own, ((0, 0), (0, CH - channels), (0, 0), (0, 0)))
    own = jnp.transpose(own, (2, 0, 1, 3))
    give = jnp.where(lat == 0, own[height - MARGIN :], own[:MARGIN])
    got = lax.ppermute(give, "lat", [(0, 1), (1, 0)])
    tall = jnp.where(
        lat == 0, jnp.concatenate([own, got], axis=0), jnp.concatenate([got, own], axis=0)
    )
    flat = (ROWS * 2 * CH * MARGIN // LANES, LANES)
    piece = (ROWS, 2, CH, MARGIN)
    west = ring(tall[..., breadth - MARGIN :].reshape(flat), "lon", 1).reshape(piece)
    east = ring(tall[..., :MARGIN].reshape(flat), "lon", -1).reshape(piece)
    zeros = jnp.zeros((ROWS, 2, CH, LANES - SIDE), BF16)
    first = jnp.concatenate([west, tall[..., : SIDE - MARGIN], zeros], axis=3)
    second = jnp.concatenate([tall[..., STRIDE - MARGIN :], east, zeros], axis=3)
    x = jnp.stack([first[:, 0], second[:, 0]])
    c = jnp.stack([first[:, 1], second[:, 1]])
    weights = prepare_weights(kernel, norm_gain, norm_bias, up_weight, up_bias, down_weight)
    field, kg, up, dn = patches(
        ocean_count.reshape(1), ocean_slots.reshape(2), x, c, blend_rows(lat), *weights
    )
    kernel_grad = jnp.sum(kg, axis=2)[:, :channels].T
    hidden = up_weight.shape[0]
    up = up[:HP] + up[HP:]
    dn = dn[:HP] + dn[HP:]
    up_grad = (up[:, :CH] + up[:, CH:])[:hidden, :channels]
    down_grad = (dn[:, :CH] + dn[:, CH:])[:hidden, :channels].T
    summed = lax.psum((kernel_grad, up_grad, down_grad), ("lon", "lat"))
    scale = 1.0 / math.sqrt(height * lax.axis_size("lat") * breadth * lax.axis_size("lon"))

    width = breadth + 2 * MARGIN
    back = (ROWS, CH, MARGIN)
    flat = (ROWS * CH * MARGIN // LANES, LANES)
    west = field[:, :, :MARGIN].astype(BF16).reshape(flat)
    east = field[:, :, width - MARGIN : width].astype(BF16).reshape(flat)
    from_east = ring(west, "lon", -1).reshape(back).astype(F32)
    from_west = ring(east, "lon", 1).reshape(back).astype(F32)
    mid = field[:, :, MARGIN : MARGIN + breadth]
    mid = mid.at[:, :, :MARGIN].add(from_west).at[:, :, breadth - MARGIN :].add(from_east)
    give = jnp.where(lat == 0, mid[height:], mid[:MARGIN]).astype(BF16)
    got = lax.ppermute(give, "lat", [(0, 1), (1, 0)]).astype(F32)
    inner = jnp.where(lat == 0, mid[:height], mid[MARGIN:])
    gap = jnp.zeros((height - MARGIN, CH, breadth), F32)
    inner = inner + jnp.where(
        lat == 0, jnp.concatenate([gap, got], axis=0), jnp.concatenate([got, gap], axis=0)
    )
    field_grad = jnp.transpose(inner, (1, 0, 2))[:channels]
    return (field_grad, summed[0] * scale, summed[1] * scale, summed[2] * scale)


def solution(mesh):
    in_specs = (
        P(None, "lat", "lon"), P(None, "lat", "lon"), P("lat", "lon"), P("lat", "lon", None),
        P("lat", "lon"), P(), P(), P(), P(), P(), P(),
    )
    out_specs = (P(None, "lat", "lon"), P(), P(), P())
    return jax.shard_map(body, mesh=mesh, in_specs=in_specs, out_specs=out_specs, check_vma=False)
```

```python
import functools
import math

import jax
import jax.numpy as jnp
import numpy as np
from jax import lax
from jax.experimental import pallas as pl
from jax.experimental.pallas import tpu as pltpu
from jax.sharding import PartitionSpec as P

STRIDE = 64
MARGIN = 16
SIDE = 96
ROWS = 80
CH = 80
HP = 320
LANES = 128
RB = 8
CELLS = RB * SIDE
CR = 8
SUM_ROWS = 768
PIECE = SUM_ROWS // 16
F32 = jnp.float32
BF16 = jnp.bfloat16

NT = (((1,), (1,)), ((), ()))

ERF_P = 0.3275911 / math.sqrt(2.0)
ERF_C = [0.5 * c for c in (0.254829592, -0.284496736, 1.421413741, -1.453152027, 1.061405429)]


def gelu_parts(h):
    a = jnp.abs(h)
    d = 1.0 + ERF_P * a
    t = pl.reciprocal(d, approx=True)
    t = t * (2.0 - d * t)
    e = jnp.exp(h * h * (-0.5))
    q = ERF_C[4] * t + ERF_C[3]
    q = q * t + ERF_C[2]
    q = q * t + ERF_C[1]
    q = q * t + ERF_C[0]
    q = q * (t * e)
    cdf = jnp.where(h > 0, 1.0 - q, q)
    act = h * cdf
    slope = cdf + h * (e * (1.0 / math.sqrt(2.0 * math.pi)))
    return act, slope


def halves(v):
    hi = v.astype(BF16)
    lo = (v - hi.astype(F32)).astype(BF16)
    return hi, lo


def pack_rows(rows, lane):
    r1 = pltpu.roll(rows[1], 96, 1)
    r2 = pltpu.roll(rows[2], 64, 1)
    r3 = pltpu.roll(rows[3], 32, 1)
    return (
        jnp.where(lane < 96, rows[0], r1),
        jnp.where(lane < 64, r1, r2),
        jnp.where(lane < 32, r2, r3),
    )


def unpack_rows(packed, lane):
    live = lane < 96
    v0, v1, v2 = packed
    zero = jnp.zeros_like(v0)
    r1 = pltpu.roll(jnp.where(lane < 96, v1, v0), 32, 1)
    r2 = pltpu.roll(jnp.where(lane < 32, v2, v1), 64, 1)
    r3 = pltpu.roll(v2, 96, 1)
    return tuple(jnp.where(live, r, zero) for r in (v0, r1, r2, r3))


def patch_kernel(
    meta_ref, own_ref, got_ref, strips_ref, blend_ref, taps_ref, gain_ref, bias_ref, upk_ref,
    dnk_ref, upt_ref,
    field_ref, rim_ref, sum_ref,
    xf, conv, cbf, dpad, nk, cbk, xhat, rstd, hid, dact, ahl, dhl, kg, gup, gdn,
):
    for ref in (field_ref, rim_ref, kg, gup, gdn):
        ref[...] = jnp.zeros(ref.shape, F32)
    for ref in (xf, dpad):
        ref[0:3] = jnp.zeros((3, CH, LANES), F32)
        ref[ROWS + 3 : ROWS + 6] = jnp.zeros((3, CH, LANES), F32)
    nk[CH:LANES, :] = jnp.zeros((LANES - CH, CELLS), BF16)
    cbk[CH:LANES, :] = jnp.zeros((LANES - CH, CELLS), BF16)
    cbk[LANES + CH :, :] = jnp.zeros((LANES - CH, CELLS), BF16)
    ones = lax.broadcasted_iota(jnp.int32, (LANES - CH, CELLS), 0) == 0
    nk[LANES + CH :, :] = jnp.where(ones, 1.0, 0.0).astype(BF16)

    def lanes(n):
        return lax.broadcasted_iota(jnp.int32, (n, LANES), 1)

    def one_patch(pos, carry):
        s = meta_ref[1 + pos]
        turn = jnp.where(s == 0, 16, 80)
        low = jnp.where(s == 0, 16, 0)
        rim = jnp.where(s == 0, 0, 80)

        def widen(source, first, count):
            def group(k, carry):
                lane = lanes(CH)
                in_own = jnp.logical_and(lane >= low, lane < low + 80)
                in_rim = jnp.logical_and(lane >= rim, lane < rim + 16)
                q = first + k
                for part in range(2):
                    edge = strips_ref[s, q, part].astype(F32)
                    for i in range(8):
                        v = pltpu.roll(source[k * 8 + i, part].astype(F32), turn, 1)
                        e = pltpu.roll(edge, (rim + LANES - 16 * i) % LANES, 1)
                        v = jnp.where(in_own, v, jnp.where(in_rim, e, 0.0))
                        if part == 0:
                            xf[q * 8 + i + 3] = v
                        else:
                            cbf[q * 8 + i] = v * blend_ref[q * 8 + i][0:1]
                return carry

            lax.fori_loop(0, count, group, 0)

        widen(own_ref, meta_ref[3], 8)
        widen(got_ref, meta_ref[4], 2)

        def conv_block(index, carry):
            g = pl.multiple_of((index // (ROWS // CR)) * 8, 8)
            r0 = (index % (ROWS // CR)) * CR
            acc = [None] * CR
            for b in range(7):
                rolled = []
                for i in range(CR + 6):
                    v = xf[r0 + i, pl.ds(g, 8), :]
                    rolled.append(v if b == 3 else pltpu.roll(v, (3 - b) % LANES, 1))
                for a in range(7):
                    tap = taps_ref[a * 7 + b, pl.ds(g, 8), :]
                    for r in range(CR):
                        term = tap * rolled[r + a]
                        acc[r] = term if acc[r] is None else acc[r] + term
            for r in range(CR):
                conv[r0 + r, pl.ds(g, 8), :] = acc[r]
            return carry

        lax.fori_loop(0, (CH // 8) * (ROWS // CR), conv_block, 0)

        def pointwise(block, carry):
            r0 = block * RB
            lane = lanes(CH)
            real = lax.broadcasted_iota(jnp.int32, (CH, LANES), 0) < 77
            gain = gain_ref[...]
            bias = bias_ref[...]
            for half in range(RB // 4):
                rows = [conv[r0 + half * 4 + i] for i in range(4)]
                for k, v in enumerate(pack_rows(rows, lane)):
                    at = pl.ds((half * 3 + k) * LANES, LANES)
                    mean = jnp.sum(v, axis=0, keepdims=True) * (1.0 / 77.0)
                    cen = jnp.where(real, v - mean, 0.0)
                    var = jnp.sum(cen * cen, axis=0, keepdims=True) * (1.0 / 77.0)
                    rs = lax.rsqrt(var + 1e-06)
                    xh = cen * rs
                    xhat[:, at] = xh
                    rstd[:, at] = jnp.broadcast_to(rs, (8, LANES))
                    hi, lo = halves(xh * gain + bias)
                    nk[0:CH, at] = hi
                    nk[LANES : LANES + CH, at] = lo
                rows = [cbf[r0 + half * 4 + i] for i in range(4)]
                for k, v in enumerate(pack_rows(rows, lane)):
                    at = pl.ds((half * 3 + k) * LANES, LANES)
                    hi, lo = halves(v)
                    cbk[0:CH, at] = hi
                    cbk[LANES : LANES + CH, at] = lo
            hid[...] = jnp.dot(upk_ref[...], nk[...], preferred_element_type=F32)
            dact[...] = jnp.dot(dnk_ref[...], cbk[...], preferred_element_type=F32)

            def hidden_chunk(i, carry):
                base = pl.multiple_of(i * 16, 16)
                for k in range(CELLS // 256):
                    at = pl.ds(k * 256, 256)
                    act, slope = gelu_parts(hid[pl.ds(base, 16), at])
                    hi, lo = halves(act)
                    ahl[pl.ds(base, 16), at] = hi
                    ahl[pl.ds(pl.multiple_of(HP + base, 16), 16), at] = lo
                    hi, lo = halves(slope * dact[pl.ds(base, 16), at])
                    dhl[pl.ds(base, 16), at] = hi
                    dhl[pl.ds(pl.multiple_of(HP + base, 16), 16), at] = lo
                return carry

            lax.fori_loop(0, HP // 16, hidden_chunk, 0)
            gdn[...] += lax.dot_general(ahl[...], cbk[...], NT, preferred_element_type=F32)
            gup[...] += lax.dot_general(dhl[...], nk[...], NT, preferred_element_type=F32)
            dnorm = jnp.dot(upt_ref[...], dhl[...], preferred_element_type=F32)
            for half in range(RB // 4):
                packed = []
                for k in range(3):
                    first = (half * 3 + k) * LANES
                    at = pl.ds(first, LANES)
                    xh = xhat[:, at]
                    dxh = dnorm[:, first : first + LANES] * gain
                    m1 = jnp.sum(dxh, axis=0, keepdims=True) * (1.0 / 77.0)
                    m2 = jnp.sum(dxh * xh, axis=0, keepdims=True) * (1.0 / 77.0)
                    v = (dxh - m1 - xh * m2) * rstd[0:1, at]
                    packed.append(jnp.where(real, v, 0.0))
                for i, row in enumerate(unpack_rows(packed, lane)):
                    dpad[r0 + half * 4 + i + 3] = row
            return carry

        lax.fori_loop(0, ROWS // RB, pointwise, 0)

        def back_block(index, carry):
            g = pl.multiple_of((index // (ROWS // CR)) * 8, 8)
            r0 = (index % (ROWS // CR)) * CR
            at = pl.ds(g, 8)
            acc = [cbf[r0 + r, at, :] for r in range(CR)]
            vals = [xf[r0 + r + 3, at, :] for r in range(CR)]
            for b in range(7):
                rolled = []
                for i in range(CR + 6):
                    v = dpad[r0 + i, at, :]
                    rolled.append(v if b == 3 else pltpu.roll(v, (b - 3) % LANES, 1))
                for a in range(7):
                    tap = taps_ref[a * 7 + b, at, :]
                    part = None
                    for r in range(CR):
                        d = rolled[r + 6 - a]
                        acc[r] = acc[r] + tap * d
                        term = vals[r] * d
                        part = term if part is None else part + term
                    kg[a * 7 + b, at, :] += part
            lane = lanes(8)
            inside = jnp.logical_and(lane >= 48 * s, lane < 80 + 48 * s)
            edge = jnp.zeros((8, LANES), F32)
            for r in range(CR):
                moved = pltpu.roll(acc[r], jnp.where(s == 0, 112, 48), 1)
                field_ref[r0 + r, at, :] += jnp.where(inside, moved, 0.0)
                moved = pltpu.roll(acc[r], (16 * r + LANES - rim) % LANES, 1)
                edge = jnp.where(jnp.logical_and(lane >= 16 * r, lane < 16 * r + 16), moved, edge)
            rim_ref[s, r0 // 8, at, :] = edge
            return carry

        lax.fori_loop(0, (CH // 8) * (ROWS // CR), back_block, 0)
        return carry

    lax.fori_loop(0, meta_ref[0], one_patch, 0)
    for first, ref in ((0, gup), (HP, gdn)):
        total = ref[0:HP, :] + ref[HP : 2 * HP, :]
        sum_ref[first : first + HP, :] = total[:, :LANES] + total[:, LANES:]
    sum_ref[2 * HP :, :] = jnp.zeros((SUM_ROWS - 2 * HP, LANES), F32)

    def tap_sum(t, carry):
        here = sum_ref[2 * HP : 2 * HP + CH, :]
        total = jnp.sum(kg[t], axis=1, keepdims=True)
        sum_ref[2 * HP : 2 * HP + CH, :] = jnp.where(lanes(CH) == t, total, here)
        return carry

    lax.fori_loop(0, 49, tap_sum, 0)


def patches(meta, own, got, strips, blend, weights):
    smem = pl.BlockSpec(memory_space=pltpu.SMEM)
    vmem = pl.BlockSpec(memory_space=pltpu.VMEM)
    return pl.pallas_call(
        patch_kernel,
        name="patches",
        out_shape=(
            jax.ShapeDtypeStruct((ROWS, CH, LANES), F32),
            jax.ShapeDtypeStruct((2, ROWS // 8, CH, LANES), F32),
            jax.ShapeDtypeStruct((SUM_ROWS, LANES), F32),
        ),
        in_specs=[smem] + [vmem] * 10,
        out_specs=(vmem,) * 3,
        scratch_shapes=[
            pltpu.VMEM((ROWS + 6, CH, LANES), F32),
            pltpu.VMEM((ROWS, CH, LANES), F32),
            pltpu.VMEM((ROWS, CH, LANES), F32),
            pltpu.VMEM((ROWS + 6, CH, LANES), F32),
            pltpu.VMEM((2 * LANES, CELLS), BF16),
            pltpu.VMEM((2 * LANES, CELLS), BF16),
            pltpu.VMEM((CH, CELLS), F32),
            pltpu.VMEM((8, CELLS), F32),
            pltpu.VMEM((HP, CELLS), F32),
            pltpu.VMEM((HP, CELLS), F32),
            pltpu.VMEM((2 * HP, CELLS), BF16),
            pltpu.VMEM((2 * HP, CELLS), BF16),
            pltpu.VMEM((49, CH, LANES), F32),
            pltpu.VMEM((2 * HP, 2 * LANES), F32),
            pltpu.VMEM((2 * HP, 2 * LANES), F32),
        ],
        compiler_params=pltpu.CompilerParams(vmem_limit_bytes=60 * 1024 * 1024),
    )(meta, own, got, strips, blend, *weights)


def place():
    lon = lax.axis_index("lon")
    lat = lax.axis_index("lat")
    count = lax.axis_size("lon")
    return lon, lat, lax.rem(lon + 1, count), lax.rem(lon + count - 1, count)


def meet(peers):
    barrier = pltpu.get_barrier_semaphore()
    for peer in peers:
        pl.semaphore_signal(barrier, inc=1, device_id=peer, device_id_type=pl.DeviceIdType.MESH)
    pl.semaphore_wait(barrier, len(peers))


def remote(source, target, sems, index, peer):
    return pltpu.make_async_remote_copy(
        src_ref=source,
        dst_ref=target,
        send_sem=sems.at[0, index],
        recv_sem=sems.at[1, index],
        device_id=peer,
        device_id_type=pl.DeviceIdType.MESH,
    )


def halo_kernel(own_ref, got_ref, strips_ref, edges, sems):
    lon, lat, east, west = place()
    other = 1 - lat
    meet([(east, lat), (west, lat), (lon, other), (east, other), (west, other)])
    give = (1 - lat) * 48
    tall = remote(own_ref.at[pl.ds(give, 16)], got_ref, sems, 0, (lon, other))
    tall.start()

    def pack(k, carry):
        lane = lax.broadcasted_iota(jnp.int32, (CH, LANES), 1)
        for part in range(2):
            acc = [jnp.zeros((CH, LANES), F32)] * 2
            for i in range(8):
                v = own_ref[k * 8 + i, part].astype(F32)
                here = jnp.logical_and(lane >= 16 * i, lane < 16 * i + 16)
                for side in range(2):
                    moved = pltpu.roll(v, (16 * i + 16 * side) % LANES, 1)
                    acc[side] = jnp.where(here, moved, acc[side])
            for side in range(2):
                edges[side, k, part] = acc[side].astype(BF16)
        return carry

    lax.fori_loop(0, 8, pack, 0)
    mine = lat * 2
    corner = (1 - lat) * 6
    far = lat * 8
    copies = [tall]
    for side, peer in ((0, west), (1, east)):
        copies.append(
            remote(edges.at[side], strips_ref.at[1 - side, pl.ds(mine, 8)], sems, 1 + side, (peer, lat))
        )
        copies.append(
            remote(
                edges.at[side, pl.ds(corner, 2)], strips_ref.at[1 - side, pl.ds(far, 2)], sems,
                3 + side, (peer, other),
            )
        )
    for copy in copies[1:]:
        copy.start()
    for copy in copies:
        copy.wait()


def halo(own):
    hbm = pl.BlockSpec(memory_space=pl.ANY)
    return pl.pallas_call(
        halo_kernel,
        name="halo",
        out_shape=(
            jax.ShapeDtypeStruct((MARGIN, 2, CH, LANES), BF16),
            jax.ShapeDtypeStruct((2, ROWS // 8, 2, CH, LANES), BF16),
        ),
        in_specs=[pl.BlockSpec(memory_space=pltpu.VMEM)],
        out_specs=(hbm, hbm),
        scratch_shapes=[
            pltpu.VMEM((2, 8, 2, CH, LANES), BF16),
            pltpu.SemaphoreType.DMA((2, 5)),
        ],
        compiler_params=pltpu.CompilerParams(
            collective_id=0, has_side_effects=True, vmem_limit_bytes=32 * 1024 * 1024
        ),
    )(own)


def fold_kernel(
    field_ref, rim_ref, sum_ref,
    out_ref, total_ref,
    edges, rows, near, corner, above, first, second, chunk, sems,
):
    lon, lat, east, west = place()
    other = 1 - lat
    half = lon // 32
    cell = lax.rem(lon, 32) // 2
    core = lax.rem(lon, 2)
    plane = [(half * 32 + lax.rem(cell + d, 16) * 2 + core, lat) for d in range(1, 16)]
    column = (half * 2 + core) * 2 + lat
    cross = []
    for d in range(1, 8):
        j = lax.rem(column + d, 8)
        cross.append(((j // 4) * 32 + cell * 2 + lax.rem(j // 2, 2), lax.rem(j, 2)))
    near_by = [(east, lat), (west, lat), (lon, other), (east, other), (west, other)]
    meet(near_by + plane + cross)

    scatter = []
    for d in range(1, 16):
        to = lax.rem(cell + d, 16)
        copy = remote(
            sum_ref.at[pl.ds(pl.multiple_of(to * PIECE, 8), PIECE)], first.at[d], sems, d, plane[d - 1]
        )
        copy.start()
        scatter.append(copy)

    mine = lat * 2
    far = (1 - lat) * 8
    margin = (1 - lat) * 64

    def narrow_rows(r, carry):
        rows[r] = field_ref[margin + r].astype(BF16)
        return carry

    lax.fori_loop(0, MARGIN, narrow_rows, 0)
    folds = [remote(rows, above, sems, 16, (lon, other))]
    folds[0].start()

    def narrow(q, carry):
        for side in range(2):
            edges[side, q] = rim_ref[side, q].astype(BF16)
        return carry

    lax.fori_loop(0, ROWS // 8, narrow, 0)
    for side, peer in ((0, west), (1, east)):
        folds.append(
            remote(edges.at[side, pl.ds(mine, 8)], near.at[1 - side], sems, 17 + side, (peer, lat))
        )
        folds.append(
            remote(edges.at[side, pl.ds(far, 2)], corner.at[1 - side], sems, 19 + side, (peer, other))
        )
    for copy in folds[1:]:
        copy.start()

    for copy in scatter:
        copy.wait()
    part = sum_ref[pl.ds(pl.multiple_of(cell * PIECE, 8), PIECE), :]
    for d in range(1, 16):
        part = part + first[d]
    second[0] = part
    crossing = []
    for d in range(1, 8):
        copy = remote(second.at[0], second.at[d], sems, 20 + d, cross[d - 1])
        copy.start()
        crossing.append(copy)
    for copy in crossing:
        copy.wait()
    whole = jnp.zeros((PIECE, LANES), F32)
    for j in range(8):
        whole = whole + second[lax.rem(column - j + 8, 8)]
    chunk[...] = whole
    here = pl.ds(pl.multiple_of(cell * PIECE, 8), PIECE)
    total_ref[here, :] = whole
    gather = []
    for d in range(1, 16):
        copy = remote(chunk, total_ref.at[here], sems, 27 + d, plane[d - 1])
        copy.start()
        gather.append(copy)

    for copy in folds:
        copy.wait()

    def finish(k, carry):
        lane = lax.broadcasted_iota(jnp.int32, (CH, LANES), 1)
        from_west = near[0, k].astype(F32)
        from_east = near[1, k].astype(F32)
        for i in range(8):
            w = pltpu.roll(from_west, (LANES - 16 * i) % LANES, 1)
            e = pltpu.roll(from_east, 112 - 16 * i, 1)
            add = jnp.where(lane < 16, w, jnp.where(lane >= 112, e, 0.0))
            out_ref[k * 8 + i] = field_ref[(mine + k) * 8 + i] + add
        return carry

    lax.fori_loop(0, 8, finish, 0)
    base = (1 - lat) * 6

    def finish_corner(k, carry):
        lane = lax.broadcasted_iota(jnp.int32, (CH, LANES), 1)
        from_west = corner[0, k].astype(F32)
        from_east = corner[1, k].astype(F32)
        for i in range(8):
            w = pltpu.roll(from_west, (LANES - 16 * i) % LANES, 1)
            e = pltpu.roll(from_east, 112 - 16 * i, 1)
            add = jnp.where(lane < 16, w, jnp.where(lane >= 112, e, 0.0))
            out_ref[(base + k) * 8 + i] += add + above[k * 8 + i].astype(F32)
        return carry

    lax.fori_loop(0, 2, finish_corner, 0)
    for copy in gather:
        copy.wait()


def fold(field, rim, sums):
    vmem = pl.BlockSpec(memory_space=pltpu.VMEM)
    return pl.pallas_call(
        fold_kernel,
        name="fold",
        out_shape=(
            jax.ShapeDtypeStruct((ROWS - MARGIN, CH, LANES), F32),
            jax.ShapeDtypeStruct((SUM_ROWS, LANES), F32),
        ),
        in_specs=[vmem] * 3,
        out_specs=(vmem,) * 2,
        scratch_shapes=[
            pltpu.VMEM((2, ROWS // 8, CH, LANES), BF16),
            pltpu.VMEM((MARGIN, CH, LANES), BF16),
            pltpu.VMEM((2, 8, CH, LANES), BF16),
            pltpu.VMEM((2, 2, CH, LANES), BF16),
            pltpu.VMEM((MARGIN, CH, LANES), BF16),
            pltpu.VMEM((16, PIECE, LANES), F32),
            pltpu.VMEM((8, PIECE, LANES), F32),
            pltpu.VMEM((PIECE, LANES), F32),
            pltpu.SemaphoreType.DMA((2, 43)),
        ],
        compiler_params=pltpu.CompilerParams(
            collective_id=1, has_side_effects=True, vmem_limit_bytes=48 * 1024 * 1024
        ),
    )(field, rim, sums)


def ramp_table(length, margin):
    offsets = jnp.arange(length, dtype=F32) + 0.5
    return jnp.minimum(1.0, jnp.minimum(offsets / (2.0 * margin), (length - offsets) / (2.0 * margin)))


def padded(array, shape):
    return jnp.pad(array, [(0, want - have) for want, have in zip(shape, array.shape)])


def prepare_weights(kernel, norm_gain, norm_bias, up_weight, up_bias, down_weight):
    taps = jnp.broadcast_to(
        padded(kernel.astype(F32).T, (49, CH))[:, :, None], (49, CH, LANES)
    )
    gain = jnp.broadcast_to(padded(norm_gain.astype(F32), (CH,))[:, None], (CH, LANES))
    bias = jnp.broadcast_to(padded(norm_bias.astype(F32), (CH,))[:, None], (CH, LANES))
    up = padded(up_weight, (HP, CH))
    gap = jnp.zeros((HP, LANES - CH), BF16)
    upk = jnp.concatenate([up, gap, up, padded(up_bias[:, None], (HP, LANES - CH))], axis=1)
    dn = padded(down_weight.T, (HP, CH))
    dnk = jnp.concatenate([dn, gap, dn, gap], axis=1)
    upt = jnp.concatenate([up.T, up.T], axis=1)
    return taps, gain, bias, upk, dnk, upt


def blend_rows(lat):
    ramp = ramp_table(SIDE, MARGIN)
    rows = lax.dynamic_slice(ramp, (jnp.where(lat == 0, MARGIN, 0),), (ROWS,))
    cols = padded(ramp, (LANES,))
    return jnp.broadcast_to((rows[:, None] * cols[None, :])[:, None, :], (ROWS, 8, LANES))


def body(
    state_field, cotangent, land_mask, ocean_slots, ocean_count,
    kernel, norm_gain, norm_bias, up_weight, up_bias, down_weight,
):
    channels, height, breadth = state_field.shape
    hidden = up_weight.shape[0]
    lat = lax.axis_index("lat")
    masked = jnp.where(land_mask[None] > 0, cotangent, jnp.zeros_like(cotangent))
    own = jnp.stack([state_field, masked])
    own = jnp.pad(own, ((0, 0), (0, CH - channels), (0, 0), (0, 0)))
    own = jnp.transpose(own, (2, 0, 1, 3))
    got, strips = halo(own)
    weights = prepare_weights(kernel, norm_gain, norm_bias, up_weight, up_bias, down_weight)
    meta = jnp.concatenate(
        [ocean_count.reshape(1), ocean_slots.reshape(2), jnp.stack([lat * 2, (1 - lat) * 8])]
    ).astype(jnp.int32)
    field, rim, sums = patches(meta, own, got, strips, blend_rows(lat), weights)
    out, total = fold(field, rim, sums)
    scale = 1.0 / math.sqrt(height * lax.axis_size("lat") * breadth * lax.axis_size("lon"))
    total = total * scale
    field_grad = jnp.transpose(out, (1, 0, 2))[:channels]
    kernel_grad = total[2 * HP : 2 * HP + channels, :49]
    up_grad = total[:hidden, :channels]
    down_grad = total[HP : HP + hidden, :channels].T
    return (field_grad, kernel_grad, up_grad, down_grad)


def solution(mesh):
    in_specs = (
        P(None, "lat", "lon"), P(None, "lat", "lon"), P("lat", "lon"), P("lat", "lon", None),
        P("lat", "lon"), P(), P(), P(), P(), P(), P(),
    )
    out_specs = (P(None, "lat", "lon"), P(), P(), P())
    return jax.shard_map(body, mesh=mesh, in_specs=in_specs, out_specs=out_specs, check_vma=False)
```

```python
import functools
import math

import jax
import jax.numpy as jnp
import numpy as np
from jax import lax
from jax.experimental import pallas as pl
from jax.experimental.pallas import tpu as pltpu
from jax.sharding import PartitionSpec as P

STRIDE = 64
MARGIN = 16
SIDE = 96
ROWS = 80
CH = 80
HP = 320
LANES = 128
RB = 16
CELLS = RB * SIDE
TILE = 256
UNROLL = 4
SUM_ROWS = 768
PIECE = SUM_ROWS // 16
F32 = jnp.float32
BF16 = jnp.bfloat16

NT = (((1,), (1,)), ((), ()))

ERF_P = 0.3275911 / math.sqrt(2.0)
ERF_C = [0.5 * c for c in (0.254829592, -0.284496736, 1.421413741, -1.453152027, 1.061405429)]


def gelu_parts(h):
    a = jnp.abs(h)
    d = 1.0 + ERF_P * a
    t = pl.reciprocal(d, approx=True)
    t = t * (2.0 - d * t)
    e = jnp.exp(h * h * (-0.5))
    q = ERF_C[4] * t + ERF_C[3]
    q = q * t + ERF_C[2]
    q = q * t + ERF_C[1]
    q = q * t + ERF_C[0]
    q = q * (t * e)
    cdf = jnp.where(h > 0, 1.0 - q, q)
    act = h * cdf
    slope = cdf + h * (e * (1.0 / math.sqrt(2.0 * math.pi)))
    return act, slope


def halves(v):
    hi = v.astype(BF16)
    lo = (v - hi.astype(F32)).astype(BF16)
    return hi, lo


def pack_rows(rows, lane):
    r1 = pltpu.roll(rows[1], 96, 1)
    r2 = pltpu.roll(rows[2], 64, 1)
    r3 = pltpu.roll(rows[3], 32, 1)
    return (
        jnp.where(lane < 96, rows[0], r1),
        jnp.where(lane < 64, r1, r2),
        jnp.where(lane < 32, r2, r3),
    )


def unpack_rows(packed, lane):
    live = lane < 96
    v0, v1, v2 = packed
    zero = jnp.zeros_like(v0)
    r1 = pltpu.roll(jnp.where(lane < 96, v1, v0), 32, 1)
    r2 = pltpu.roll(jnp.where(lane < 32, v2, v1), 64, 1)
    r3 = pltpu.roll(v2, 96, 1)
    return tuple(jnp.where(live, r, zero) for r in (v0, r1, r2, r3))


def patch_kernel(
    meta_ref, own_ref, got_ref, strips_ref, blend_ref, ahead_ref, back_ref, gain_ref, bias_ref,
    upk_ref, dnk_ref, upt_ref,
    field_ref, rim_ref, sum_ref,
    xf, conv, cbf, dcv, nk, cbk, xhat, rstd, dnorm, hid, dact, ahl, dhl, gup, gdn, weights, data, lines, xt,
):
    gup[...] = jnp.zeros(gup.shape, F32)
    gdn[...] = jnp.zeros(gdn.shape, F32)
    for ref in (xf, dcv):
        for p in range(2):
            ref[p, 0 : 3 * CH] = jnp.zeros((3 * CH, LANES), F32)
            ref[p, (ROWS + 3) * CH :] = jnp.zeros((13 * CH, LANES), F32)
    weights[...] = jnp.zeros(weights.shape, BF16)
    nk[CH:LANES, :] = jnp.zeros((LANES - CH, CELLS), BF16)
    cbk[CH:LANES, :] = jnp.zeros((LANES - CH, CELLS), BF16)
    cbk[LANES + CH :, :] = jnp.zeros((LANES - CH, CELLS), BF16)
    ones = lax.broadcasted_iota(jnp.int32, (LANES - CH, CELLS), 0) == 0
    nk[LANES + CH :, :] = jnp.where(ones, 1.0, 0.0).astype(BF16)

    def lanes(n):
        return lax.broadcasted_iota(jnp.int32, (n, LANES), 1)

    def row(r):
        return pl.ds(pl.multiple_of(r * CH, 8), CH)

    def active(s):
        here = jnp.logical_and(meta_ref[0] > 0, meta_ref[1] == s)
        return jnp.logical_or(here, jnp.logical_and(meta_ref[0] > 1, meta_ref[2] == s))

    on = [jnp.where(active(s), 1.0, 0.0) for s in range(2)]

    def widen(source, first, count):
        def group(k, carry):
            lane = lanes(CH)
            q = first + k
            for s in range(2):
                low, turn, rim = ((16, 16, 0), (0, 80, 80))[s]
                in_own = jnp.logical_and(lane >= low, lane < low + 80)
                in_rim = jnp.logical_and(lane >= rim, lane < rim + 16)
                for part in range(2):
                    edge = strips_ref[s, q, part].astype(F32)
                    for i in range(8):
                        v = pltpu.roll(source[k * 8 + i, part].astype(F32), turn, 1)
                        e = pltpu.roll(edge, (rim + LANES - 16 * i) % LANES, 1)
                        v = jnp.where(in_own, v, jnp.where(in_rim, e, 0.0))
                        if part == 0:
                            xf[s, row(q * 8 + i + 3), :] = v
                        else:
                            cbf[s, row(q * 8 + i), :] = v * (blend_ref[q * 8 + i][0:1] * on[s])
            return carry

        lax.fori_loop(0, count, group, 0)

    widen(own_ref, meta_ref[3], 8)
    widen(got_ref, meta_ref[4], 2)

    def band(source, c, slot, sign):
        for a in range(7):
            base = source[c * 7 + a].astype(F32)
            for m in range(6):
                tile = (base if m == 0 else pltpu.roll(base, 16 * m, 1)).astype(BF16)
                for q in range(2):
                    u = a + q if sign > 0 else q + 6 - a
                    weights[slot, u * LANES + 16 * m : u * LANES + 16 * (m + 1), q * LANES : (q + 1) * LANES] = tile

    def every_other(ref, p, parity, c):
        return ref[p, pl.ds(parity * CH + c, 48, stride=2 * CH), :]

    def moved_rows(slot, kind, u):
        near = u // 2
        return jnp.concatenate(
            [lines[slot, kind, 2 * p + u % 2, near : near + ROWS // 2] for p in range(2)], axis=0
        ).astype(BF16)

    def conv_channel(c, slot):
        band(ahead_ref, c, slot, 1)
        for p in range(2):
            for parity in range(2):
                lines[slot, 0, 2 * p + parity] = every_other(xf, p, parity, c)
        for u in range(8):
            data[slot, 0:ROWS, u * LANES : (u + 1) * LANES] = moved_rows(slot, 0, u)
        for q in range(2):
            near = (q + 3) // 2
            v = jnp.concatenate(
                [lines[slot, 0, 2 * p + (q + 3) % 2, near : near + ROWS // 2] for p in range(2)], axis=0
            )
            v = v.T[:SIDE].astype(BF16)
            xt[c, q * SIDE : (q + 1) * SIDE] = jnp.concatenate([v, v], axis=1)
        out = jnp.dot(data[slot, 0:ROWS, :], weights[slot], preferred_element_type=F32)
        for p in range(2):
            for q in range(2):
                conv[p, pl.ds(q * CH + c, ROWS // 2, stride=2 * CH), :] = out[
                    p * (ROWS // 2) : (p + 1) * (ROWS // 2), q * LANES : (q + 1) * LANES
                ]

    def conv_channels(i, carry):
        for slot in range(UNROLL):
            conv_channel(i * UNROLL + slot, slot)
        return carry

    lax.fori_loop(0, CH // UNROLL, conv_channels, 0)

    def pointwise(index, carry):
        p = index // (ROWS // RB)
        r0 = (index % (ROWS // RB)) * RB
        lane = lanes(CH)
        real = lax.broadcasted_iota(jnp.int32, (CH, LANES), 0) < 77
        gain = gain_ref[...]
        bias = bias_ref[...]
        for half in range(RB // 4):
            rows = [conv[p, row(r0 + half * 4 + i), :] for i in range(4)]
            for k, v in enumerate(pack_rows(rows, lane)):
                at = pl.ds((half * 3 + k) * LANES, LANES)
                mean = jnp.sum(jnp.where(real, v, 0.0), axis=0, keepdims=True) * (1.0 / 77.0)
                cen = jnp.where(real, v - mean, 0.0)
                var = jnp.sum(cen * cen, axis=0, keepdims=True) * (1.0 / 77.0)
                rs = lax.rsqrt(var + 1e-06)
                xh = cen * rs
                xhat[:, at] = xh
                rstd[:, at] = jnp.broadcast_to(rs, (8, LANES))
                hi, lo = halves(xh * gain + bias)
                nk[0:CH, at] = hi
                nk[LANES : LANES + CH, at] = lo
            rows = [cbf[p, row(r0 + half * 4 + i), :] for i in range(4)]
            for k, v in enumerate(pack_rows(rows, lane)):
                at = pl.ds((half * 3 + k) * LANES, LANES)
                hi, lo = halves(v)
                cbk[0:CH, at] = hi
                cbk[LANES : LANES + CH, at] = lo
        def ahead(t):
            at = pl.ds(t * TILE, TILE)
            hid[t % 2] = jnp.dot(upk_ref[...], nk[:, at], preferred_element_type=F32)
            dact[t % 2] = jnp.dot(dnk_ref[...], cbk[:, at], preferred_element_type=F32)

        tiles = CELLS // TILE
        ahead(0)
        for t in range(tiles):
            if t + 1 < tiles:
                ahead(t + 1)
            at = pl.ds(t * TILE, TILE)
            for i in range(HP // 16):
                part = pl.ds(i * 16, 16)
                rest = pl.ds(HP + i * 16, 16)
                act, slope = gelu_parts(hid[t % 2, part, :])
                ahl[part, at], ahl[rest, at] = halves(act)
                dhl[part, at], dhl[rest, at] = halves(slope * dact[t % 2, part, :])
            dnorm[:, at] = jnp.dot(upt_ref[...], dhl[:, at], preferred_element_type=F32)
            if t % 3 == 2:
                three = pl.ds((t - 2) * TILE, 3 * TILE)
                gdn[...] += lax.dot_general(ahl[:, three], cbk[:, three], NT, preferred_element_type=F32)
                gup[...] += lax.dot_general(dhl[:, three], nk[:, three], NT, preferred_element_type=F32)
        for half in range(RB // 4):
            packed = []
            for k in range(3):
                first = (half * 3 + k) * LANES
                at = pl.ds(first, LANES)
                xh = xhat[:, at]
                dxh = dnorm[:, at] * gain
                m1 = jnp.sum(dxh, axis=0, keepdims=True) * (1.0 / 77.0)
                m2 = jnp.sum(dxh * xh, axis=0, keepdims=True) * (1.0 / 77.0)
                v = (dxh - m1 - xh * m2) * rstd[0:1, at]
                packed.append(jnp.where(real, v, 0.0))
            for i, v in enumerate(unpack_rows(packed, lane)):
                at = row(r0 + half * 4 + i + 3)
                dcv[p, at, :] = v
        return carry

    lax.fori_loop(0, 2 * (ROWS // RB), pointwise, 0)

    def back_channel(c, slot):
        band(back_ref, c, slot, -1)
        for p in range(2):
            for parity in range(2):
                v = every_other(dcv, p, parity, c)
                hi = v.astype(BF16).astype(F32)
                lines[slot, 0, 2 * p + parity] = hi
                lines[slot, 1, 2 * p + parity] = v - hi
        for u in range(8):
            for k in range(2):
                data[slot, k * ROWS : (k + 1) * ROWS, u * LANES : (u + 1) * LANES] = moved_rows(slot, k, u)
        out = jnp.dot(data[slot], weights[slot], preferred_element_type=F32)
        out = out[:ROWS] + out[ROWS:]
        for p in range(2):
            for q in range(2):
                at = pl.ds(q * CH + c, ROWS // 2, stride=2 * CH)
                cbf[p, at, :] = cbf[p, at, :] + out[
                    p * (ROWS // 2) : (p + 1) * (ROWS // 2), q * LANES : (q + 1) * LANES
                ]
        total = None
        sub = lax.broadcasted_iota(jnp.int32, (8, LANES), 0)
        lane = lanes(8)
        line = jnp.zeros((8, LANES), F32)
        prods = jnp.dot(xt[c], data[slot], preferred_element_type=F32)
        for a in range(7):
            v = None
            for m in range(12):
                here = [
                    prods[q * SIDE + 8 * m : q * SIDE + 8 * (m + 1), u * LANES : (u + 1) * LANES]
                    for q, u in ((0, 6 - a), (1, 7 - a))
                ]
                t = here[0] + here[1]
                if m:
                    t = pltpu.roll(t, LANES - 8 * m, 1)
                v = t if v is None else v + t
            for bit in (1, 2, 4):
                v = jnp.where((sub // bit) % 2 == 1, pltpu.roll(v, LANES - bit, 1), v)
            v = pltpu.roll(v, 3 + 8 * a, 1)
            line = jnp.where(jnp.logical_and(lane >= 8 * a, lane < 8 * a + 7), v, line)
        sum_ref[pl.ds(2 * HP + c, 1), :] = jnp.sum(line, axis=0, keepdims=True)

    def back_channels(i, carry):
        for slot in range(UNROLL):
            back_channel(i * UNROLL + slot, slot)
        return carry

    lax.fori_loop(0, CH // UNROLL, back_channels, 0)

    def assemble(k, carry):
        lane = lanes(CH)
        edge = [jnp.zeros((CH, LANES), F32)] * 2
        for i in range(8):
            d0 = cbf[0, row(k * 8 + i), :]
            d1 = cbf[1, row(k * 8 + i), :]
            west = jnp.where(lane < 80, pltpu.roll(d0, 112, 1), 0.0)
            east = jnp.where(lane >= 48, pltpu.roll(d1, 48, 1), 0.0)
            field_ref[k * 8 + i] = west + east
            here = jnp.logical_and(lane >= 16 * i, lane < 16 * i + 16)
            for s, d in ((0, d0), (1, d1)):
                moved = pltpu.roll(d, (16 * i + LANES - 80 * s) % LANES, 1)
                edge[s] = jnp.where(here, moved, edge[s])
        for s in range(2):
            rim_ref[s, k] = edge[s]
        return carry

    lax.fori_loop(0, ROWS // 8, assemble, 0)
    for first, ref in ((0, gup), (HP, gdn)):
        total = ref[0:HP, :] + ref[HP : 2 * HP, :]
        sum_ref[first : first + HP, :] = total[:, :LANES] + total[:, LANES:]
    sum_ref[2 * HP + CH :, :] = jnp.zeros((SUM_ROWS - 2 * HP - CH, LANES), F32)


def patches(meta, own, got, strips, blend, weights):
    smem = pl.BlockSpec(memory_space=pltpu.SMEM)
    vmem = pl.BlockSpec(memory_space=pltpu.VMEM)
    return pl.pallas_call(
        patch_kernel,
        name="patches",
        out_shape=(
            jax.ShapeDtypeStruct((ROWS, CH, LANES), F32),
            jax.ShapeDtypeStruct((2, ROWS // 8, CH, LANES), F32),
            jax.ShapeDtypeStruct((SUM_ROWS, LANES), F32),
        ),
        in_specs=[smem] + [vmem] * 11,
        out_specs=(vmem,) * 3,
        scratch_shapes=[
            pltpu.VMEM((2, (ROWS + 16) * CH, LANES), F32),
            pltpu.VMEM((2, ROWS * CH, LANES), F32),
            pltpu.VMEM((2, ROWS * CH, LANES), F32),
            pltpu.VMEM((2, (ROWS + 16) * CH, LANES), F32),
            pltpu.VMEM((2 * LANES, CELLS), BF16),
            pltpu.VMEM((2 * LANES, CELLS), BF16),
            pltpu.VMEM((CH, CELLS), F32),
            pltpu.VMEM((8, CELLS), F32),
            pltpu.VMEM((CH, CELLS), F32),
            pltpu.VMEM((2, HP, TILE), F32),
            pltpu.VMEM((2, HP, TILE), F32),
            pltpu.VMEM((2 * HP, CELLS), BF16),
            pltpu.VMEM((2 * HP, CELLS), BF16),
            pltpu.VMEM((2 * HP, 2 * LANES), F32),
            pltpu.VMEM((2 * HP, 2 * LANES), F32),
            pltpu.VMEM((UNROLL, 8 * LANES, 2 * LANES), BF16),
            pltpu.VMEM((UNROLL, 2 * ROWS, 8 * LANES), BF16),
            pltpu.VMEM((UNROLL, 2, 4, 48, LANES), F32),
            pltpu.VMEM((CH, 2 * SIDE, 2 * ROWS), BF16),
        ],
        compiler_params=pltpu.CompilerParams(vmem_limit_bytes=63 * 1024 * 1024),
    )(meta, own, got, strips, blend, *weights)


def place():
    lon = lax.axis_index("lon")
    lat = lax.axis_index("lat")
    count = lax.axis_size("lon")
    return lon, lat, lax.rem(lon + 1, count), lax.rem(lon + count - 1, count)


def meet(peers):
    barrier = pltpu.get_barrier_semaphore()
    for peer in peers:
        pl.semaphore_signal(barrier, inc=1, device_id=peer, device_id_type=pl.DeviceIdType.MESH)
    pl.semaphore_wait(barrier, len(peers))


def remote(source, target, sems, index, peer):
    return pltpu.make_async_remote_copy(
        src_ref=source,
        dst_ref=target,
        send_sem=sems.at[0, index],
        recv_sem=sems.at[1, index],
        device_id=peer,
        device_id_type=pl.DeviceIdType.MESH,
    )


def halo_kernel(own_ref, got_ref, strips_ref, edges, sems):
    lon, lat, east, west = place()
    other = 1 - lat
    meet([(east, lat), (west, lat), (lon, other), (east, other), (west, other)])
    give = (1 - lat) * 48
    tall = remote(own_ref.at[pl.ds(give, 16)], got_ref, sems, 0, (lon, other))
    tall.start()

    def pack(k, carry):
        lane = lax.broadcasted_iota(jnp.int32, (CH, LANES), 1)
        for part in range(2):
            acc = [jnp.zeros((CH, LANES), F32)] * 2
            for i in range(8):
                v = own_ref[k * 8 + i, part].astype(F32)
                here = jnp.logical_and(lane >= 16 * i, lane < 16 * i + 16)
                for side in range(2):
                    moved = pltpu.roll(v, (16 * i + 16 * side) % LANES, 1)
                    acc[side] = jnp.where(here, moved, acc[side])
            for side in range(2):
                edges[side, k, part] = acc[side].astype(BF16)
        return carry

    lax.fori_loop(0, 8, pack, 0)
    mine = lat * 2
    corner = (1 - lat) * 6
    far = lat * 8
    copies = [tall]
    for side, peer in ((0, west), (1, east)):
        copies.append(
            remote(edges.at[side], strips_ref.at[1 - side, pl.ds(mine, 8)], sems, 1 + side, (peer, lat))
        )
        copies.append(
            remote(
                edges.at[side, pl.ds(corner, 2)], strips_ref.at[1 - side, pl.ds(far, 2)], sems,
                3 + side, (peer, other),
            )
        )
    for copy in copies[1:]:
        copy.start()
    for copy in copies:
        copy.wait()


def halo(own):
    hbm = pl.BlockSpec(memory_space=pl.ANY)
    return pl.pallas_call(
        halo_kernel,
        name="halo",
        out_shape=(
            jax.ShapeDtypeStruct((MARGIN, 2, CH, LANES), BF16),
            jax.ShapeDtypeStruct((2, ROWS // 8, 2, CH, LANES), BF16),
        ),
        in_specs=[pl.BlockSpec(memory_space=pltpu.VMEM)],
        out_specs=(hbm, hbm),
        scratch_shapes=[
            pltpu.VMEM((2, 8, 2, CH, LANES), BF16),
            pltpu.SemaphoreType.DMA((2, 5)),
        ],
        compiler_params=pltpu.CompilerParams(
            collective_id=0, has_side_effects=True, vmem_limit_bytes=32 * 1024 * 1024
        ),
    )(own)


def fold_kernel(
    field_ref, rim_ref, sum_ref,
    out_ref, total_ref,
    edges, rows, near, corner, above, first, second, chunk, sems,
):
    lon, lat, east, west = place()
    other = 1 - lat
    half = lon // 32
    cell = lax.rem(lon, 32) // 2
    core = lax.rem(lon, 2)
    plane = [(half * 32 + lax.rem(cell + d, 16) * 2 + core, lat) for d in range(1, 16)]
    column = (half * 2 + core) * 2 + lat
    cross = []
    for d in range(1, 8):
        j = lax.rem(column + d, 8)
        cross.append(((j // 4) * 32 + cell * 2 + lax.rem(j // 2, 2), lax.rem(j, 2)))
    near_by = [(east, lat), (west, lat), (lon, other), (east, other), (west, other)]
    meet(near_by + plane + cross)

    scatter = []
    for d in range(1, 16):
        to = lax.rem(cell + d, 16)
        copy = remote(
            sum_ref.at[pl.ds(pl.multiple_of(to * PIECE, 8), PIECE)], first.at[d], sems, d, plane[d - 1]
        )
        copy.start()
        scatter.append(copy)

    mine = lat * 2
    far = (1 - lat) * 8
    margin = (1 - lat) * 64

    def narrow_rows(r, carry):
        rows[r] = field_ref[margin + r].astype(BF16)
        return carry

    lax.fori_loop(0, MARGIN, narrow_rows, 0)
    folds = [remote(rows, above, sems, 16, (lon, other))]
    folds[0].start()

    def narrow(q, carry):
        for side in range(2):
            edges[side, q] = rim_ref[side, q].astype(BF16)
        return carry

    lax.fori_loop(0, ROWS // 8, narrow, 0)
    for side, peer in ((0, west), (1, east)):
        folds.append(
            remote(edges.at[side, pl.ds(mine, 8)], near.at[1 - side], sems, 17 + side, (peer, lat))
        )
        folds.append(
            remote(edges.at[side, pl.ds(far, 2)], corner.at[1 - side], sems, 19 + side, (peer, other))
        )
    for copy in folds[1:]:
        copy.start()

    for copy in scatter:
        copy.wait()
    part = sum_ref[pl.ds(pl.multiple_of(cell * PIECE, 8), PIECE), :]
    for d in range(1, 16):
        part = part + first[d]
    second[0] = part
    crossing = []
    for d in range(1, 8):
        copy = remote(second.at[0], second.at[d], sems, 20 + d, cross[d - 1])
        copy.start()
        crossing.append(copy)
    for copy in crossing:
        copy.wait()
    whole = jnp.zeros((PIECE, LANES), F32)
    for j in range(8):
        whole = whole + second[lax.rem(column - j + 8, 8)]
    chunk[...] = whole
    here = pl.ds(pl.multiple_of(cell * PIECE, 8), PIECE)
    total_ref[here, :] = whole
    gather = []
    for d in range(1, 16):
        copy = remote(chunk, total_ref.at[here], sems, 27 + d, plane[d - 1])
        copy.start()
        gather.append(copy)

    for copy in folds:
        copy.wait()

    def finish(k, carry):
        lane = lax.broadcasted_iota(jnp.int32, (CH, LANES), 1)
        from_west = near[0, k].astype(F32)
        from_east = near[1, k].astype(F32)
        for i in range(8):
            w = pltpu.roll(from_west, (LANES - 16 * i) % LANES, 1)
            e = pltpu.roll(from_east, 112 - 16 * i, 1)
            add = jnp.where(lane < 16, w, jnp.where(lane >= 112, e, 0.0))
            out_ref[k * 8 + i] = field_ref[(mine + k) * 8 + i] + add
        return carry

    lax.fori_loop(0, 8, finish, 0)
    base = (1 - lat) * 6

    def finish_corner(k, carry):
        lane = lax.broadcasted_iota(jnp.int32, (CH, LANES), 1)
        from_west = corner[0, k].astype(F32)
        from_east = corner[1, k].astype(F32)
        for i in range(8):
            w = pltpu.roll(from_west, (LANES - 16 * i) % LANES, 1)
            e = pltpu.roll(from_east, 112 - 16 * i, 1)
            add = jnp.where(lane < 16, w, jnp.where(lane >= 112, e, 0.0))
            out_ref[(base + k) * 8 + i] += add + above[k * 8 + i].astype(F32)
        return carry

    lax.fori_loop(0, 2, finish_corner, 0)
    for copy in gather:
        copy.wait()


def fold(field, rim, sums):
    vmem = pl.BlockSpec(memory_space=pltpu.VMEM)
    return pl.pallas_call(
        fold_kernel,
        name="fold",
        out_shape=(
            jax.ShapeDtypeStruct((ROWS - MARGIN, CH, LANES), F32),
            jax.ShapeDtypeStruct((SUM_ROWS, LANES), F32),
        ),
        in_specs=[vmem] * 3,
        out_specs=(vmem,) * 2,
        scratch_shapes=[
            pltpu.VMEM((2, ROWS // 8, CH, LANES), BF16),
            pltpu.VMEM((MARGIN, CH, LANES), BF16),
            pltpu.VMEM((2, 8, CH, LANES), BF16),
            pltpu.VMEM((2, 2, CH, LANES), BF16),
            pltpu.VMEM((MARGIN, CH, LANES), BF16),
            pltpu.VMEM((16, PIECE, LANES), F32),
            pltpu.VMEM((8, PIECE, LANES), F32),
            pltpu.VMEM((PIECE, LANES), F32),
            pltpu.SemaphoreType.DMA((2, 43)),
        ],
        compiler_params=pltpu.CompilerParams(
            collective_id=1, has_side_effects=True, vmem_limit_bytes=48 * 1024 * 1024
        ),
    )(field, rim, sums)


def ramp_table(length, margin):
    offsets = jnp.arange(length, dtype=F32) + 0.5
    return jnp.minimum(1.0, jnp.minimum(offsets / (2.0 * margin), (length - offsets) / (2.0 * margin)))


def padded(array, shape):
    return jnp.pad(array, [(0, want - have) for want, have in zip(shape, array.shape)])


def prepare_weights(kernel, norm_gain, norm_bias, up_weight, up_bias, down_weight):
    by_row = padded(kernel, (CH, 49)).reshape(CH * 7, 7)
    i = jnp.arange(16)[:, None]
    j = (jnp.arange(LANES)[None, :] + 64) % LANES - 64
    bands = []
    for gap in (i - j + 3, j - i + 3):
        band = jnp.zeros((CH * 7, 16, LANES), BF16)
        for b in range(7):
            band = jnp.where((gap == b)[None], by_row[:, b][:, None, None], band)
        bands.append(band)
    gain = jnp.broadcast_to(padded(norm_gain.astype(F32), (CH,))[:, None], (CH, LANES))
    bias = jnp.broadcast_to(padded(norm_bias.astype(F32), (CH,))[:, None], (CH, LANES))
    up = padded(up_weight, (HP, CH))
    gap = jnp.zeros((HP, LANES - CH), BF16)
    upk = jnp.concatenate([up, gap, up, padded(up_bias[:, None], (HP, LANES - CH))], axis=1)
    dn = padded(down_weight.T, (HP, CH))
    dnk = jnp.concatenate([dn, gap, dn, gap], axis=1)
    upt = jnp.concatenate([up.T, up.T], axis=1)
    return *bands, gain, bias, upk, dnk, upt


def blend_rows(lat):
    ramp = ramp_table(SIDE, MARGIN)
    rows = lax.dynamic_slice(ramp, (jnp.where(lat == 0, MARGIN, 0),), (ROWS,))
    cols = padded(ramp, (LANES,))
    return jnp.broadcast_to((rows[:, None] * cols[None, :])[:, None, :], (ROWS, 8, LANES))


def body(
    state_field, cotangent, land_mask, ocean_slots, ocean_count,
    kernel, norm_gain, norm_bias, up_weight, up_bias, down_weight,
):
    channels, height, breadth = state_field.shape
    hidden = up_weight.shape[0]
    lat = lax.axis_index("lat")
    masked = jnp.where(land_mask[None] > 0, cotangent, jnp.zeros_like(cotangent))
    own = jnp.stack([state_field, masked])
    own = jnp.pad(own, ((0, 0), (0, CH - channels), (0, 0), (0, 0)))
    own = jnp.transpose(own, (2, 0, 1, 3))
    got, strips = halo(own)
    weights = prepare_weights(kernel, norm_gain, norm_bias, up_weight, up_bias, down_weight)
    meta = jnp.concatenate(
        [ocean_count.reshape(1), ocean_slots.reshape(2), jnp.stack([lat * 2, (1 - lat) * 8])]
    ).astype(jnp.int32)
    field, rim, sums = patches(meta, own, got, strips, blend_rows(lat), weights)
    out, total = fold(field, rim, sums)
    scale = 1.0 / math.sqrt(height * lax.axis_size("lat") * breadth * lax.axis_size("lon"))
    total = total * scale
    field_grad = jnp.transpose(out, (1, 0, 2))[:channels]
    taps = total[2 * HP : 2 * HP + channels, :56].reshape(channels, 7, 8)
    kernel_grad = taps[:, :, 6::-1].reshape(channels, 49)
    up_grad = total[:hidden, :channels]
    down_grad = total[HP : HP + hidden, :channels].T
    return (field_grad, kernel_grad, up_grad, down_grad)


def solution(mesh):
    in_specs = (
        P(None, "lat", "lon"), P(None, "lat", "lon"), P("lat", "lon"), P("lat", "lon", None),
        P("lat", "lon"), P(), P(), P(), P(), P(), P(),
    )
    out_specs = (P(None, "lat", "lon"), P(), P(), P())
    return jax.shard_map(body, mesh=mesh, in_specs=in_specs, out_specs=out_specs, check_vma=False)
```

```python
import functools
import math

import jax
import jax.numpy as jnp
import numpy as np
from jax import lax
from jax.experimental import pallas as pl
from jax.experimental.pallas import tpu as pltpu
from jax.sharding import PartitionSpec as P

STRIDE = 64
MARGIN = 16
SIDE = 96
ROWS = 80
REAL = 77
CH = 80
HP = 320
LANES = 128
RB = 16
CELLS = RB * SIDE
TILE = 256
UNROLL = 11
SUM_ROWS = 768
PIECE = SUM_ROWS // 16
F32 = jnp.float32
BF16 = jnp.bfloat16

NT = (((1,), (1,)), ((), ()))

ERF_P = 0.3275911 / math.sqrt(2.0)
ERF_C = [0.5 * c for c in (0.254829592, -0.284496736, 1.421413741, -1.453152027, 1.061405429)]


def gelu_parts(h):
    a = jnp.abs(h)
    d = 1.0 + ERF_P * a
    t = pl.reciprocal(d, approx=True)
    t = t * (2.0 - d * t)
    e = jnp.exp2(h * h * (-0.5 / math.log(2.0)))
    q = ERF_C[4] * t + ERF_C[3]
    q = q * t + ERF_C[2]
    q = q * t + ERF_C[1]
    q = q * t + ERF_C[0]
    q = q * (t * e)
    cdf = jnp.where(h > 0, 1.0 - q, q)
    act = h * cdf
    slope = cdf + h * (e * (1.0 / math.sqrt(2.0 * math.pi)))
    return act, slope


def halves(v):
    hi = v.astype(BF16)
    lo = (v - hi.astype(F32)).astype(BF16)
    return hi, lo


def pack_rows(rows, lane):
    r1 = pltpu.roll(rows[1], 96, 1)
    r2 = pltpu.roll(rows[2], 64, 1)
    r3 = pltpu.roll(rows[3], 32, 1)
    return (
        jnp.where(lane < 96, rows[0], r1),
        jnp.where(lane < 64, r1, r2),
        jnp.where(lane < 32, r2, r3),
    )


def unpack_rows(packed, lane):
    live = lane < 96
    v0, v1, v2 = packed
    zero = jnp.zeros_like(v0)
    r1 = pltpu.roll(jnp.where(lane < 96, v1, v0), 32, 1)
    r2 = pltpu.roll(jnp.where(lane < 32, v2, v1), 64, 1)
    r3 = pltpu.roll(v2, 96, 1)
    return tuple(jnp.where(live, r, zero) for r in (v0, r1, r2, r3))


def ramp(index):
    offset = index + 0.5
    return jnp.minimum(1.0, jnp.minimum(offset / (2.0 * MARGIN), (SIDE - offset) / (2.0 * MARGIN)))


def patch_kernel(
    meta_ref, taps_ref, own_ref, got_ref, strips_ref, vec_ref, up_ref, down_ref,
    field_ref, rim_ref, sum_ref,
    xf, conv, cbf, dcv, nk, cbk, xhat, rstd, dnorm, hid, dact, ahl, dhl, gup, gdn, weights, data, lines, xt,
    gain_ref, bias_ref, upk_ref, dnk_ref, upt_ref, wide,
):
    sum_ref[2 * HP :, :] = jnp.zeros((SUM_ROWS - 2 * HP, LANES), F32)
    gup[...] = jnp.zeros(gup.shape, F32)
    gdn[...] = jnp.zeros(gdn.shape, F32)
    for ref in (xf, dcv):
        for p in range(2):
            ref[p, 0 : 3 * CH] = jnp.zeros((3 * CH, LANES), F32)
            ref[p, (ROWS + 3) * CH :] = jnp.zeros((13 * CH, LANES), F32)
    weights[...] = jnp.zeros(weights.shape, BF16)
    nk[CH:LANES, :] = jnp.zeros((LANES - CH, CELLS), BF16)
    cbk[CH:LANES, :] = jnp.zeros((LANES - CH, CELLS), BF16)
    cbk[LANES + CH :, :] = jnp.zeros((LANES - CH, CELLS), BF16)
    ones = lax.broadcasted_iota(jnp.int32, (LANES - CH, CELLS), 0) == 0
    nk[LANES + CH :, :] = jnp.where(ones, 1.0, 0.0).astype(BF16)

    def lanes(n):
        return lax.broadcasted_iota(jnp.int32, (n, LANES), 1)

    for k, ref in ((0, gain_ref), (1, bias_ref)):
        ref[...] = jnp.broadcast_to(vec_ref[k : k + 1, 0:LANES], (LANES, LANES)).T[:CH]
    hidden, channels = up_ref.shape
    wide[...] = jnp.zeros(wide.shape, F32)
    wide[0:hidden, 0:channels] = up_ref[...].astype(F32)
    up = wide[:, 0:LANES]
    up_bias = jnp.broadcast_to(vec_ref[2:3, :], (LANES, 3 * LANES)).T[:HP]
    upk_ref[:, 0:LANES] = up.astype(BF16)
    upk_ref[:, LANES:] = jnp.where(lanes(HP) == CH, up_bias, up).astype(BF16)
    up = up.T[:CH]
    upt_ref[...] = jnp.concatenate([up, up], axis=1).astype(BF16)
    wide[...] = jnp.zeros(wide.shape, F32)
    wide[0:channels, 0:hidden] = down_ref[...].astype(F32)
    down = wide[0:LANES, :].T[:HP].astype(BF16)
    dnk_ref[:, 0:LANES] = down
    dnk_ref[:, LANES:] = down

    def row(r):
        return pl.ds(pl.multiple_of(r * CH, 8), CH)

    def active(s):
        here = jnp.logical_and(meta_ref[0] > 0, meta_ref[1] == s)
        return jnp.logical_or(here, jnp.logical_and(meta_ref[0] > 1, meta_ref[2] == s))

    on = [jnp.where(active(s), 1.0, 0.0) for s in range(2)]

    def widen(source, first, count):
        def group(k, carry):
            lane = lanes(CH)
            q = first + k
            col_ramp = ramp(lanes(8).astype(F32)[0:1])
            row_ramps = [
                ramp(jnp.full((1, LANES), q * 8 + i + 16 - 8 * meta_ref[3], jnp.int32).astype(F32))
                for i in range(8)
            ]
            for s in range(2):
                low, turn, rim = ((16, 16, 0), (0, 80, 80))[s]
                in_own = jnp.logical_and(lane >= low, lane < low + 80)
                in_rim = jnp.logical_and(lane >= rim, lane < rim + 16)
                for part in range(2):
                    edge = strips_ref[s, q, part].astype(F32)
                    for i in range(8):
                        v = pltpu.roll(source[k * 8 + i, part].astype(F32), turn, 1)
                        e = pltpu.roll(edge, (rim + LANES - 16 * i) % LANES, 1)
                        v = jnp.where(in_own, v, jnp.where(in_rim, e, 0.0))
                        if part == 0:
                            xf[s, row(q * 8 + i + 3), :] = v
                        else:
                            cbf[s, row(q * 8 + i), :] = v * (row_ramps[i] * col_ramp * on[s])
            return carry

        lax.fori_loop(0, count, group, 0)

    widen(own_ref, meta_ref[3], 8)
    widen(got_ref, meta_ref[4], 2)

    def band(c, slot, sign):
        i = lax.broadcasted_iota(jnp.int32, (16, LANES), 0)
        j = lanes(16)
        j = jnp.where(j >= 64, j - LANES, j)
        gap = (i - j) * sign + 3
        for a in range(7):
            base = jnp.zeros((16, LANES), F32)
            for b in range(7):
                base = jnp.where(gap == b, taps_ref[c * 49 + a * 7 + b], base)
            for m in range(6):
                tile = (base if m == 0 else pltpu.roll(base, 16 * m, 1)).astype(BF16)
                for q in range(2):
                    u = a + q if sign > 0 else q + 6 - a
                    weights[slot, u * LANES + 16 * m : u * LANES + 16 * (m + 1), q * LANES : (q + 1) * LANES] = tile

    def every_other(ref, p, parity, c):
        return ref[p, pl.ds(parity * CH + c, 48, stride=2 * CH), :]

    def moved_rows(slot, kind, u):
        near = u // 2
        return jnp.concatenate(
            [lines[slot, kind, 2 * p + u % 2, near : near + ROWS // 2] for p in range(2)], axis=0
        ).astype(BF16)

    def conv_channel(c, slot):
        band(c, slot, 1)
        for p in range(2):
            for parity in range(2):
                lines[slot, 0, 2 * p + parity] = every_other(xf, p, parity, c)
        for u in range(8):
            data[slot, 0:ROWS, u * LANES : (u + 1) * LANES] = moved_rows(slot, 0, u)
        for q in range(2):
            near = (q + 3) // 2
            v = jnp.concatenate(
                [lines[slot, 0, 2 * p + (q + 3) % 2, near : near + ROWS // 2] for p in range(2)], axis=0
            )
            v = v.T[:SIDE].astype(BF16)
            xt[c, q * SIDE : (q + 1) * SIDE] = jnp.concatenate([v, v], axis=1)
        out = jnp.dot(data[slot, 0:ROWS, :], weights[slot], preferred_element_type=F32)
        for p in range(2):
            for q in range(2):
                conv[p, pl.ds(q * CH + c, ROWS // 2, stride=2 * CH), :] = out[
                    p * (ROWS // 2) : (p + 1) * (ROWS // 2), q * LANES : (q + 1) * LANES
                ]

    def conv_channels(i, carry):
        for slot in range(UNROLL):
            conv_channel(i * UNROLL + slot, slot)
        return carry

    lax.fori_loop(0, REAL // UNROLL, conv_channels, 0)

    def pointwise(index, carry):
        p = index // (ROWS // RB)
        r0 = (index % (ROWS // RB)) * RB
        lane = lanes(CH)
        real = lax.broadcasted_iota(jnp.int32, (CH, LANES), 0) < 77
        gain = gain_ref[...]
        bias = bias_ref[...]
        for half in range(RB // 4):
            rows = [conv[p, row(r0 + half * 4 + i), :] for i in range(4)]
            for k, v in enumerate(pack_rows(rows, lane)):
                at = pl.ds((half * 3 + k) * LANES, LANES)
                mean = jnp.sum(jnp.where(real, v, 0.0), axis=0, keepdims=True) * (1.0 / 77.0)
                cen = jnp.where(real, v - mean, 0.0)
                var = jnp.sum(cen * cen, axis=0, keepdims=True) * (1.0 / 77.0)
                rs = lax.rsqrt(var + 1e-06)
                xh = cen * rs
                xhat[:, at] = xh
                rstd[:, at] = jnp.broadcast_to(rs, (8, LANES))
                hi, lo = halves(xh * gain + bias)
                nk[0:CH, at] = hi
                nk[LANES : LANES + CH, at] = lo
            rows = [cbf[p, row(r0 + half * 4 + i), :] for i in range(4)]
            for k, v in enumerate(pack_rows(rows, lane)):
                at = pl.ds((half * 3 + k) * LANES, LANES)
                hi, lo = halves(v)
                cbk[0:CH, at] = hi
                cbk[LANES : LANES + CH, at] = lo
        def ahead(t):
            at = pl.ds(t * TILE, TILE)
            hid[t % 2] = jnp.dot(upk_ref[...], nk[:, at], preferred_element_type=F32)
            dact[t % 2] = jnp.dot(dnk_ref[...], cbk[:, at], preferred_element_type=F32)

        tiles = CELLS // TILE
        ahead(0)
        for t in range(tiles):
            if t + 1 < tiles:
                ahead(t + 1)
            at = pl.ds(t * TILE, TILE)
            for i in range(HP // 16):
                part = pl.ds(i * 16, 16)
                rest = pl.ds(HP + i * 16, 16)
                act, slope = gelu_parts(hid[t % 2, part, :])
                ahl[part, at], ahl[rest, at] = halves(act)
                dhl[part, at], dhl[rest, at] = halves(slope * dact[t % 2, part, :])
            dnorm[:, at] = jnp.dot(upt_ref[...], dhl[:, at], preferred_element_type=F32)
            if t % 3 == 2:
                three = pl.ds((t - 2) * TILE, 3 * TILE)
                gdn[...] += lax.dot_general(ahl[:, three], cbk[:, three], NT, preferred_element_type=F32)
                gup[...] += lax.dot_general(dhl[:, three], nk[:, three], NT, preferred_element_type=F32)
        for half in range(RB // 4):
            packed = []
            for k in range(3):
                first = (half * 3 + k) * LANES
                at = pl.ds(first, LANES)
                xh = xhat[:, at]
                dxh = dnorm[:, at] * gain
                m1 = jnp.sum(dxh, axis=0, keepdims=True) * (1.0 / 77.0)
                m2 = jnp.sum(dxh * xh, axis=0, keepdims=True) * (1.0 / 77.0)
                v = (dxh - m1 - xh * m2) * rstd[0:1, at]
                packed.append(jnp.where(real, v, 0.0))
            for i, v in enumerate(unpack_rows(packed, lane)):
                at = row(r0 + half * 4 + i + 3)
                dcv[p, at, :] = v
        return carry

    lax.fori_loop(0, 2 * (ROWS // RB), pointwise, 0)

    def back_channel(c, slot):
        band(c, slot, -1)
        for p in range(2):
            for parity in range(2):
                v = every_other(dcv, p, parity, c)
                hi = v.astype(BF16).astype(F32)
                lines[slot, 0, 2 * p + parity] = hi
                lines[slot, 1, 2 * p + parity] = v - hi
        for u in range(8):
            for k in range(2):
                data[slot, k * ROWS : (k + 1) * ROWS, u * LANES : (u + 1) * LANES] = moved_rows(slot, k, u)
        out = jnp.dot(data[slot], weights[slot], preferred_element_type=F32)
        out = out[:ROWS] + out[ROWS:]
        for p in range(2):
            for q in range(2):
                at = pl.ds(q * CH + c, ROWS // 2, stride=2 * CH)
                cbf[p, at, :] = cbf[p, at, :] + out[
                    p * (ROWS // 2) : (p + 1) * (ROWS // 2), q * LANES : (q + 1) * LANES
                ]
        total = None
        sub = lax.broadcasted_iota(jnp.int32, (8, LANES), 0)
        lane = lanes(8)
        line = jnp.zeros((8, LANES), F32)
        prods = jnp.dot(xt[c], data[slot], preferred_element_type=F32)
        for a in range(7):
            v = None
            for m in range(12):
                here = [
                    prods[q * SIDE + 8 * m : q * SIDE + 8 * (m + 1), u * LANES : (u + 1) * LANES]
                    for q, u in ((0, 6 - a), (1, 7 - a))
                ]
                t = here[0] + here[1]
                if m:
                    t = pltpu.roll(t, LANES - 8 * m, 1)
                v = t if v is None else v + t
            for bit in (1, 2, 4):
                v = jnp.where((sub // bit) % 2 == 1, pltpu.roll(v, LANES - bit, 1), v)
            v = pltpu.roll(v, 3 + 8 * a, 1)
            line = jnp.where(jnp.logical_and(lane >= 8 * a, lane < 8 * a + 7), v, line)
        sum_ref[pl.ds(2 * HP + c, 1), :] = jnp.sum(line, axis=0, keepdims=True)

    def back_channels(i, carry):
        for slot in range(UNROLL):
            back_channel(i * UNROLL + slot, slot)
        return carry

    lax.fori_loop(0, REAL // UNROLL, back_channels, 0)

    def assemble(k, carry):
        lane = lanes(CH)
        edge = [jnp.zeros((CH, LANES), F32)] * 2
        for i in range(8):
            d0 = cbf[0, row(k * 8 + i), :]
            d1 = cbf[1, row(k * 8 + i), :]
            west = jnp.where(lane < 80, pltpu.roll(d0, 112, 1), 0.0)
            east = jnp.where(lane >= 48, pltpu.roll(d1, 48, 1), 0.0)
            field_ref[k * 8 + i] = west + east
            here = jnp.logical_and(lane >= 16 * i, lane < 16 * i + 16)
            for s, d in ((0, d0), (1, d1)):
                moved = pltpu.roll(d, (16 * i + LANES - 80 * s) % LANES, 1)
                edge[s] = jnp.where(here, moved, edge[s])
        for s in range(2):
            rim_ref[s, k] = edge[s]
        return carry

    lax.fori_loop(0, ROWS // 8, assemble, 0)
    for first, ref in ((0, gup), (HP, gdn)):
        total = ref[0:HP, :] + ref[HP : 2 * HP, :]
        sum_ref[first : first + HP, :] = total[:, :LANES] + total[:, LANES:]


def patches(meta, own, got, strips, weights):
    taps, *rest = weights
    smem = pl.BlockSpec(memory_space=pltpu.SMEM)
    vmem = pl.BlockSpec(memory_space=pltpu.VMEM)
    return pl.pallas_call(
        patch_kernel,
        name="patches",
        out_shape=(
            jax.ShapeDtypeStruct((ROWS, CH, LANES), F32),
            jax.ShapeDtypeStruct((2, ROWS // 8, CH, LANES), F32),
            jax.ShapeDtypeStruct((SUM_ROWS, LANES), F32),
        ),
        in_specs=[smem] * 2 + [vmem] * 6,
        out_specs=(vmem,) * 3,
        scratch_shapes=[
            pltpu.VMEM((2, (ROWS + 16) * CH, LANES), F32),
            pltpu.VMEM((2, ROWS * CH, LANES), F32),
            pltpu.VMEM((2, ROWS * CH, LANES), F32),
            pltpu.VMEM((2, (ROWS + 16) * CH, LANES), F32),
            pltpu.VMEM((2 * LANES, CELLS), BF16),
            pltpu.VMEM((2 * LANES, CELLS), BF16),
            pltpu.VMEM((CH, CELLS), F32),
            pltpu.VMEM((8, CELLS), F32),
            pltpu.VMEM((CH, CELLS), F32),
            pltpu.VMEM((2, HP, TILE), F32),
            pltpu.VMEM((2, HP, TILE), F32),
            pltpu.VMEM((2 * HP, CELLS), BF16),
            pltpu.VMEM((2 * HP, CELLS), BF16),
            pltpu.VMEM((2 * HP, 2 * LANES), F32),
            pltpu.VMEM((2 * HP, 2 * LANES), F32),
            pltpu.VMEM((UNROLL, 8 * LANES, 2 * LANES), BF16),
            pltpu.VMEM((UNROLL, 2 * ROWS, 8 * LANES), BF16),
            pltpu.VMEM((UNROLL, 2, 4, 48, LANES), F32),
            pltpu.VMEM((REAL, 2 * SIDE, 2 * ROWS), BF16),
            pltpu.VMEM((CH, LANES), F32),
            pltpu.VMEM((CH, LANES), F32),
            pltpu.VMEM((HP, 2 * LANES), BF16),
            pltpu.VMEM((HP, 2 * LANES), BF16),
            pltpu.VMEM((CH, 2 * HP), BF16),
            pltpu.VMEM((HP, 3 * LANES), F32),
        ],
        compiler_params=pltpu.CompilerParams(vmem_limit_bytes=63 * 1024 * 1024),
    )(meta, taps, own, got, strips, *rest)


def place():
    lon = lax.axis_index("lon")
    lat = lax.axis_index("lat")
    count = lax.axis_size("lon")
    return lon, lat, lax.rem(lon + 1, count), lax.rem(lon + count - 1, count)


def meet(peers):
    barrier = pltpu.get_barrier_semaphore()
    for peer in peers:
        pl.semaphore_signal(barrier, inc=1, device_id=peer, device_id_type=pl.DeviceIdType.MESH)
    pl.semaphore_wait(barrier, len(peers))


def remote(source, target, sems, index, peer):
    return pltpu.make_async_remote_copy(
        src_ref=source,
        dst_ref=target,
        send_sem=sems.at[0, index],
        recv_sem=sems.at[1, index],
        device_id=peer,
        device_id_type=pl.DeviceIdType.MESH,
    )


def halo_kernel(own_ref, got_ref, strips_ref, edges, sems):
    lon, lat, east, west = place()
    other = 1 - lat
    meet([(east, lat), (west, lat), (lon, other), (east, other), (west, other)])
    give = (1 - lat) * 48
    tall = remote(own_ref.at[pl.ds(give, 16)], got_ref, sems, 0, (lon, other))
    tall.start()

    def pack(k, carry):
        lane = lax.broadcasted_iota(jnp.int32, (CH, LANES), 1)
        for part in range(2):
            acc = [jnp.zeros((CH, LANES), F32)] * 2
            for i in range(8):
                v = own_ref[k * 8 + i, part].astype(F32)
                here = jnp.logical_and(lane >= 16 * i, lane < 16 * i + 16)
                for side in range(2):
                    moved = pltpu.roll(v, (16 * i + 16 * side) % LANES, 1)
                    acc[side] = jnp.where(here, moved, acc[side])
            for side in range(2):
                edges[side, k, part] = acc[side].astype(BF16)
        return carry

    lax.fori_loop(0, 8, pack, 0)
    mine = lat * 2
    corner = (1 - lat) * 6
    far = lat * 8
    copies = [tall]
    for side, peer in ((0, west), (1, east)):
        copies.append(
            remote(edges.at[side], strips_ref.at[1 - side, pl.ds(mine, 8)], sems, 1 + side, (peer, lat))
        )
        copies.append(
            remote(
                edges.at[side, pl.ds(corner, 2)], strips_ref.at[1 - side, pl.ds(far, 2)], sems,
                3 + side, (peer, other),
            )
        )
    for copy in copies[1:]:
        copy.start()
    for copy in copies:
        copy.wait()


def halo(own):
    hbm = pl.BlockSpec(memory_space=pl.ANY)
    return pl.pallas_call(
        halo_kernel,
        name="halo",
        out_shape=(
            jax.ShapeDtypeStruct((MARGIN, 2, CH, LANES), BF16),
            jax.ShapeDtypeStruct((2, ROWS // 8, 2, CH, LANES), BF16),
        ),
        in_specs=[pl.BlockSpec(memory_space=pltpu.VMEM)],
        out_specs=(hbm, hbm),
        scratch_shapes=[
            pltpu.VMEM((2, 8, 2, CH, LANES), BF16),
            pltpu.SemaphoreType.DMA((2, 5)),
        ],
        compiler_params=pltpu.CompilerParams(
            collective_id=0, has_side_effects=True, vmem_limit_bytes=32 * 1024 * 1024
        ),
    )(own)


def fold_kernel(
    field_ref, rim_ref, sum_ref,
    out_ref, total_ref,
    edges, rows, near, corner, above, first, second, chunk, sems,
):
    lon, lat, east, west = place()
    other = 1 - lat
    half = lon // 32
    cell = lax.rem(lon, 32) // 2
    core = lax.rem(lon, 2)
    plane = [(half * 32 + lax.rem(cell + d, 16) * 2 + core, lat) for d in range(1, 16)]
    column = (half * 2 + core) * 2 + lat
    cross = []
    for d in range(1, 8):
        j = lax.rem(column + d, 8)
        cross.append(((j // 4) * 32 + cell * 2 + lax.rem(j // 2, 2), lax.rem(j, 2)))
    near_by = [(east, lat), (west, lat), (lon, other), (east, other), (west, other)]
    meet(near_by + plane + cross)

    scatter = []
    for d in range(1, 16):
        to = lax.rem(cell + d, 16)
        copy = remote(
            sum_ref.at[pl.ds(pl.multiple_of(to * PIECE, 8), PIECE)], first.at[d], sems, d, plane[d - 1]
        )
        copy.start()
        scatter.append(copy)

    mine = lat * 2
    far = (1 - lat) * 8
    margin = (1 - lat) * 64

    def narrow_rows(r, carry):
        rows[r] = field_ref[margin + r].astype(BF16)
        return carry

    lax.fori_loop(0, MARGIN, narrow_rows, 0)
    folds = [remote(rows, above, sems, 16, (lon, other))]
    folds[0].start()

    def narrow(q, carry):
        for side in range(2):
            edges[side, q] = rim_ref[side, q].astype(BF16)
        return carry

    lax.fori_loop(0, ROWS // 8, narrow, 0)
    for side, peer in ((0, west), (1, east)):
        folds.append(
            remote(edges.at[side, pl.ds(mine, 8)], near.at[1 - side], sems, 17 + side, (peer, lat))
        )
        folds.append(
            remote(edges.at[side, pl.ds(far, 2)], corner.at[1 - side], sems, 19 + side, (peer, other))
        )
    for copy in folds[1:]:
        copy.start()

    for copy in scatter:
        copy.wait()
    part = sum_ref[pl.ds(pl.multiple_of(cell * PIECE, 8), PIECE), :]
    for d in range(1, 16):
        part = part + first[d]
    second[0] = part
    crossing = []
    for d in range(1, 8):
        copy = remote(second.at[0], second.at[d], sems, 20 + d, cross[d - 1])
        copy.start()
        crossing.append(copy)
    for copy in crossing:
        copy.wait()
    whole = jnp.zeros((PIECE, LANES), F32)
    for j in range(8):
        whole = whole + second[lax.rem(column - j + 8, 8)]
    chunk[...] = whole
    here = pl.ds(pl.multiple_of(cell * PIECE, 8), PIECE)
    total_ref[here, :] = whole
    gather = []
    for d in range(1, 16):
        copy = remote(chunk, total_ref.at[here], sems, 27 + d, plane[d - 1])
        copy.start()
        gather.append(copy)

    for copy in folds:
        copy.wait()

    def finish(k, carry):
        lane = lax.broadcasted_iota(jnp.int32, (CH, LANES), 1)
        from_west = near[0, k].astype(F32)
        from_east = near[1, k].astype(F32)
        for i in range(8):
            w = pltpu.roll(from_west, (LANES - 16 * i) % LANES, 1)
            e = pltpu.roll(from_east, 112 - 16 * i, 1)
            add = jnp.where(lane < 16, w, jnp.where(lane >= 112, e, 0.0))
            out_ref[k * 8 + i] = field_ref[(mine + k) * 8 + i] + add
        return carry

    lax.fori_loop(0, 8, finish, 0)
    base = (1 - lat) * 6

    def finish_corner(k, carry):
        lane = lax.broadcasted_iota(jnp.int32, (CH, LANES), 1)
        from_west = corner[0, k].astype(F32)
        from_east = corner[1, k].astype(F32)
        for i in range(8):
            w = pltpu.roll(from_west, (LANES - 16 * i) % LANES, 1)
            e = pltpu.roll(from_east, 112 - 16 * i, 1)
            add = jnp.where(lane < 16, w, jnp.where(lane >= 112, e, 0.0))
            out_ref[(base + k) * 8 + i] += add + above[k * 8 + i].astype(F32)
        return carry

    lax.fori_loop(0, 2, finish_corner, 0)
    for copy in gather:
        copy.wait()


def fold(field, rim, sums):
    vmem = pl.BlockSpec(memory_space=pltpu.VMEM)
    return pl.pallas_call(
        fold_kernel,
        name="fold",
        out_shape=(
            jax.ShapeDtypeStruct((ROWS - MARGIN, CH, LANES), F32),
            jax.ShapeDtypeStruct((SUM_ROWS, LANES), F32),
        ),
        in_specs=[vmem] * 3,
        out_specs=(vmem,) * 2,
        scratch_shapes=[
            pltpu.VMEM((2, ROWS // 8, CH, LANES), BF16),
            pltpu.VMEM((MARGIN, CH, LANES), BF16),
            pltpu.VMEM((2, 8, CH, LANES), BF16),
            pltpu.VMEM((2, 2, CH, LANES), BF16),
            pltpu.VMEM((MARGIN, CH, LANES), BF16),
            pltpu.VMEM((16, PIECE, LANES), F32),
            pltpu.VMEM((8, PIECE, LANES), F32),
            pltpu.VMEM((PIECE, LANES), F32),
            pltpu.SemaphoreType.DMA((2, 43)),
        ],
        compiler_params=pltpu.CompilerParams(
            collective_id=1, has_side_effects=True, vmem_limit_bytes=48 * 1024 * 1024
        ),
    )(field, rim, sums)


def prepare_weights(kernel, norm_gain, norm_bias, up_weight, up_bias, down_weight):
    width = 3 * LANES
    vectors = jnp.stack(
        [jnp.pad(v, (0, width - v.shape[0])) for v in (norm_gain, norm_bias, up_bias)]
    ).astype(F32)
    return kernel.astype(F32).reshape(-1), vectors, up_weight, down_weight


def body(
    state_field, cotangent, land_mask, ocean_slots, ocean_count,
    kernel, norm_gain, norm_bias, up_weight, up_bias, down_weight,
):
    channels, height, breadth = state_field.shape
    hidden = up_weight.shape[0]
    lat = lax.axis_index("lat")
    masked = jnp.where(land_mask[None] > 0, cotangent, jnp.zeros_like(cotangent))
    own = jnp.stack([state_field, masked])
    own = jnp.pad(own, ((0, 0), (0, CH - channels), (0, 0), (0, 0)))
    own = jnp.transpose(own, (2, 0, 1, 3))
    got, strips = halo(own)
    weights = prepare_weights(kernel, norm_gain, norm_bias, up_weight, up_bias, down_weight)
    meta = jnp.concatenate(
        [ocean_count.reshape(1), ocean_slots.reshape(2), jnp.stack([lat * 2, (1 - lat) * 8])]
    ).astype(jnp.int32)
    field, rim, sums = patches(meta, own, got, strips, weights)
    out, total = fold(field, rim, sums)
    scale = 1.0 / math.sqrt(height * lax.axis_size("lat") * breadth * lax.axis_size("lon"))
    total = total * scale
    field_grad = jnp.transpose(out, (1, 0, 2))[:channels]
    taps = total[2 * HP : 2 * HP + channels, :56].reshape(channels, 7, 8)
    kernel_grad = taps[:, :, 6::-1].reshape(channels, 49)
    up_grad = total[:hidden, :channels]
    down_grad = total[HP : HP + hidden, :channels].T
    return (field_grad, kernel_grad, up_grad, down_grad)


def solution(mesh):
    in_specs = (
        P(None, "lat", "lon"), P(None, "lat", "lon"), P("lat", "lon"), P("lat", "lon", None),
        P("lat", "lon"), P(), P(), P(), P(), P(), P(),
    )
    out_specs = (P(None, "lat", "lon"), P(), P(), P())
    return jax.shard_map(body, mesh=mesh, in_specs=in_specs, out_specs=out_specs, check_vma=False)
```

```python
import functools
import math

import jax
import jax.numpy as jnp
import numpy as np
from jax import lax
from jax.experimental import pallas as pl
from jax.experimental.pallas import tpu as pltpu
from jax.sharding import PartitionSpec as P

STRIDE = 64
MARGIN = 16
SIDE = 96
ROWS = 80
REAL = 77
CH = 80
HP = 320
LANES = 128
RB = 16
CELLS = RB * SIDE
TILE = 256
UNROLL = 7
PIECE = 2 * HP // 16
TAPS = 128
F32 = jnp.float32
BF16 = jnp.bfloat16

NT = (((1,), (1,)), ((), ()))

ERF_P = 0.3275911 / math.sqrt(2.0)
ERF_C = [0.5 * c for c in (0.254829592, -0.284496736, 1.421413741, -1.453152027, 1.061405429)]


def gelu_parts(h):
    a = jnp.abs(h)
    d = 1.0 + ERF_P * a
    t = pl.reciprocal(d, approx=True)
    t = t * (2.0 - d * t)
    e = jnp.exp2(h * h * (-0.5 / math.log(2.0)))
    q = ERF_C[4] * t + ERF_C[3]
    q = q * t + ERF_C[2]
    q = q * t + ERF_C[1]
    q = q * t + ERF_C[0]
    q = q * (t * e)
    cdf = jnp.where(h > 0, 1.0 - q, q)
    act = h * cdf
    slope = cdf + h * (e * (1.0 / math.sqrt(2.0 * math.pi)))
    return act, slope


def halves(v):
    hi = v.astype(BF16)
    lo = (v - hi.astype(F32)).astype(BF16)
    return hi, lo


def pack_rows(rows, lane):
    r1 = pltpu.roll(rows[1], 96, 1)
    r2 = pltpu.roll(rows[2], 64, 1)
    r3 = pltpu.roll(rows[3], 32, 1)
    return (
        jnp.where(lane < 96, rows[0], r1),
        jnp.where(lane < 64, r1, r2),
        jnp.where(lane < 32, r2, r3),
    )


def unpack_rows(packed, lane):
    live = lane < 96
    v0, v1, v2 = packed
    zero = jnp.zeros_like(v0)
    r1 = pltpu.roll(jnp.where(lane < 96, v1, v0), 32, 1)
    r2 = pltpu.roll(jnp.where(lane < 32, v2, v1), 64, 1)
    r3 = pltpu.roll(v2, 96, 1)
    return tuple(jnp.where(live, r, zero) for r in (v0, r1, r2, r3))


def place():
    lon = lax.axis_index("lon")
    lat = lax.axis_index("lat")
    count = lax.axis_size("lon")
    return lon, lat, lax.rem(lon + 1, count), lax.rem(lon + count - 1, count)


def meet(peers):
    barrier = pltpu.get_barrier_semaphore()
    for peer in peers:
        pl.semaphore_signal(barrier, inc=1, device_id=peer, device_id_type=pl.DeviceIdType.MESH)
    pl.semaphore_wait(barrier, len(peers))


def remote(source, target, sems, index, peer):
    return pltpu.make_async_remote_copy(
        src_ref=source,
        dst_ref=target,
        send_sem=sems.at[0, index],
        recv_sem=sems.at[1, index],
        device_id=peer,
        device_id_type=pl.DeviceIdType.MESH,
    )


def ramp(index):
    offset = index + 0.5
    return jnp.minimum(1.0, jnp.minimum(offset / (2.0 * MARGIN), (SIDE - offset) / (2.0 * MARGIN)))


def patch_kernel(
    count_ref, slots_ref, taps_ref, own_ref, vec_ref, up_ref, down_ref,
    out_ref, total_ref, taps_out_ref,
    xf, conv, cbf, dcv, nk, cbk, xhat, rstd, dnorm, hid, dact, ahl, dhl, gup, gdn, weights, data,
    lines, xt, gain_ref, bias_ref, upk_ref, dnk_ref, upt_ref, wide,
    edges, got_ref, strips_ref, rims, rows, near, corner, above,
    sum_ref, first, second, chunk, ksum, kfirst, ksecond, kchunk, sems,
):
    lon, lat, east, west = place()
    other = 1 - lat
    half = lon // 32
    cell = lax.rem(lon, 32) // 2
    core = lax.rem(lon, 2)
    plane = [(half * 32 + lax.rem(cell + d, 16) * 2 + core, lat) for d in range(1, 16)]
    column = (half * 2 + core) * 2 + lat
    cross = []
    for d in range(1, 8):
        j = lax.rem(column + d, 8)
        cross.append(((j // 4) * 32 + cell * 2 + lax.rem(j // 2, 2), lax.rem(j, 2)))
    near_by = [(east, lat), (west, lat), (lon, other), (east, other), (west, other)]
    meet(near_by + plane + cross)
    mine = lat * 2
    theirs = (1 - lat) * 8

    give = (1 - lat) * 48
    halo = [remote(own_ref.at[pl.ds(give, 16)], got_ref, sems, 0, (lon, other))]
    halo[0].start()

    def pack(k, carry):
        lane = lax.broadcasted_iota(jnp.int32, (CH, LANES), 1)
        for part in range(2):
            acc = [jnp.zeros((CH, LANES), F32)] * 2
            for i in range(8):
                v = own_ref[k * 8 + i, part].astype(F32)
                here = jnp.logical_and(lane >= 16 * i, lane < 16 * i + 16)
                for side in range(2):
                    moved = pltpu.roll(v, (16 * i + 16 * side) % LANES, 1)
                    acc[side] = jnp.where(here, moved, acc[side])
            for side in range(2):
                edges[side, k, part] = acc[side].astype(BF16)
        return carry

    lax.fori_loop(0, 8, pack, 0)
    for side, peer in ((0, west), (1, east)):
        halo.append(
            remote(edges.at[side], strips_ref.at[1 - side, pl.ds(mine, 8)], sems, 1 + side, (peer, lat))
        )
        halo.append(
            remote(
                edges.at[side, pl.ds((1 - lat) * 6, 2)],
                strips_ref.at[1 - side, pl.ds(lat * 8, 2)],
                sems, 3 + side, (peer, other),
            )
        )
    for copy in halo[1:]:
        copy.start()

    def spread(source, size, slots, base):
        return [
            remote(
                source.at[pl.ds(pl.multiple_of(lax.rem(cell + d, 16) * size, 8), size)],
                slots.at[d], sems, base + d, plane[d - 1],
            )
            for d in range(1, 16)
        ]

    def across(slots, base):
        return [remote(slots.at[0], slots.at[d], sems, base + d, cross[d - 1]) for d in range(1, 8)]

    def collect(source, target, size, base):
        here = pl.ds(pl.multiple_of(cell * size, 8), size)
        return [
            remote(source, target.at[here], sems, base + d, plane[d - 1]) for d in range(1, 16)
        ]

    def start(copies):
        for copy in copies:
            copy.start()

    def wait(copies):
        for copy in copies:
            copy.wait()

    def piece_sum(source, size, slots):
        part = source[pl.ds(pl.multiple_of(cell * size, 8), size), :]
        for d in range(1, 16):
            part = part + slots[d]
        return part

    def column_sum(slots, size):
        whole = jnp.zeros((size, LANES), F32)
        for j in range(8):
            whole = whole + slots[lax.rem(column - j + 8, 8)]
        return whole

    ksum[...] = jnp.zeros(ksum.shape, F32)
    gup[...] = jnp.zeros(gup.shape, F32)
    gdn[...] = jnp.zeros(gdn.shape, F32)
    for ref in (xf, dcv):
        for p in range(2):
            ref[p, 0 : 3 * CH] = jnp.zeros((3 * CH, LANES), F32)
            ref[p, (ROWS + 3) * CH :] = jnp.zeros((13 * CH, LANES), F32)
    weights[...] = jnp.zeros(weights.shape, BF16)
    nk[CH:LANES, :] = jnp.zeros((LANES - CH, CELLS), BF16)
    cbk[CH:LANES, :] = jnp.zeros((LANES - CH, CELLS), BF16)
    cbk[LANES + CH :, :] = jnp.zeros((LANES - CH, CELLS), BF16)
    ones = lax.broadcasted_iota(jnp.int32, (LANES - CH, CELLS), 0) == 0
    nk[LANES + CH :, :] = jnp.where(ones, 1.0, 0.0).astype(BF16)

    def lanes(n):
        return lax.broadcasted_iota(jnp.int32, (n, LANES), 1)

    for k, ref in ((0, gain_ref), (1, bias_ref)):
        ref[...] = jnp.broadcast_to(vec_ref[k : k + 1, 0:LANES], (LANES, LANES)).T[:CH]
    hidden, channels = up_ref.shape
    wide[...] = jnp.zeros(wide.shape, F32)
    wide[0:hidden, 0:channels] = up_ref[...].astype(F32)
    up = wide[:, 0:LANES]
    up_bias = jnp.broadcast_to(vec_ref[2:3, :], (LANES, 3 * LANES)).T[:HP]
    upk_ref[:, 0:LANES] = up.astype(BF16)
    upk_ref[:, LANES:] = jnp.where(lanes(HP) == CH, up_bias, up).astype(BF16)
    up = up.T[:CH]
    upt_ref[...] = jnp.concatenate([up, up], axis=1).astype(BF16)
    wide[...] = jnp.zeros(wide.shape, F32)
    wide[0:channels, 0:hidden] = down_ref[...].astype(F32)
    down = wide[0:LANES, :].T[:HP].astype(BF16)
    dnk_ref[:, 0:LANES] = down
    dnk_ref[:, LANES:] = down

    def row(r):
        return pl.ds(pl.multiple_of(r * CH, 8), CH)

    def active(s):
        here = jnp.logical_and(count_ref[0] > 0, slots_ref[0] == s)
        return jnp.logical_or(here, jnp.logical_and(count_ref[0] > 1, slots_ref[1] == s))

    on = [jnp.where(active(s), 1.0, 0.0) for s in range(2)]

    def widen(source, first, count):
        def group(k, carry):
            lane = lanes(CH)
            q = first + k
            col_ramp = ramp(lanes(8).astype(F32)[0:1])
            row_ramps = [
                ramp(jnp.full((1, LANES), q * 8 + i + 16 - 16 * lat, jnp.int32).astype(F32))
                for i in range(8)
            ]
            for s in range(2):
                low, turn, rim = ((16, 16, 0), (0, 80, 80))[s]
                in_own = jnp.logical_and(lane >= low, lane < low + 80)
                in_rim = jnp.logical_and(lane >= rim, lane < rim + 16)
                for part in range(2):
                    edge = strips_ref[s, q, part].astype(F32)
                    for i in range(8):
                        v = pltpu.roll(source[k * 8 + i, part].astype(F32), turn, 1)
                        e = pltpu.roll(edge, (rim + LANES - 16 * i) % LANES, 1)
                        v = jnp.where(in_own, v, jnp.where(in_rim, e, 0.0))
                        if part == 0:
                            xf[s, row(q * 8 + i + 3), :] = v
                        else:
                            cbf[s, row(q * 8 + i), :] = v * (row_ramps[i] * col_ramp * on[s])
            return carry

        lax.fori_loop(0, count, group, 0)

    wait(halo)
    widen(own_ref, mine, 8)
    widen(got_ref, theirs, 2)

    def band(c, slot, sign):
        i = lax.broadcasted_iota(jnp.int32, (16, LANES), 0)
        j = lanes(16)
        j = jnp.where(j >= 64, j - LANES, j)
        gap = (i - j) * sign + 3
        for a in range(7):
            base = jnp.zeros((16, LANES), F32)
            for b in range(7):
                base = jnp.where(gap == b, taps_ref[c * 49 + a * 7 + b], base)
            for m in range(6):
                tile = (base if m == 0 else pltpu.roll(base, 16 * m, 1)).astype(BF16)
                for q in range(2):
                    u = a + q if sign > 0 else q + 6 - a
                    weights[slot, u * LANES + 16 * m : u * LANES + 16 * (m + 1), q * LANES : (q + 1) * LANES] = tile

    def every_other(ref, p, parity, c):
        return ref[p, pl.ds(parity * CH + c, 48, stride=2 * CH), :]

    def moved_rows(slot, kind, u):
        near = u // 2
        return jnp.concatenate(
            [lines[slot, kind, 2 * p + u % 2, near : near + ROWS // 2] for p in range(2)], axis=0
        ).astype(BF16)

    def conv_channel(c, slot):
        band(c, slot, 1)
        for p in range(2):
            for parity in range(2):
                lines[slot, 0, 2 * p + parity] = every_other(xf, p, parity, c)
        for u in range(8):
            data[slot, 0:ROWS, u * LANES : (u + 1) * LANES] = moved_rows(slot, 0, u)
        for q in range(2):
            near = (q + 3) // 2
            v = jnp.concatenate(
                [lines[slot, 0, 2 * p + (q + 3) % 2, near : near + ROWS // 2] for p in range(2)], axis=0
            )
            v = v.T[:SIDE].astype(BF16)
            xt[c, q * SIDE : (q + 1) * SIDE] = jnp.concatenate([v, v], axis=1)
        out = jnp.dot(data[slot, 0:ROWS, :], weights[slot], preferred_element_type=F32)
        for p in range(2):
            for q in range(2):
                conv[p, pl.ds(q * CH + c, ROWS // 2, stride=2 * CH), :] = out[
                    p * (ROWS // 2) : (p + 1) * (ROWS // 2), q * LANES : (q + 1) * LANES
                ]

    def conv_channels(i, carry):
        for slot in range(UNROLL):
            conv_channel(i * UNROLL + slot, slot)
        return carry

    lax.fori_loop(0, REAL // UNROLL, conv_channels, 0)

    def pointwise(index, carry):
        p = index // (ROWS // RB)
        r0 = (index % (ROWS // RB)) * RB
        lane = lanes(CH)
        real = lax.broadcasted_iota(jnp.int32, (CH, LANES), 0) < 77
        gain = gain_ref[...]
        bias = bias_ref[...]
        for half in range(RB // 4):
            rows = [conv[p, row(r0 + half * 4 + i), :] for i in range(4)]
            for k, v in enumerate(pack_rows(rows, lane)):
                at = pl.ds((half * 3 + k) * LANES, LANES)
                mean = jnp.sum(jnp.where(real, v, 0.0), axis=0, keepdims=True) * (1.0 / 77.0)
                cen = jnp.where(real, v - mean, 0.0)
                var = jnp.sum(cen * cen, axis=0, keepdims=True) * (1.0 / 77.0)
                rs = lax.rsqrt(var + 1e-06)
                xh = cen * rs
                xhat[:, at] = xh
                rstd[:, at] = jnp.broadcast_to(rs, (8, LANES))
                hi, lo = halves(xh * gain + bias)
                nk[0:CH, at] = hi
                nk[LANES : LANES + CH, at] = lo
            rows = [cbf[p, row(r0 + half * 4 + i), :] for i in range(4)]
            for k, v in enumerate(pack_rows(rows, lane)):
                at = pl.ds((half * 3 + k) * LANES, LANES)
                hi, lo = halves(v)
                cbk[0:CH, at] = hi
                cbk[LANES : LANES + CH, at] = lo
        def ahead(t):
            at = pl.ds(t * TILE, TILE)
            hid[t % 2] = jnp.dot(upk_ref[...], nk[:, at], preferred_element_type=F32)
            dact[t % 2] = jnp.dot(dnk_ref[...], cbk[:, at], preferred_element_type=F32)

        tiles = CELLS // TILE
        ahead(0)
        for t in range(tiles):
            if t + 1 < tiles:
                ahead(t + 1)
            at = pl.ds(t * TILE, TILE)
            for i in range(HP // 16):
                part = pl.ds(i * 16, 16)
                rest = pl.ds(HP + i * 16, 16)
                act, slope = gelu_parts(hid[t % 2, part, :])
                ahl[part, at], ahl[rest, at] = halves(act)
                dhl[part, at], dhl[rest, at] = halves(slope * dact[t % 2, part, :])
            dnorm[:, at] = jnp.dot(upt_ref[...], dhl[:, at], preferred_element_type=F32)
            if t % 3 == 2:
                three = pl.ds((t - 2) * TILE, 3 * TILE)
                gdn[...] += lax.dot_general(ahl[:, three], cbk[:, three], NT, preferred_element_type=F32)
                gup[...] += lax.dot_general(dhl[:, three], nk[:, three], NT, preferred_element_type=F32)
        for half in range(RB // 4):
            packed = []
            for k in range(3):
                first = (half * 3 + k) * LANES
                at = pl.ds(first, LANES)
                xh = xhat[:, at]
                dxh = dnorm[:, at] * gain
                m1 = jnp.sum(dxh, axis=0, keepdims=True) * (1.0 / 77.0)
                m2 = jnp.sum(dxh * xh, axis=0, keepdims=True) * (1.0 / 77.0)
                v = (dxh - m1 - xh * m2) * rstd[0:1, at]
                packed.append(jnp.where(real, v, 0.0))
            for i, v in enumerate(unpack_rows(packed, lane)):
                at = row(r0 + half * 4 + i + 3)
                dcv[p, at, :] = v
        return carry

    lax.fori_loop(0, 2 * (ROWS // RB), pointwise, 0)

    for place_at, ref in ((0, gup), (HP, gdn)):
        total = ref[0:HP, :] + ref[HP : 2 * HP, :]
        sum_ref[place_at : place_at + HP, :] = total[:, :LANES] + total[:, LANES:]
    start(spread(sum_ref, PIECE, first, 10))

    def back_channel(c, slot):
        band(c, slot, -1)
        for p in range(2):
            for parity in range(2):
                v = every_other(dcv, p, parity, c)
                hi = v.astype(BF16).astype(F32)
                lines[slot, 0, 2 * p + parity] = hi
                lines[slot, 1, 2 * p + parity] = v - hi
        for u in range(8):
            for k in range(2):
                data[slot, k * ROWS : (k + 1) * ROWS, u * LANES : (u + 1) * LANES] = moved_rows(slot, k, u)
        out = jnp.dot(data[slot], weights[slot], preferred_element_type=F32)
        out = out[:ROWS] + out[ROWS:]
        for p in range(2):
            for q in range(2):
                at = pl.ds(q * CH + c, ROWS // 2, stride=2 * CH)
                cbf[p, at, :] = cbf[p, at, :] + out[
                    p * (ROWS // 2) : (p + 1) * (ROWS // 2), q * LANES : (q + 1) * LANES
                ]
        total = None
        sub = lax.broadcasted_iota(jnp.int32, (8, LANES), 0)
        lane = lanes(8)
        line = jnp.zeros((8, LANES), F32)
        prods = jnp.dot(xt[c], data[slot], preferred_element_type=F32)
        for a in range(7):
            v = None
            for m in range(12):
                here = [
                    prods[q * SIDE + 8 * m : q * SIDE + 8 * (m + 1), u * LANES : (u + 1) * LANES]
                    for q, u in ((0, 6 - a), (1, 7 - a))
                ]
                t = here[0] + here[1]
                if m:
                    t = pltpu.roll(t, LANES - 8 * m, 1)
                v = t if v is None else v + t
            for bit in (1, 2, 4):
                v = jnp.where((sub // bit) % 2 == 1, pltpu.roll(v, LANES - bit, 1), v)
            v = pltpu.roll(v, 3 + 8 * a, 1)
            line = jnp.where(jnp.logical_and(lane >= 8 * a, lane < 8 * a + 7), v, line)
        ksum[pl.ds(c, 1), :] = jnp.sum(line, axis=0, keepdims=True)

    def back_channels(i, carry):
        for slot in range(UNROLL):
            back_channel(i * UNROLL + slot, slot)

        @pl.when(i == 3)
        def _():
            wait(spread(sum_ref, PIECE, first, 10))
            second[0] = piece_sum(sum_ref, PIECE, first)
            start(across(second, 26))

        @pl.when(i == 6)
        def _():
            wait(across(second, 26))
            chunk[...] = column_sum(second, PIECE)
            start(collect(chunk, total_ref, PIECE, 34))

        return carry

    lax.fori_loop(0, REAL // UNROLL, back_channels, 0)
    total_ref[pl.ds(pl.multiple_of(cell * PIECE, 8), PIECE), :] = chunk[...]
    start(spread(ksum, 8, kfirst, 50))

    def assemble(k, carry):
        lane = lanes(CH)
        edge = [jnp.zeros((CH, LANES), F32)] * 2
        for i in range(8):
            d0 = cbf[0, row(k * 8 + i), :]
            d1 = cbf[1, row(k * 8 + i), :]
            west_part = jnp.where(lane < 80, pltpu.roll(d0, 112, 1), 0.0)
            east_part = jnp.where(lane >= 48, pltpu.roll(d1, 48, 1), 0.0)
            conv[0, row(k * 8 + i), :] = west_part + east_part
            here = jnp.logical_and(lane >= 16 * i, lane < 16 * i + 16)
            for s, d in ((0, d0), (1, d1)):
                moved = pltpu.roll(d, (16 * i + LANES - 80 * s) % LANES, 1)
                edge[s] = jnp.where(here, moved, edge[s])
        for s in range(2):
            rims[s, k] = edge[s].astype(BF16)
        return carry

    lax.fori_loop(theirs, theirs + 2, assemble, 0)

    def narrow_rows(r, carry):
        rows[r] = conv[0, row(theirs * 8 + r), :].astype(BF16)
        return carry

    lax.fori_loop(0, MARGIN, narrow_rows, 0)
    folds = [remote(rows, above, sems, 5, (lon, other))]
    for side, peer in ((0, west), (1, east)):
        folds.append(
            remote(rims.at[side, pl.ds(theirs, 2)], corner.at[1 - side], sems, 6 + side, (peer, other))
        )
    start(folds)
    lax.fori_loop(mine, mine + 8, assemble, 0)
    sides = []
    for side, peer in ((0, west), (1, east)):
        sides.append(
            remote(rims.at[side, pl.ds(mine, 8)], near.at[1 - side], sems, 8 + side, (peer, lat))
        )
    start(sides)

    wait(spread(ksum, 8, kfirst, 50))
    ksecond[0] = piece_sum(ksum, 8, kfirst)
    start(across(ksecond, 66))
    wait(across(ksecond, 66))
    kchunk[...] = column_sum(ksecond, 8)
    taps_out_ref[pl.ds(pl.multiple_of(cell * 8, 8), 8), :] = kchunk[...]
    start(collect(kchunk, taps_out_ref, 8, 74))
    wait(sides)

    def finish(k, carry):
        lane = lanes(CH)
        from_west = near[0, k].astype(F32)
        from_east = near[1, k].astype(F32)
        for i in range(8):
            w = pltpu.roll(from_west, (LANES - 16 * i) % LANES, 1)
            e = pltpu.roll(from_east, 112 - 16 * i, 1)
            add = jnp.where(lane < 16, w, jnp.where(lane >= 112, e, 0.0))
            out_ref[k * 8 + i] = conv[0, row((mine + k) * 8 + i), :] + add
        return carry

    lax.fori_loop(0, 8, finish, 0)
    wait(folds)
    base = (1 - lat) * 6

    def finish_corner(k, carry):
        lane = lanes(CH)
        from_west = corner[0, k].astype(F32)
        from_east = corner[1, k].astype(F32)
        for i in range(8):
            w = pltpu.roll(from_west, (LANES - 16 * i) % LANES, 1)
            e = pltpu.roll(from_east, 112 - 16 * i, 1)
            add = jnp.where(lane < 16, w, jnp.where(lane >= 112, e, 0.0))
            out_ref[(base + k) * 8 + i] += add + above[k * 8 + i].astype(F32)
        return carry

    lax.fori_loop(0, 2, finish_corner, 0)
    wait(collect(chunk, total_ref, PIECE, 34))
    wait(collect(kchunk, taps_out_ref, 8, 74))


def patches(count, slots, own, weights):
    taps, *rest = weights
    smem = pl.BlockSpec(memory_space=pltpu.SMEM)
    vmem = pl.BlockSpec(memory_space=pltpu.VMEM)
    return pl.pallas_call(
        patch_kernel,
        name="patches",
        out_shape=(
            jax.ShapeDtypeStruct((ROWS - MARGIN, CH, LANES), F32),
            jax.ShapeDtypeStruct((2 * HP, LANES), F32),
            jax.ShapeDtypeStruct((TAPS, LANES), F32),
        ),
        in_specs=[smem] * 3 + [vmem] * 4,
        out_specs=(vmem,) * 3,
        scratch_shapes=[
            pltpu.VMEM((2, (ROWS + 16) * CH, LANES), F32),
            pltpu.VMEM((2, ROWS * CH, LANES), F32),
            pltpu.VMEM((2, ROWS * CH, LANES), F32),
            pltpu.VMEM((2, (ROWS + 16) * CH, LANES), F32),
            pltpu.VMEM((2 * LANES, CELLS), BF16),
            pltpu.VMEM((2 * LANES, CELLS), BF16),
            pltpu.VMEM((CH, CELLS), F32),
            pltpu.VMEM((8, CELLS), F32),
            pltpu.VMEM((CH, CELLS), F32),
            pltpu.VMEM((2, HP, TILE), F32),
            pltpu.VMEM((2, HP, TILE), F32),
            pltpu.VMEM((2 * HP, CELLS), BF16),
            pltpu.VMEM((2 * HP, CELLS), BF16),
            pltpu.VMEM((2 * HP, 2 * LANES), F32),
            pltpu.VMEM((2 * HP, 2 * LANES), F32),
            pltpu.VMEM((UNROLL, 8 * LANES, 2 * LANES), BF16),
            pltpu.VMEM((UNROLL, 2 * ROWS, 8 * LANES), BF16),
            pltpu.VMEM((UNROLL, 2, 4, 48, LANES), F32),
            pltpu.VMEM((REAL, 2 * SIDE, 2 * ROWS), BF16),
            pltpu.VMEM((CH, LANES), F32),
            pltpu.VMEM((CH, LANES), F32),
            pltpu.VMEM((HP, 2 * LANES), BF16),
            pltpu.VMEM((HP, 2 * LANES), BF16),
            pltpu.VMEM((CH, 2 * HP), BF16),
            pltpu.VMEM((HP, 3 * LANES), F32),
            pltpu.VMEM((2, 8, 2, CH, LANES), BF16),
            pltpu.VMEM((MARGIN, 2, CH, LANES), BF16),
            pltpu.VMEM((2, ROWS // 8, 2, CH, LANES), BF16),
            pltpu.VMEM((2, ROWS // 8, CH, LANES), BF16),
            pltpu.VMEM((MARGIN, CH, LANES), BF16),
            pltpu.VMEM((2, 8, CH, LANES), BF16),
            pltpu.VMEM((2, 2, CH, LANES), BF16),
            pltpu.VMEM((MARGIN, CH, LANES), BF16),
            pltpu.VMEM((2 * HP, LANES), F32),
            pltpu.VMEM((16, PIECE, LANES), F32),
            pltpu.VMEM((8, PIECE, LANES), F32),
            pltpu.VMEM((PIECE, LANES), F32),
            pltpu.VMEM((TAPS, LANES), F32),
            pltpu.VMEM((16, 8, LANES), F32),
            pltpu.VMEM((8, 8, LANES), F32),
            pltpu.VMEM((8, LANES), F32),
            pltpu.SemaphoreType.DMA((2, 90)),
        ],
        compiler_params=pltpu.CompilerParams(
            collective_id=0, has_side_effects=True, vmem_limit_bytes=63 * 1024 * 1024
        ),
    )(count, slots, taps, own, *rest)


def prepare_weights(kernel, norm_gain, norm_bias, up_weight, up_bias, down_weight):
    width = 3 * LANES
    vectors = jnp.stack(
        [jnp.pad(v, (0, width - v.shape[0])) for v in (norm_gain, norm_bias, up_bias)]
    ).astype(F32)
    return kernel.astype(F32).reshape(-1), vectors, up_weight, down_weight


def body(
    state_field, cotangent, land_mask, ocean_slots, ocean_count,
    kernel, norm_gain, norm_bias, up_weight, up_bias, down_weight,
):
    channels, height, breadth = state_field.shape
    hidden = up_weight.shape[0]
    masked = jnp.where(land_mask[None] > 0, cotangent, jnp.zeros_like(cotangent))
    own = jnp.stack([state_field, masked])
    own = jnp.pad(own, ((0, 0), (0, CH - channels), (0, 0), (0, 0)))
    own = jnp.transpose(own, (2, 0, 1, 3))
    weights = prepare_weights(kernel, norm_gain, norm_bias, up_weight, up_bias, down_weight)
    out, total, taps = patches(ocean_count.reshape(1), ocean_slots.reshape(2), own, weights)
    scale = 1.0 / math.sqrt(height * lax.axis_size("lat") * breadth * lax.axis_size("lon"))
    total = total * scale
    field_grad = jnp.transpose(out, (1, 0, 2))[:channels]
    taps = (taps * scale)[:channels, :56].reshape(channels, 7, 8)
    kernel_grad = taps[:, :, 6::-1].reshape(channels, 49)
    up_grad = total[:hidden, :channels]
    down_grad = total[HP : HP + hidden, :channels].T
    return (field_grad, kernel_grad, up_grad, down_grad)


def solution(mesh):
    in_specs = (
        P(None, "lat", "lon"), P(None, "lat", "lon"), P("lat", "lon"), P("lat", "lon", None),
        P("lat", "lon"), P(), P(), P(), P(), P(), P(),
    )
    out_specs = (P(None, "lat", "lon"), P(), P(), P())
    return jax.shard_map(body, mesh=mesh, in_specs=in_specs, out_specs=out_specs, check_vma=False)
```

```python
import functools
import math

import jax
import jax.numpy as jnp
import numpy as np
from jax import lax
from jax.experimental import pallas as pl
from jax.experimental.pallas import tpu as pltpu
from jax.sharding import PartitionSpec as P

STRIDE = 64
MARGIN = 16
SIDE = 96
ROWS = 80
REAL = 77
CH = 80
HP = 320
LANES = 128
RB = 16
CELLS = RB * SIDE
TILE = 256
UNROLL = 7
PIECE = 2 * HP // 16
CUT = 48
TAPS = 128
F32 = jnp.float32
BF16 = jnp.bfloat16

NT = (((1,), (1,)), ((), ()))

ERF_P = 0.3275911 / math.sqrt(2.0)
ERF_C = [0.5 * c for c in (0.254829592, -0.284496736, 1.421413741, -1.453152027, 1.061405429)]


def gelu_parts(h):
    a = jnp.abs(h)
    d = 1.0 + ERF_P * a
    t = pl.reciprocal(d, approx=True)
    t = t * (2.0 - d * t)
    e = jnp.exp2(h * h * (-0.5 / math.log(2.0)))
    q = ERF_C[4] * t + ERF_C[3]
    q = q * t + ERF_C[2]
    q = q * t + ERF_C[1]
    q = q * t + ERF_C[0]
    q = q * (t * e)
    cdf = jnp.where(h > 0, 1.0 - q, q)
    act = h * cdf
    slope = cdf + h * (e * (1.0 / math.sqrt(2.0 * math.pi)))
    return act, slope


def halves(v):
    hi = v.astype(BF16)
    lo = (v - hi.astype(F32)).astype(BF16)
    return hi, lo


def pack_rows(rows, lane):
    r1 = pltpu.roll(rows[1], 96, 1)
    r2 = pltpu.roll(rows[2], 64, 1)
    r3 = pltpu.roll(rows[3], 32, 1)
    return (
        jnp.where(lane < 96, rows[0], r1),
        jnp.where(lane < 64, r1, r2),
        jnp.where(lane < 32, r2, r3),
    )


def unpack_rows(packed, lane):
    live = lane < 96
    v0, v1, v2 = packed
    zero = jnp.zeros_like(v0)
    r1 = pltpu.roll(jnp.where(lane < 96, v1, v0), 32, 1)
    r2 = pltpu.roll(jnp.where(lane < 32, v2, v1), 64, 1)
    r3 = pltpu.roll(v2, 96, 1)
    return tuple(jnp.where(live, r, zero) for r in (v0, r1, r2, r3))


def place():
    lon = lax.axis_index("lon")
    lat = lax.axis_index("lat")
    count = lax.axis_size("lon")
    return lon, lat, lax.rem(lon + 1, count), lax.rem(lon + count - 1, count)


def meet(peers):
    barrier = pltpu.get_barrier_semaphore()
    for peer in peers:
        pl.semaphore_signal(barrier, inc=1, device_id=peer, device_id_type=pl.DeviceIdType.MESH)
    pl.semaphore_wait(barrier, len(peers))


def remote(source, target, sems, index, peer):
    return pltpu.make_async_remote_copy(
        src_ref=source,
        dst_ref=target,
        send_sem=sems.at[0, index],
        recv_sem=sems.at[1, index],
        device_id=peer,
        device_id_type=pl.DeviceIdType.MESH,
    )


def ramp(index):
    offset = index + 0.5
    return jnp.minimum(1.0, jnp.minimum(offset / (2.0 * MARGIN), (SIDE - offset) / (2.0 * MARGIN)))


def patch_kernel(
    count_ref, slots_ref, kernel_ref, x_ref, c_ref, gain_row, bias_row, up_bias_row, up_ref, down_ref,
    out_ref, total_ref, taps_out_ref,
    xf, conv, cbf, dcv, nk, cbk, xhat, rstd, dnorm, hid, dact, ahl, dhl, gup, gdn, weights, data,
    lines, xt, gain_ref, bias_ref, upk_ref, dnk_ref, upt_ref, wide, taps, taps_ref, taps_sem,
    edges, got, strips,
    rims_a, rows_a, near_a, corner_a, above_a, rims_b, rows_b, near_b, corner_b, above_b,
    sum_ref, first, second, chunk, ksum, kfirst, ksecond, kchunk, sems,
):
    lon, lat, east, west = place()
    other = 1 - lat
    half = lon // 32
    cell = lax.rem(lon, 32) // 2
    core = lax.rem(lon, 2)
    plane = [(half * 32 + lax.rem(cell + d, 16) * 2 + core, lat) for d in range(1, 16)]
    column = (half * 2 + core) * 2 + lat
    cross = []
    for d in range(1, 8):
        j = lax.rem(column + d, 8)
        cross.append(((j // 4) * 32 + cell * 2 + lax.rem(j // 2, 2), lax.rem(j, 2)))
    near_by = [(east, lat), (west, lat), (lon, other), (east, other), (west, other)]
    meet(near_by + plane + cross)
    mine = lat * 2
    theirs = (1 - lat) * 8

    give = (1 - lat) * 48
    halos = []
    for part, source in ((0, x_ref), (1, c_ref)):
        halo = [remote(source.at[pl.ds(give, 16)], got.at[part], sems, 5 * part, (lon, other))]
        halo[0].start()

        def pack(k, carry):
            lane = lax.broadcasted_iota(jnp.int32, (REAL, LANES), 1)
            acc = [jnp.zeros((REAL, LANES), F32)] * 2
            for i in range(8):
                v = source[k * 8 + i].astype(F32)
                here = jnp.logical_and(lane >= 16 * i, lane < 16 * i + 16)
                for side in range(2):
                    moved = pltpu.roll(v, (16 * i + 16 * side) % LANES, 1)
                    acc[side] = jnp.where(here, moved, acc[side])
            for side in range(2):
                edges[part, side, k] = acc[side].astype(BF16)
            return carry

        lax.fori_loop(0, 8, pack, 0)
        for side, peer in ((0, west), (1, east)):
            halo.append(
                remote(
                    edges.at[part, side], strips.at[part, 1 - side, pl.ds(mine, 8)], sems,
                    5 * part + 1 + side, (peer, lat),
                )
            )
            halo.append(
                remote(
                    edges.at[part, side, pl.ds((1 - lat) * 6, 2)],
                    strips.at[part, 1 - side, pl.ds(lat * 8, 2)],
                    sems, 5 * part + 3 + side, (peer, other),
                )
            )
        for copy in halo[1:]:
            copy.start()
        halos.append(halo)

    taps[...] = jnp.zeros(taps.shape, F32)
    taps[0:49, 0:REAL] = kernel_ref[...].astype(F32)
    taps_copy = pltpu.make_async_copy(taps, taps_ref, taps_sem)
    taps_copy.start()

    def spread(source, size, slots, base):
        return [
            remote(
                source.at[pl.ds(pl.multiple_of(lax.rem(cell + d, 16) * size, 8), size)],
                slots.at[d], sems, base + d, plane[d - 1],
            )
            for d in range(1, 16)
        ]

    def across(slots, base):
        return [remote(slots.at[0], slots.at[d], sems, base + d, cross[d - 1]) for d in range(1, 8)]

    def collect(source, target, size, base):
        here = pl.ds(pl.multiple_of(cell * size, 8), size)
        return [
            remote(source, target.at[here], sems, base + d, plane[d - 1]) for d in range(1, 16)
        ]

    def start(copies):
        for copy in copies:
            copy.start()

    def wait(copies):
        for copy in copies:
            copy.wait()

    def piece_sum(source, size, slots):
        part = source[pl.ds(pl.multiple_of(cell * size, 8), size), :]
        for d in range(1, 16):
            part = part + slots[d]
        return part

    def column_sum(slots, size):
        whole = jnp.zeros((size, LANES), F32)
        for j in range(8):
            whole = whole + slots[lax.rem(column - j + 8, 8)]
        return whole

    ksum[...] = jnp.zeros(ksum.shape, F32)
    gup[...] = jnp.zeros(gup.shape, F32)
    gdn[...] = jnp.zeros(gdn.shape, F32)
    for ref in (xf, dcv):
        for p in range(2):
            ref[p, 0 : 3 * CH] = jnp.zeros((3 * CH, LANES), F32)
            ref[p, (ROWS + 3) * CH :] = jnp.zeros((13 * CH, LANES), F32)
    weights[...] = jnp.zeros(weights.shape, BF16)
    nk[CH:LANES, :] = jnp.zeros((LANES - CH, CELLS), BF16)
    cbk[CH:LANES, :] = jnp.zeros((LANES - CH, CELLS), BF16)
    cbk[LANES + CH :, :] = jnp.zeros((LANES - CH, CELLS), BF16)
    ones = lax.broadcasted_iota(jnp.int32, (LANES - CH, CELLS), 0) == 0
    nk[LANES + CH :, :] = jnp.where(ones, 1.0, 0.0).astype(BF16)

    def lanes(n):
        return lax.broadcasted_iota(jnp.int32, (n, LANES), 1)

    hidden = up_bias_row.shape[1]
    wide[...] = jnp.zeros(wide.shape, F32)
    for source, ref in ((gain_row, gain_ref), (bias_row, bias_ref)):
        wide[0:1, 0:REAL] = source[...].astype(F32)
        ref[...] = jnp.broadcast_to(wide[0:1, 0:LANES], (LANES, LANES)).T[:CH]
    wide[0:1, 0:hidden] = up_bias_row[...].astype(F32)
    up_bias = jnp.broadcast_to(wide[0:1, :], (LANES, 3 * LANES)).T[:HP]
    wide[0:REAL, 0:hidden] = up_ref[...].astype(F32)
    upt = wide[0:CH, 0:HP]
    upt_ref[...] = jnp.concatenate([upt, upt], axis=1).astype(BF16)
    up = wide[0:LANES, :].T[:HP]
    upk_ref[:, 0:LANES] = up.astype(BF16)
    upk_ref[:, LANES:] = jnp.where(lanes(HP) == CH, up_bias, up).astype(BF16)
    wide[0:REAL, 0:hidden] = down_ref[...].astype(F32)
    down = wide[0:LANES, :].T[:HP].astype(BF16)
    dnk_ref[:, 0:LANES] = down
    dnk_ref[:, LANES:] = down

    def clear(r, carry):
        for s in range(2):
            cbf[s, pl.ds(pl.multiple_of(r * CH + CH - 8, 8), 8), :] = jnp.zeros((8, LANES), F32)
        return carry

    lax.fori_loop(0, ROWS, clear, 0)
    taps_copy.wait()

    def row(r):
        return pl.ds(pl.multiple_of(r * CH, 8), CH)

    def active(s):
        here = jnp.logical_and(count_ref[0] > 0, slots_ref[0] == s)
        return jnp.logical_or(here, jnp.logical_and(count_ref[0] > 1, slots_ref[1] == s))

    on = [jnp.where(active(s), 1.0, 0.0) for s in range(2)]

    def widen(part, source, q0, count):
        def group(k, carry):
            lane = lanes(REAL)
            q = q0 + k
            if part:
                col_ramp = ramp(lanes(8).astype(F32)[0:1])
                row_ramps = [
                    ramp(jnp.full((1, LANES), q * 8 + i + 16 - 16 * lat, jnp.int32).astype(F32))
                    for i in range(8)
                ]
            for s in range(2):
                low, turn, rim = ((16, 16, 0), (0, 80, 80))[s]
                in_own = jnp.logical_and(lane >= low, lane < low + 80)
                in_rim = jnp.logical_and(lane >= rim, lane < rim + 16)
                edge = strips[part, s, q].astype(F32)
                for i in range(8):
                    v = pltpu.roll(source(k * 8 + i).astype(F32), turn, 1)
                    e = pltpu.roll(edge, (rim + LANES - 16 * i) % LANES, 1)
                    v = jnp.where(in_own, v, jnp.where(in_rim, e, 0.0))
                    if part:
                        at = pl.ds(pl.multiple_of((q * 8 + i) * CH, 8), REAL)
                        cbf[s, at, :] = v * (row_ramps[i] * col_ramp * on[s])
                    else:
                        at = pl.ds(pl.multiple_of((q * 8 + i + 3) * CH, 8), REAL)
                        xf[s, at, :] = v
            return carry

        lax.fori_loop(0, count, group, 0)

    wait(halos[0])
    widen(0, lambda r: x_ref[r], mine, 8)
    widen(0, lambda r: got[0, r], theirs, 2)

    def band(c, slot, sign):
        i = lax.broadcasted_iota(jnp.int32, (16, LANES), 0)
        j = lanes(16)
        j = jnp.where(j >= 64, j - LANES, j)
        gap = (i - j) * sign + 3
        for a in range(7):
            base = jnp.zeros((16, LANES), F32)
            for b in range(7):
                base = jnp.where(gap == b, taps_ref[a * 7 + b, c], base)
            for m in range(6):
                tile = (base if m == 0 else pltpu.roll(base, 16 * m, 1)).astype(BF16)
                for q in range(2):
                    u = a + q if sign > 0 else q + 6 - a
                    weights[slot, u * LANES + 16 * m : u * LANES + 16 * (m + 1), q * LANES : (q + 1) * LANES] = tile

    def every_other(ref, p, parity, c):
        return ref[p, pl.ds(parity * CH + c, 48, stride=2 * CH), :]

    def moved_rows(slot, kind, u):
        near = u // 2
        return jnp.concatenate(
            [lines[slot, kind, 2 * p + u % 2, near : near + ROWS // 2] for p in range(2)], axis=0
        ).astype(BF16)

    def conv_channel(c, slot):
        band(c, slot, 1)
        for p in range(2):
            for parity in range(2):
                lines[slot, 0, 2 * p + parity] = every_other(xf, p, parity, c)
        for u in range(8):
            data[slot, 0:ROWS, u * LANES : (u + 1) * LANES] = moved_rows(slot, 0, u)
        for q in range(2):
            near = (q + 3) // 2
            v = jnp.concatenate(
                [lines[slot, 0, 2 * p + (q + 3) % 2, near : near + ROWS // 2] for p in range(2)], axis=0
            )
            v = v.T[:SIDE].astype(BF16)
            xt[c, q * SIDE : (q + 1) * SIDE] = jnp.concatenate([v, v], axis=1)
        out = jnp.dot(data[slot, 0:ROWS, :], weights[slot], preferred_element_type=F32)
        for p in range(2):
            for q in range(2):
                conv[p, pl.ds(q * CH + c, ROWS // 2, stride=2 * CH), :] = out[
                    p * (ROWS // 2) : (p + 1) * (ROWS // 2), q * LANES : (q + 1) * LANES
                ]

    def conv_channels(i, carry):
        for slot in range(UNROLL):
            conv_channel(i * UNROLL + slot, slot)
        return carry

    lax.fori_loop(0, REAL // UNROLL, conv_channels, 0)

    wait(halos[1])
    widen(1, lambda r: c_ref[r], mine, 8)
    widen(1, lambda r: got[1, r], theirs, 2)

    def pointwise(index, carry):
        p = index // (ROWS // RB)
        r0 = (index % (ROWS // RB)) * RB
        lane = lanes(CH)
        real = lax.broadcasted_iota(jnp.int32, (CH, LANES), 0) < 77
        gain = gain_ref[...]
        bias = bias_ref[...]
        for half in range(RB // 4):
            rows = [conv[p, row(r0 + half * 4 + i), :] for i in range(4)]
            for k, v in enumerate(pack_rows(rows, lane)):
                at = pl.ds((half * 3 + k) * LANES, LANES)
                mean = jnp.sum(jnp.where(real, v, 0.0), axis=0, keepdims=True) * (1.0 / 77.0)
                cen = jnp.where(real, v - mean, 0.0)
                var = jnp.sum(cen * cen, axis=0, keepdims=True) * (1.0 / 77.0)
                rs = lax.rsqrt(var + 1e-06)
                xh = cen * rs
                xhat[:, at] = xh
                rstd[:, at] = jnp.broadcast_to(rs, (8, LANES))
                hi, lo = halves(xh * gain + bias)
                nk[0:CH, at] = hi
                nk[LANES : LANES + CH, at] = lo
            rows = [cbf[p, row(r0 + half * 4 + i), :] for i in range(4)]
            for k, v in enumerate(pack_rows(rows, lane)):
                at = pl.ds((half * 3 + k) * LANES, LANES)
                hi, lo = halves(v)
                cbk[0:CH, at] = hi
                cbk[LANES : LANES + CH, at] = lo
        def ahead(t):
            at = pl.ds(t * TILE, TILE)
            hid[t % 2] = jnp.dot(upk_ref[...], nk[:, at], preferred_element_type=F32)
            dact[t % 2] = jnp.dot(dnk_ref[...], cbk[:, at], preferred_element_type=F32)

        tiles = CELLS // TILE
        ahead(0)
        for t in range(tiles):
            if t + 1 < tiles:
                ahead(t + 1)
            at = pl.ds(t * TILE, TILE)
            for i in range(HP // 16):
                part = pl.ds(i * 16, 16)
                rest = pl.ds(HP + i * 16, 16)
                act, slope = gelu_parts(hid[t % 2, part, :])
                ahl[part, at], ahl[rest, at] = halves(act)
                dhl[part, at], dhl[rest, at] = halves(slope * dact[t % 2, part, :])
            dnorm[:, at] = jnp.dot(upt_ref[...], dhl[:, at], preferred_element_type=F32)
            if t % 3 == 2:
                three = pl.ds((t - 2) * TILE, 3 * TILE)
                gdn[...] += lax.dot_general(ahl[:, three], cbk[:, three], NT, preferred_element_type=F32)
                gup[...] += lax.dot_general(dhl[:, three], nk[:, three], NT, preferred_element_type=F32)
        for half in range(RB // 4):
            packed = []
            for k in range(3):
                first = (half * 3 + k) * LANES
                at = pl.ds(first, LANES)
                xh = xhat[:, at]
                dxh = dnorm[:, at] * gain
                m1 = jnp.sum(dxh, axis=0, keepdims=True) * (1.0 / 77.0)
                m2 = jnp.sum(dxh * xh, axis=0, keepdims=True) * (1.0 / 77.0)
                v = (dxh - m1 - xh * m2) * rstd[0:1, at]
                packed.append(jnp.where(real, v, 0.0))
            for i, v in enumerate(unpack_rows(packed, lane)):
                at = row(r0 + half * 4 + i + 3)
                dcv[p, at, :] = v
        return carry

    lax.fori_loop(0, 2 * (ROWS // RB), pointwise, 0)

    for place_at, ref in ((0, gup), (HP, gdn)):
        total = ref[0:HP, :] + ref[HP : 2 * HP, :]
        sum_ref[place_at : place_at + HP, :] = total[:, :LANES] + total[:, LANES:]
    start(spread(sum_ref, PIECE, first, 20))

    def back_channel(c, slot):
        band(c, slot, -1)
        for p in range(2):
            for parity in range(2):
                v = every_other(dcv, p, parity, c)
                hi = v.astype(BF16).astype(F32)
                lines[slot, 0, 2 * p + parity] = hi
                lines[slot, 1, 2 * p + parity] = v - hi
        for u in range(8):
            for k in range(2):
                data[slot, k * ROWS : (k + 1) * ROWS, u * LANES : (u + 1) * LANES] = moved_rows(slot, k, u)
        out = jnp.dot(data[slot], weights[slot], preferred_element_type=F32)
        out = out[:ROWS] + out[ROWS:]
        for p in range(2):
            for q in range(2):
                at = pl.ds(q * CH + c, ROWS // 2, stride=2 * CH)
                cbf[p, at, :] = cbf[p, at, :] + out[
                    p * (ROWS // 2) : (p + 1) * (ROWS // 2), q * LANES : (q + 1) * LANES
                ]
        total = None
        sub = lax.broadcasted_iota(jnp.int32, (8, LANES), 0)
        lane = lanes(8)
        line = jnp.zeros((8, LANES), F32)
        prods = jnp.dot(xt[c], data[slot], preferred_element_type=F32)
        for a in range(7):
            v = None
            for m in range(12):
                here = [
                    prods[q * SIDE + 8 * m : q * SIDE + 8 * (m + 1), u * LANES : (u + 1) * LANES]
                    for q, u in ((0, 6 - a), (1, 7 - a))
                ]
                t = here[0] + here[1]
                if m:
                    t = pltpu.roll(t, LANES - 8 * m, 1)
                v = t if v is None else v + t
            for bit in (1, 2, 4):
                v = jnp.where((sub // bit) % 2 == 1, pltpu.roll(v, LANES - bit, 1), v)
            v = pltpu.roll(v, 3 + 8 * a, 1)
            line = jnp.where(jnp.logical_and(lane >= 8 * a, lane < 8 * a + 7), v, line)
        ksum[pl.ds(c, 1), :] = jnp.sum(line, axis=0, keepdims=True)

    def fold_copies(bufs, base):
        rims, rows, near, corner, above = bufs
        margin = [remote(rows, above, sems, base, (lon, other))]
        sides = []
        for side, peer in ((0, west), (1, east)):
            margin.append(
                remote(
                    rims.at[side, pl.ds(theirs, 2)], corner.at[1 - side], sems, base + 1 + side,
                    (peer, other),
                )
            )
            sides.append(
                remote(rims.at[side, pl.ds(mine, 8)], near.at[1 - side], sems, base + 3 + side, (peer, lat))
            )
        return margin, sides

    def leave(c0, count, bufs, base):
        rims, rows, near, corner, above = bufs
        margin, sides = fold_copies(bufs, base)

        def some(r):
            return pl.ds(pl.multiple_of(r * CH + c0, 8), count)

        def assemble(k, carry):
            lane = lanes(count)
            edge = [jnp.zeros((count, LANES), F32)] * 2
            for i in range(8):
                d0 = cbf[0, some(k * 8 + i), :]
                d1 = cbf[1, some(k * 8 + i), :]
                west_part = jnp.where(lane < 80, pltpu.roll(d0, 112, 1), 0.0)
                east_part = jnp.where(lane >= 48, pltpu.roll(d1, 48, 1), 0.0)
                conv[0, some(k * 8 + i), :] = west_part + east_part
                here = jnp.logical_and(lane >= 16 * i, lane < 16 * i + 16)
                for s, d in ((0, d0), (1, d1)):
                    moved = pltpu.roll(d, (16 * i + LANES - 80 * s) % LANES, 1)
                    edge[s] = jnp.where(here, moved, edge[s])
            for s in range(2):
                rims[s, k] = edge[s].astype(BF16)
            return carry

        lax.fori_loop(theirs, theirs + 2, assemble, 0)

        def narrow_rows(r, carry):
            rows[r] = conv[0, some(theirs * 8 + r), :].astype(BF16)
            return carry

        lax.fori_loop(0, MARGIN, narrow_rows, 0)
        start(margin)
        lax.fori_loop(mine, mine + 8, assemble, 0)
        start(sides)

    def arrive(c0, count, bufs, base):
        rims, rows, near, corner, above = bufs
        margin, sides = fold_copies(bufs, base)

        def added(source, k, i, lane):
            w = pltpu.roll(source[0, k].astype(F32), (LANES - 16 * i) % LANES, 1)
            e = pltpu.roll(source[1, k].astype(F32), 112 - 16 * i, 1)
            return jnp.where(lane < 16, w, jnp.where(lane >= 112, e, 0.0))

        def finish(k, carry):
            lane = lanes(count)
            for i in range(8):
                at = pl.ds(pl.multiple_of(((mine + k) * 8 + i) * CH + c0, 8), count)
                out_ref[k * 8 + i, c0 : c0 + count] = conv[0, at, :] + added(near, k, i, lane)
            return carry

        def finish_corner(k, carry):
            lane = lanes(count)
            for i in range(8):
                add = added(corner, k, i, lane) + above[k * 8 + i].astype(F32)
                out_ref[((1 - lat) * 6 + k) * 8 + i, c0 : c0 + count] += add
            return carry

        wait(sides)
        lax.fori_loop(0, 8, finish, 0)
        wait(margin)
        lax.fori_loop(0, 2, finish_corner, 0)

    bufs_a = (rims_a, rows_a, near_a, corner_a, above_a)
    bufs_b = (rims_b, rows_b, near_b, corner_b, above_b)

    def back_channels(i, carry):
        for slot in range(UNROLL):
            back_channel(i * UNROLL + slot, slot)

        @pl.when(i == 14 // UNROLL)
        def _():
            wait(spread(sum_ref, PIECE, first, 20))
            second[0] = piece_sum(sum_ref, PIECE, first)
            start(across(second, 36))

        @pl.when(i == 33 // UNROLL)
        def _():
            wait(across(second, 36))
            chunk[...] = column_sum(second, PIECE)
            start(collect(chunk, total_ref, PIECE, 44))

        @pl.when(i == (CUT - 1) // UNROLL)
        def _():
            leave(0, CUT, bufs_a, 10)

        return carry

    lax.fori_loop(0, REAL // UNROLL, back_channels, 0)
    start(spread(ksum, 8, kfirst, 60))
    leave(CUT, CH - CUT, bufs_b, 15)
    total_ref[pl.ds(pl.multiple_of(cell * PIECE, 8), PIECE), :] = chunk[...]
    wait(spread(ksum, 8, kfirst, 60))
    ksecond[0] = piece_sum(ksum, 8, kfirst)
    start(across(ksecond, 76))
    arrive(0, CUT, bufs_a, 10)
    wait(across(ksecond, 76))
    kchunk[...] = column_sum(ksecond, 8)
    taps_out_ref[pl.ds(pl.multiple_of(cell * 8, 8), 8), :] = kchunk[...]
    start(collect(kchunk, taps_out_ref, 8, 84))
    arrive(CUT, CH - CUT, bufs_b, 15)
    wait(collect(chunk, total_ref, PIECE, 44))
    wait(collect(kchunk, taps_out_ref, 8, 84))


def patches(count, slots, *arrays):
    smem = pl.BlockSpec(memory_space=pltpu.SMEM)
    vmem = pl.BlockSpec(memory_space=pltpu.VMEM)
    return pl.pallas_call(
        patch_kernel,
        name="patches",
        out_shape=(
            jax.ShapeDtypeStruct((ROWS - MARGIN, CH, LANES), F32),
            jax.ShapeDtypeStruct((2 * HP, LANES), F32),
            jax.ShapeDtypeStruct((TAPS, LANES), F32),
        ),
        in_specs=[smem] * 2 + [vmem] * 8,
        out_specs=(vmem,) * 3,
        scratch_shapes=[
            pltpu.VMEM((2, (ROWS + 16) * CH, LANES), F32),
            pltpu.VMEM((2, ROWS * CH, LANES), F32),
            pltpu.VMEM((2, ROWS * CH, LANES), F32),
            pltpu.VMEM((2, (ROWS + 16) * CH, LANES), F32),
            pltpu.VMEM((2 * LANES, CELLS), BF16),
            pltpu.VMEM((2 * LANES, CELLS), BF16),
            pltpu.VMEM((CH, CELLS), F32),
            pltpu.VMEM((8, CELLS), F32),
            pltpu.VMEM((CH, CELLS), F32),
            pltpu.VMEM((2, HP, TILE), F32),
            pltpu.VMEM((2, HP, TILE), F32),
            pltpu.VMEM((2 * HP, CELLS), BF16),
            pltpu.VMEM((2 * HP, CELLS), BF16),
            pltpu.VMEM((2 * HP, 2 * LANES), F32),
            pltpu.VMEM((2 * HP, 2 * LANES), F32),
            pltpu.VMEM((UNROLL, 8 * LANES, 2 * LANES), BF16),
            pltpu.VMEM((UNROLL, 2 * ROWS, 8 * LANES), BF16),
            pltpu.VMEM((UNROLL, 2, 4, 48, LANES), F32),
            pltpu.VMEM((REAL, 2 * SIDE, 2 * ROWS), BF16),
            pltpu.VMEM((CH, LANES), F32),
            pltpu.VMEM((CH, LANES), F32),
            pltpu.VMEM((HP, 2 * LANES), BF16),
            pltpu.VMEM((HP, 2 * LANES), BF16),
            pltpu.VMEM((CH, 2 * HP), BF16),
            pltpu.VMEM((HP, 3 * LANES), F32),
            pltpu.VMEM((56, LANES), F32),
            pltpu.SMEM((56, LANES), F32),
            pltpu.SemaphoreType.DMA,
            pltpu.VMEM((2, 2, 8, REAL, LANES), BF16),
            pltpu.VMEM((2, MARGIN, REAL, LANES), BF16),
            pltpu.VMEM((2, 2, ROWS // 8, REAL, LANES), BF16),
            *(
                pltpu.VMEM((*lead, count, LANES), BF16)
                for count in (CUT, CH - CUT)
                for lead in ((2, ROWS // 8), (MARGIN,), (2, 8), (2, 2), (MARGIN,))
            ),
            pltpu.VMEM((2 * HP, LANES), F32),
            pltpu.VMEM((16, PIECE, LANES), F32),
            pltpu.VMEM((8, PIECE, LANES), F32),
            pltpu.VMEM((PIECE, LANES), F32),
            pltpu.VMEM((TAPS, LANES), F32),
            pltpu.VMEM((16, 8, LANES), F32),
            pltpu.VMEM((8, 8, LANES), F32),
            pltpu.VMEM((8, LANES), F32),
            pltpu.SemaphoreType.DMA((2, 100)),
        ],
        compiler_params=pltpu.CompilerParams(
            collective_id=0, has_side_effects=True, vmem_limit_bytes=63 * 1024 * 1024
        ),
    )(count, slots, *arrays)


def body(
    state_field, cotangent, land_mask, ocean_slots, ocean_count,
    kernel, norm_gain, norm_bias, up_weight, up_bias, down_weight,
):
    channels, height, breadth = state_field.shape
    hidden = up_weight.shape[0]
    masked = jnp.where(land_mask[None] > 0, cotangent, jnp.zeros_like(cotangent))
    out, total, taps = patches(
        ocean_count.reshape(1), ocean_slots.reshape(2), kernel.T,
        jnp.transpose(state_field, (1, 0, 2)), jnp.transpose(masked, (1, 0, 2)),
        norm_gain[None], norm_bias[None], up_bias[None], up_weight.T, down_weight,
    )
    scale = 1.0 / math.sqrt(height * lax.axis_size("lat") * breadth * lax.axis_size("lon"))
    total = total * scale
    field_grad = jnp.transpose(out, (1, 0, 2))[:channels]
    taps = (taps * scale)[:channels, :56].reshape(channels, 7, 8)
    kernel_grad = taps[:, :, 6::-1].reshape(channels, 49)
    up_grad = total[:hidden, :channels]
    down_grad = total[HP : HP + hidden, :channels].T
    return (field_grad, kernel_grad, up_grad, down_grad)


def solution(mesh):
    in_specs = (
        P(None, "lat", "lon"), P(None, "lat", "lon"), P("lat", "lon"), P("lat", "lon", None),
        P("lat", "lon"), P(), P(), P(), P(), P(), P(),
    )
    out_specs = (P(None, "lat", "lon"), P(), P(), P())
    return jax.shard_map(body, mesh=mesh, in_specs=in_specs, out_specs=out_specs, check_vma=False)
```

```python
import functools
import math

import jax
import jax.numpy as jnp
import numpy as np
from jax import lax
from jax.experimental import pallas as pl
from jax.experimental.pallas import tpu as pltpu
from jax.sharding import PartitionSpec as P

STRIDE = 64
MARGIN = 16
SIDE = 96
ROWS = 80
REAL = 77
CH = 80
HP = 320
LANES = 128
RB = 16
CELLS = RB * SIDE
TILE = 256
UNROLL = 7
PIECE = 2 * HP // 16
CUT = 48
TAPS = 128
F32 = jnp.float32
BF16 = jnp.bfloat16

NT = (((1,), (1,)), ((), ()))


def gelu_parts(h):
    cdf = 0.5 * lax.erf(h * math.sqrt(0.5)) + 0.5
    e = jnp.exp2(h * h * (-0.5 / math.log(2.0)))
    return h * cdf, cdf + h * (e * (1.0 / math.sqrt(2.0 * math.pi)))


def halves(v):
    hi = v.astype(BF16)
    lo = (v - hi.astype(F32)).astype(BF16)
    return hi, lo


def pack_rows(rows, lane):
    r1 = pltpu.roll(rows[1], 96, 1)
    r2 = pltpu.roll(rows[2], 64, 1)
    r3 = pltpu.roll(rows[3], 32, 1)
    return (
        jnp.where(lane < 96, rows[0], r1),
        jnp.where(lane < 64, r1, r2),
        jnp.where(lane < 32, r2, r3),
    )


def unpack_rows(packed, lane):
    live = lane < 96
    v0, v1, v2 = packed
    zero = jnp.zeros_like(v0)
    r1 = pltpu.roll(jnp.where(lane < 96, v1, v0), 32, 1)
    r2 = pltpu.roll(jnp.where(lane < 32, v2, v1), 64, 1)
    r3 = pltpu.roll(v2, 96, 1)
    return tuple(jnp.where(live, r, zero) for r in (v0, r1, r2, r3))


def place():
    lon = lax.axis_index("lon")
    lat = lax.axis_index("lat")
    count = lax.axis_size("lon")
    return lon, lat, lax.rem(lon + 1, count), lax.rem(lon + count - 1, count)


def meet(peers):
    barrier = pltpu.get_barrier_semaphore()
    for peer in peers:
        pl.semaphore_signal(barrier, inc=1, device_id=peer, device_id_type=pl.DeviceIdType.MESH)
    pl.semaphore_wait(barrier, len(peers))


def remote(source, target, sems, index, peer):
    return pltpu.make_async_remote_copy(
        src_ref=source,
        dst_ref=target,
        send_sem=sems.at[0, index],
        recv_sem=sems.at[1, index],
        device_id=peer,
        device_id_type=pl.DeviceIdType.MESH,
    )


def ramp(index):
    offset = index + 0.5
    return jnp.minimum(1.0, jnp.minimum(offset / (2.0 * MARGIN), (SIDE - offset) / (2.0 * MARGIN)))


def patch_kernel(
    count_ref, slots_ref, kernel_ref, x_ref, c_ref, gain_row, bias_row, up_bias_row, up_ref, down_ref,
    out_ref, total_ref, taps_out_ref,
    xf, conv, cbf, dcv, nk, cbk, xhat, rstd, dnorm, hid, dact, ahl, dhl, gup, gdn, weights, data,
    lines, xt, gain_ref, bias_ref, upk_ref, dnk_ref, upt_ref, wide, taps, taps_ref, taps_sem,
    edges, got, strips,
    rims_a, rows_a, near_a, corner_a, above_a, rims_b, rows_b, near_b, corner_b, above_b,
    sum_ref, first, second, chunk, ksum, kfirst, ksecond, kchunk, sems,
):
    lon, lat, east, west = place()
    other = 1 - lat
    half = lon // 32
    cell = lax.rem(lon, 32) // 2
    core = lax.rem(lon, 2)
    plane = [(half * 32 + lax.rem(cell + d, 16) * 2 + core, lat) for d in range(1, 16)]
    column = (half * 2 + core) * 2 + lat
    cross = []
    for d in range(1, 8):
        j = lax.rem(column + d, 8)
        cross.append(((j // 4) * 32 + cell * 2 + lax.rem(j // 2, 2), lax.rem(j, 2)))
    near_by = [(east, lat), (west, lat), (lon, other), (east, other), (west, other)]
    meet(near_by + plane + cross)
    mine = lat * 2
    theirs = (1 - lat) * 8

    give = (1 - lat) * 48
    halos = []
    for part, source in ((0, x_ref), (1, c_ref)):
        halo = [remote(source.at[pl.ds(give, 16)], got.at[part], sems, 5 * part, (lon, other))]
        halo[0].start()

        def pack(k, carry):
            lane = lax.broadcasted_iota(jnp.int32, (REAL, LANES), 1)
            acc = [jnp.zeros((REAL, LANES), F32)] * 2
            for i in range(8):
                v = source[k * 8 + i].astype(F32)
                here = jnp.logical_and(lane >= 16 * i, lane < 16 * i + 16)
                for side in range(2):
                    moved = pltpu.roll(v, (16 * i + 16 * side) % LANES, 1)
                    acc[side] = jnp.where(here, moved, acc[side])
            for side in range(2):
                edges[part, side, k] = acc[side].astype(BF16)
            return carry

        lax.fori_loop(0, 8, pack, 0)
        for side, peer in ((0, west), (1, east)):
            halo.append(
                remote(
                    edges.at[part, side], strips.at[part, 1 - side, pl.ds(mine, 8)], sems,
                    5 * part + 1 + side, (peer, lat),
                )
            )
            halo.append(
                remote(
                    edges.at[part, side, pl.ds((1 - lat) * 6, 2)],
                    strips.at[part, 1 - side, pl.ds(lat * 8, 2)],
                    sems, 5 * part + 3 + side, (peer, other),
                )
            )
        for copy in halo[1:]:
            copy.start()
        halos.append(halo)

    taps[...] = jnp.zeros(taps.shape, F32)
    taps[0:49, 0:REAL] = kernel_ref[...].astype(F32)
    taps_copy = pltpu.make_async_copy(taps, taps_ref, taps_sem)
    taps_copy.start()

    def spread(source, size, slots, base):
        return [
            remote(
                source.at[pl.ds(pl.multiple_of(lax.rem(cell + d, 16) * size, 8), size)],
                slots.at[d], sems, base + d, plane[d - 1],
            )
            for d in range(1, 16)
        ]

    def across(slots, base):
        return [remote(slots.at[0], slots.at[d], sems, base + d, cross[d - 1]) for d in range(1, 8)]

    def collect(source, target, size, base):
        here = pl.ds(pl.multiple_of(cell * size, 8), size)
        return [
            remote(source, target.at[here], sems, base + d, plane[d - 1]) for d in range(1, 16)
        ]

    def start(copies):
        for copy in copies:
            copy.start()

    def wait(copies):
        for copy in copies:
            copy.wait()

    def piece_sum(source, size, slots):
        part = source[pl.ds(pl.multiple_of(cell * size, 8), size), :]
        for d in range(1, 16):
            part = part + slots[d]
        return part

    def column_sum(slots, size):
        whole = jnp.zeros((size, LANES), F32)
        for j in range(8):
            whole = whole + slots[lax.rem(column - j + 8, 8)]
        return whole

    ksum[...] = jnp.zeros(ksum.shape, F32)
    gup[...] = jnp.zeros(gup.shape, F32)
    gdn[...] = jnp.zeros(gdn.shape, F32)
    for ref in (xf, dcv):
        for p in range(2):
            ref[p, 0 : 3 * CH] = jnp.zeros((3 * CH, LANES), F32)
            ref[p, (ROWS + 3) * CH :] = jnp.zeros((13 * CH, LANES), F32)
    weights[...] = jnp.zeros(weights.shape, BF16)
    nk[CH:LANES, :] = jnp.zeros((LANES - CH, CELLS), BF16)
    cbk[CH:LANES, :] = jnp.zeros((LANES - CH, CELLS), BF16)
    cbk[LANES + CH :, :] = jnp.zeros((LANES - CH, CELLS), BF16)
    ones = lax.broadcasted_iota(jnp.int32, (LANES - CH, CELLS), 0) == 0
    nk[LANES + CH :, :] = jnp.where(ones, 1.0, 0.0).astype(BF16)

    def lanes(n):
        return lax.broadcasted_iota(jnp.int32, (n, LANES), 1)

    hidden = up_bias_row.shape[1]
    wide[...] = jnp.zeros(wide.shape, F32)
    for source, ref in ((gain_row, gain_ref), (bias_row, bias_ref)):
        wide[0:1, 0:REAL] = source[...].astype(F32)
        ref[...] = jnp.broadcast_to(wide[0:1, 0:LANES], (LANES, LANES)).T[:CH]
    wide[0:1, 0:hidden] = up_bias_row[...].astype(F32)
    up_bias = jnp.broadcast_to(wide[0:1, :], (LANES, 3 * LANES)).T[:HP]
    wide[0:REAL, 0:hidden] = up_ref[...].astype(F32)
    upt = wide[0:CH, 0:HP]
    upt_ref[...] = jnp.concatenate([upt, upt], axis=1).astype(BF16)
    up = wide[0:LANES, :].T[:HP]
    upk_ref[:, 0:LANES] = up.astype(BF16)
    upk_ref[:, LANES:] = jnp.where(lanes(HP) == CH, up_bias, up).astype(BF16)
    wide[0:REAL, 0:hidden] = down_ref[...].astype(F32)
    down = wide[0:LANES, :].T[:HP].astype(BF16)
    dnk_ref[:, 0:LANES] = down
    dnk_ref[:, LANES:] = down

    def clear(r, carry):
        for s in range(2):
            cbf[s, pl.ds(pl.multiple_of(r * CH + CH - 8, 8), 8), :] = jnp.zeros((8, LANES), F32)
        return carry

    lax.fori_loop(0, ROWS, clear, 0)
    taps_copy.wait()

    def row(r):
        return pl.ds(pl.multiple_of(r * CH, 8), CH)

    def active(s):
        here = jnp.logical_and(count_ref[0] > 0, slots_ref[0] == s)
        return jnp.logical_or(here, jnp.logical_and(count_ref[0] > 1, slots_ref[1] == s))

    on = [jnp.where(active(s), 1.0, 0.0) for s in range(2)]

    def widen(part, source, q0, count):
        def group(k, carry):
            lane = lanes(REAL)
            q = q0 + k
            if part:
                col_ramp = ramp(lanes(8).astype(F32)[0:1])
                row_ramps = [
                    ramp(jnp.full((1, LANES), q * 8 + i + 16 - 16 * lat, jnp.int32).astype(F32))
                    for i in range(8)
                ]
            for s in range(2):
                low, turn, rim = ((16, 16, 0), (0, 80, 80))[s]
                in_own = jnp.logical_and(lane >= low, lane < low + 80)
                in_rim = jnp.logical_and(lane >= rim, lane < rim + 16)
                edge = strips[part, s, q].astype(F32)
                for i in range(8):
                    v = pltpu.roll(source(k * 8 + i).astype(F32), turn, 1)
                    e = pltpu.roll(edge, (rim + LANES - 16 * i) % LANES, 1)
                    v = jnp.where(in_own, v, jnp.where(in_rim, e, 0.0))
                    if part:
                        at = pl.ds(pl.multiple_of((q * 8 + i) * CH, 8), REAL)
                        cbf[s, at, :] = v * (row_ramps[i] * col_ramp * on[s])
                    else:
                        at = pl.ds(pl.multiple_of((q * 8 + i + 3) * CH, 8), REAL)
                        xf[s, at, :] = v
            return carry

        lax.fori_loop(0, count, group, 0)

    wait(halos[0])
    widen(0, lambda r: x_ref[r], mine, 8)
    widen(0, lambda r: got[0, r], theirs, 2)

    def band(c, slot, sign):
        i = lax.broadcasted_iota(jnp.int32, (16, LANES), 0)
        j = lanes(16)
        j = jnp.where(j >= 64, j - LANES, j)
        gap = (i - j) * sign + 3
        for a in range(7):
            base = jnp.zeros((16, LANES), F32)
            for b in range(7):
                base = jnp.where(gap == b, taps_ref[a * 7 + b, c], base)
            for m in range(6):
                tile = (base if m == 0 else pltpu.roll(base, 16 * m, 1)).astype(BF16)
                for q in range(2):
                    u = a + q if sign > 0 else q + 6 - a
                    weights[slot, u * LANES + 16 * m : u * LANES + 16 * (m + 1), q * LANES : (q + 1) * LANES] = tile

    def every_other(ref, p, parity, c):
        return ref[p, pl.ds(parity * CH + c, 48, stride=2 * CH), :]

    def moved_rows(slot, kind, u):
        near = u // 2
        return jnp.concatenate(
            [lines[slot, kind, 2 * p + u % 2, near : near + ROWS // 2] for p in range(2)], axis=0
        ).astype(BF16)

    def conv_channel(c, slot):
        band(c, slot, 1)
        for p in range(2):
            for parity in range(2):
                lines[slot, 0, 2 * p + parity] = every_other(xf, p, parity, c)
        for u in range(8):
            data[slot, 0:ROWS, u * LANES : (u + 1) * LANES] = moved_rows(slot, 0, u)
        for q in range(2):
            near = (q + 3) // 2
            v = jnp.concatenate(
                [lines[slot, 0, 2 * p + (q + 3) % 2, near : near + ROWS // 2] for p in range(2)], axis=0
            )
            v = v.T[:SIDE].astype(BF16)
            xt[c, q * SIDE : (q + 1) * SIDE] = jnp.concatenate([v, v], axis=1)
        out = jnp.dot(data[slot, 0:ROWS, :], weights[slot], preferred_element_type=F32)
        for p in range(2):
            for q in range(2):
                conv[p, pl.ds(q * CH + c, ROWS // 2, stride=2 * CH), :] = out[
                    p * (ROWS // 2) : (p + 1) * (ROWS // 2), q * LANES : (q + 1) * LANES
                ]

    def conv_channels(i, carry):
        for slot in range(UNROLL):
            conv_channel(i * UNROLL + slot, slot)
        return carry

    lax.fori_loop(0, REAL // UNROLL, conv_channels, 0)

    wait(halos[1])
    widen(1, lambda r: c_ref[r], mine, 8)
    widen(1, lambda r: got[1, r], theirs, 2)

    def pointwise(index, carry):
        p = index // (ROWS // RB)
        r0 = (index % (ROWS // RB)) * RB
        lane = lanes(CH)
        real = lax.broadcasted_iota(jnp.int32, (CH, LANES), 0) < 77
        gain = gain_ref[...]
        bias = bias_ref[...]
        for half in range(RB // 4):
            rows = [conv[p, row(r0 + half * 4 + i), :] for i in range(4)]
            for k, v in enumerate(pack_rows(rows, lane)):
                at = pl.ds((half * 3 + k) * LANES, LANES)
                mean = jnp.sum(jnp.where(real, v, 0.0), axis=0, keepdims=True) * (1.0 / 77.0)
                cen = jnp.where(real, v - mean, 0.0)
                var = jnp.sum(cen * cen, axis=0, keepdims=True) * (1.0 / 77.0)
                rs = lax.rsqrt(var + 1e-06)
                xh = cen * rs
                xhat[:, at] = xh
                rstd[:, at] = jnp.broadcast_to(rs, (8, LANES))
                hi, lo = halves(xh * gain + bias)
                nk[0:CH, at] = hi
                nk[LANES : LANES + CH, at] = lo
            rows = [cbf[p, row(r0 + half * 4 + i), :] for i in range(4)]
            for k, v in enumerate(pack_rows(rows, lane)):
                at = pl.ds((half * 3 + k) * LANES, LANES)
                hi, lo = halves(v)
                cbk[0:CH, at] = hi
                cbk[LANES : LANES + CH, at] = lo
        def ahead(t):
            at = pl.ds(t * TILE, TILE)
            hid[t % 2] = jnp.dot(upk_ref[...], nk[:, at], preferred_element_type=F32)
            dact[t % 2] = jnp.dot(dnk_ref[...], cbk[:, at], preferred_element_type=F32)

        tiles = CELLS // TILE
        def behind(t):
            at = pl.ds(t * TILE, TILE)
            dnorm[:, at] = jnp.dot(upt_ref[...], dhl[:, at], preferred_element_type=F32)
            if t % 2 == 1:
                two = pl.ds((t - 1) * TILE, 2 * TILE)
                gdn[...] += lax.dot_general(ahl[:, two], cbk[:, two], NT, preferred_element_type=F32)
                gup[...] += lax.dot_general(dhl[:, two], nk[:, two], NT, preferred_element_type=F32)

        ahead(0)
        for t in range(tiles):
            if t + 1 < tiles:
                ahead(t + 1)
            if t:
                behind(t - 1)
            at = pl.ds(t * TILE, TILE)
            for i in range(HP // 16):
                part = pl.ds(i * 16, 16)
                rest = pl.ds(HP + i * 16, 16)
                act, slope = gelu_parts(hid[t % 2, part, :])
                ahl[part, at], ahl[rest, at] = halves(act)
                dhl[part, at], dhl[rest, at] = halves(slope * dact[t % 2, part, :])
        behind(tiles - 1)
        for half in range(RB // 4):
            packed = []
            for k in range(3):
                first = (half * 3 + k) * LANES
                at = pl.ds(first, LANES)
                xh = xhat[:, at]
                dxh = dnorm[:, at] * gain
                m1 = jnp.sum(dxh, axis=0, keepdims=True) * (1.0 / 77.0)
                m2 = jnp.sum(dxh * xh, axis=0, keepdims=True) * (1.0 / 77.0)
                v = (dxh - m1 - xh * m2) * rstd[0:1, at]
                packed.append(jnp.where(real, v, 0.0))
            for i, v in enumerate(unpack_rows(packed, lane)):
                at = row(r0 + half * 4 + i + 3)
                dcv[p, at, :] = v
        return carry

    lax.fori_loop(0, 2 * (ROWS // RB), pointwise, 0)

    for place_at, ref in ((0, gup), (HP, gdn)):
        total = ref[0:HP, :] + ref[HP : 2 * HP, :]
        sum_ref[place_at : place_at + HP, :] = total[:, :LANES] + total[:, LANES:]
    start(spread(sum_ref, PIECE, first, 20))

    def back_channel(c, slot):
        band(c, slot, -1)
        for p in range(2):
            for parity in range(2):
                v = every_other(dcv, p, parity, c)
                hi = v.astype(BF16).astype(F32)
                lines[slot, 0, 2 * p + parity] = hi
                lines[slot, 1, 2 * p + parity] = v - hi
        for u in range(8):
            for k in range(2):
                data[slot, k * ROWS : (k + 1) * ROWS, u * LANES : (u + 1) * LANES] = moved_rows(slot, k, u)
        out = jnp.dot(data[slot], weights[slot], preferred_element_type=F32)
        out = out[:ROWS] + out[ROWS:]
        for p in range(2):
            for q in range(2):
                at = pl.ds(q * CH + c, ROWS // 2, stride=2 * CH)
                cbf[p, at, :] = cbf[p, at, :] + out[
                    p * (ROWS // 2) : (p + 1) * (ROWS // 2), q * LANES : (q + 1) * LANES
                ]
        total = None
        sub = lax.broadcasted_iota(jnp.int32, (8, LANES), 0)
        lane = lanes(8)
        line = jnp.zeros((8, LANES), F32)
        prods = jnp.dot(xt[c], data[slot], preferred_element_type=F32)
        for a in range(7):
            v = None
            for m in range(12):
                here = [
                    prods[q * SIDE + 8 * m : q * SIDE + 8 * (m + 1), u * LANES : (u + 1) * LANES]
                    for q, u in ((0, 6 - a), (1, 7 - a))
                ]
                t = here[0] + here[1]
                if m:
                    t = pltpu.roll(t, LANES - 8 * m, 1)
                v = t if v is None else v + t
            for bit in (1, 2, 4):
                v = jnp.where((sub // bit) % 2 == 1, pltpu.roll(v, LANES - bit, 1), v)
            v = pltpu.roll(v, 3 + 8 * a, 1)
            line = jnp.where(jnp.logical_and(lane >= 8 * a, lane < 8 * a + 7), v, line)
        ksum[pl.ds(c, 1), :] = jnp.sum(line, axis=0, keepdims=True)

    def fold_copies(bufs, base):
        rims, rows, near, corner, above = bufs
        margin = [remote(rows, above, sems, base, (lon, other))]
        sides = []
        for side, peer in ((0, west), (1, east)):
            margin.append(
                remote(
                    rims.at[side, pl.ds(theirs, 2)], corner.at[1 - side], sems, base + 1 + side,
                    (peer, other),
                )
            )
            sides.append(
                remote(rims.at[side, pl.ds(mine, 8)], near.at[1 - side], sems, base + 3 + side, (peer, lat))
            )
        return margin, sides

    def leave(c0, count, bufs, base):
        rims, rows, near, corner, above = bufs
        margin, sides = fold_copies(bufs, base)

        def some(r):
            return pl.ds(pl.multiple_of(r * CH + c0, 8), count)

        def assemble(k, carry):
            lane = lanes(count)
            edge = [jnp.zeros((count, LANES), F32)] * 2
            for i in range(8):
                d0 = cbf[0, some(k * 8 + i), :]
                d1 = cbf[1, some(k * 8 + i), :]
                west_part = jnp.where(lane < 80, pltpu.roll(d0, 112, 1), 0.0)
                east_part = jnp.where(lane >= 48, pltpu.roll(d1, 48, 1), 0.0)
                conv[0, some(k * 8 + i), :] = west_part + east_part
                here = jnp.logical_and(lane >= 16 * i, lane < 16 * i + 16)
                for s, d in ((0, d0), (1, d1)):
                    moved = pltpu.roll(d, (16 * i + LANES - 80 * s) % LANES, 1)
                    edge[s] = jnp.where(here, moved, edge[s])
            for s in range(2):
                rims[s, k] = edge[s].astype(BF16)
            return carry

        lax.fori_loop(theirs, theirs + 2, assemble, 0)

        def narrow_rows(r, carry):
            rows[r] = conv[0, some(theirs * 8 + r), :].astype(BF16)
            return carry

        lax.fori_loop(0, MARGIN, narrow_rows, 0)
        start(margin)
        lax.fori_loop(mine, mine + 8, assemble, 0)
        start(sides)

    def arrive(c0, count, bufs, base):
        rims, rows, near, corner, above = bufs
        margin, sides = fold_copies(bufs, base)

        def added(source, k, i, lane):
            w = pltpu.roll(source[0, k].astype(F32), (LANES - 16 * i) % LANES, 1)
            e = pltpu.roll(source[1, k].astype(F32), 112 - 16 * i, 1)
            return jnp.where(lane < 16, w, jnp.where(lane >= 112, e, 0.0))

        def finish(k, carry):
            lane = lanes(count)
            for i in range(8):
                at = pl.ds(pl.multiple_of(((mine + k) * 8 + i) * CH + c0, 8), count)
                out_ref[k * 8 + i, c0 : c0 + count] = conv[0, at, :] + added(near, k, i, lane)
            return carry

        def finish_corner(k, carry):
            lane = lanes(count)
            for i in range(8):
                add = added(corner, k, i, lane) + above[k * 8 + i].astype(F32)
                out_ref[((1 - lat) * 6 + k) * 8 + i, c0 : c0 + count] += add
            return carry

        wait(sides)
        lax.fori_loop(0, 8, finish, 0)
        wait(margin)
        lax.fori_loop(0, 2, finish_corner, 0)

    bufs_a = (rims_a, rows_a, near_a, corner_a, above_a)
    bufs_b = (rims_b, rows_b, near_b, corner_b, above_b)

    def back_channels(i, carry):
        for slot in range(UNROLL):
            back_channel(i * UNROLL + slot, slot)

        @pl.when(i == 14 // UNROLL)
        def _():
            wait(spread(sum_ref, PIECE, first, 20))
            second[0] = piece_sum(sum_ref, PIECE, first)
            start(across(second, 36))

        @pl.when(i == 33 // UNROLL)
        def _():
            wait(across(second, 36))
            chunk[...] = column_sum(second, PIECE)
            start(collect(chunk, total_ref, PIECE, 44))

        @pl.when(i == (CUT - 1) // UNROLL)
        def _():
            leave(0, CUT, bufs_a, 10)

        return carry

    lax.fori_loop(0, REAL // UNROLL, back_channels, 0)
    start(spread(ksum, 8, kfirst, 60))
    leave(CUT, CH - CUT, bufs_b, 15)
    total_ref[pl.ds(pl.multiple_of(cell * PIECE, 8), PIECE), :] = chunk[...]
    wait(spread(ksum, 8, kfirst, 60))
    ksecond[0] = piece_sum(ksum, 8, kfirst)
    start(across(ksecond, 76))
    arrive(0, CUT, bufs_a, 10)
    wait(across(ksecond, 76))
    kchunk[...] = column_sum(ksecond, 8)
    taps_out_ref[pl.ds(pl.multiple_of(cell * 8, 8), 8), :] = kchunk[...]
    start(collect(kchunk, taps_out_ref, 8, 84))
    arrive(CUT, CH - CUT, bufs_b, 15)
    wait(collect(chunk, total_ref, PIECE, 44))
    wait(collect(kchunk, taps_out_ref, 8, 84))


def patches(count, slots, *arrays):
    smem = pl.BlockSpec(memory_space=pltpu.SMEM)
    vmem = pl.BlockSpec(memory_space=pltpu.VMEM)
    return pl.pallas_call(
        patch_kernel,
        name="patches",
        out_shape=(
            jax.ShapeDtypeStruct((ROWS - MARGIN, CH, LANES), F32),
            jax.ShapeDtypeStruct((2 * HP, LANES), F32),
            jax.ShapeDtypeStruct((TAPS, LANES), F32),
        ),
        in_specs=[smem] * 2 + [vmem] * 8,
        out_specs=(vmem,) * 3,
        scratch_shapes=[
            pltpu.VMEM((2, (ROWS + 16) * CH, LANES), F32),
            pltpu.VMEM((2, ROWS * CH, LANES), F32),
            pltpu.VMEM((2, ROWS * CH, LANES), F32),
            pltpu.VMEM((2, (ROWS + 16) * CH, LANES), F32),
            pltpu.VMEM((2 * LANES, CELLS), BF16),
            pltpu.VMEM((2 * LANES, CELLS), BF16),
            pltpu.VMEM((CH, CELLS), F32),
            pltpu.VMEM((8, CELLS), F32),
            pltpu.VMEM((CH, CELLS), F32),
            pltpu.VMEM((2, HP, TILE), F32),
            pltpu.VMEM((2, HP, TILE), F32),
            pltpu.VMEM((2 * HP, CELLS), BF16),
            pltpu.VMEM((2 * HP, CELLS), BF16),
            pltpu.VMEM((2 * HP, 2 * LANES), F32),
            pltpu.VMEM((2 * HP, 2 * LANES), F32),
            pltpu.VMEM((UNROLL, 8 * LANES, 2 * LANES), BF16),
            pltpu.VMEM((UNROLL, 2 * ROWS, 8 * LANES), BF16),
            pltpu.VMEM((UNROLL, 2, 4, 48, LANES), F32),
            pltpu.VMEM((REAL, 2 * SIDE, 2 * ROWS), BF16),
            pltpu.VMEM((CH, LANES), F32),
            pltpu.VMEM((CH, LANES), F32),
            pltpu.VMEM((HP, 2 * LANES), BF16),
            pltpu.VMEM((HP, 2 * LANES), BF16),
            pltpu.VMEM((CH, 2 * HP), BF16),
            pltpu.VMEM((HP, 3 * LANES), F32),
            pltpu.VMEM((56, LANES), F32),
            pltpu.SMEM((56, LANES), F32),
            pltpu.SemaphoreType.DMA,
            pltpu.VMEM((2, 2, 8, REAL, LANES), BF16),
            pltpu.VMEM((2, MARGIN, REAL, LANES), BF16),
            pltpu.VMEM((2, 2, ROWS // 8, REAL, LANES), BF16),
            *(
                pltpu.VMEM((*lead, count, LANES), BF16)
                for count in (CUT, CH - CUT)
                for lead in ((2, ROWS // 8), (MARGIN,), (2, 8), (2, 2), (MARGIN,))
            ),
            pltpu.VMEM((2 * HP, LANES), F32),
            pltpu.VMEM((16, PIECE, LANES), F32),
            pltpu.VMEM((8, PIECE, LANES), F32),
            pltpu.VMEM((PIECE, LANES), F32),
            pltpu.VMEM((TAPS, LANES), F32),
            pltpu.VMEM((16, 8, LANES), F32),
            pltpu.VMEM((8, 8, LANES), F32),
            pltpu.VMEM((8, LANES), F32),
            pltpu.SemaphoreType.DMA((2, 100)),
        ],
        compiler_params=pltpu.CompilerParams(
            collective_id=0, has_side_effects=True, vmem_limit_bytes=63 * 1024 * 1024
        ),
    )(count, slots, *arrays)


def body(
    state_field, cotangent, land_mask, ocean_slots, ocean_count,
    kernel, norm_gain, norm_bias, up_weight, up_bias, down_weight,
):
    channels, height, breadth = state_field.shape
    hidden = up_weight.shape[0]
    masked = jnp.where(land_mask[None] > 0, cotangent, jnp.zeros_like(cotangent))
    out, total, taps = patches(
        ocean_count.reshape(1), ocean_slots.reshape(2), kernel.T,
        jnp.transpose(state_field, (1, 0, 2)), jnp.transpose(masked, (1, 0, 2)),
        norm_gain[None], norm_bias[None], up_bias[None], up_weight.T, down_weight,
    )
    scale = 1.0 / math.sqrt(height * lax.axis_size("lat") * breadth * lax.axis_size("lon"))
    total = total * scale
    field_grad = jnp.transpose(out, (1, 0, 2))[:channels]
    taps = (taps * scale)[:channels, :56].reshape(channels, 7, 8)
    kernel_grad = taps[:, :, 6::-1].reshape(channels, 49)
    up_grad = total[:hidden, :channels]
    down_grad = total[HP : HP + hidden, :channels].T
    return (field_grad, kernel_grad, up_grad, down_grad)


def solution(mesh):
    in_specs = (
        P(None, "lat", "lon"), P(None, "lat", "lon"), P("lat", "lon"), P("lat", "lon", None),
        P("lat", "lon"), P(), P(), P(), P(), P(), P(),
    )
    out_specs = (P(None, "lat", "lon"), P(), P(), P())
    return jax.shard_map(body, mesh=mesh, in_specs=in_specs, out_specs=out_specs, check_vma=False)
```

```python
import functools
import math

import jax
import jax.numpy as jnp
import numpy as np
from jax import lax
from jax.experimental import pallas as pl
from jax.experimental.pallas import tpu as pltpu
from jax.sharding import PartitionSpec as P

STRIDE = 64
MARGIN = 16
SIDE = 96
ROWS = 80
REAL = 77
CH = 80
PITCH = 88
HP = 320
LANES = 128
RB = 16
CELLS = RB * SIDE
TILE = 256
UNROLL = 7
PIECE = 2 * HP // 16
CUT = 48
TAPS = 128
F32 = jnp.float32
BF16 = jnp.bfloat16

NT = (((1,), (1,)), ((), ()))


def gelu_parts(h):
    cdf = 0.5 * lax.erf(h * math.sqrt(0.5)) + 0.5
    e = jnp.exp2(h * h * (-0.5 / math.log(2.0)))
    return h * cdf, cdf + h * (e * (1.0 / math.sqrt(2.0 * math.pi)))


def halves(v):
    hi = v.astype(BF16)
    lo = (v - hi.astype(F32)).astype(BF16)
    return hi, lo


def pack_rows(rows, lane):
    r1 = pltpu.roll(rows[1], 96, 1)
    r2 = pltpu.roll(rows[2], 64, 1)
    r3 = pltpu.roll(rows[3], 32, 1)
    return (
        jnp.where(lane < 96, rows[0], r1),
        jnp.where(lane < 64, r1, r2),
        jnp.where(lane < 32, r2, r3),
    )


def unpack_rows(packed, lane):
    live = lane < 96
    v0, v1, v2 = packed
    zero = jnp.zeros_like(v0)
    r1 = pltpu.roll(jnp.where(lane < 96, v1, v0), 32, 1)
    r2 = pltpu.roll(jnp.where(lane < 32, v2, v1), 64, 1)
    r3 = pltpu.roll(v2, 96, 1)
    return tuple(jnp.where(live, r, zero) for r in (v0, r1, r2, r3))


def place():
    lon = lax.axis_index("lon")
    lat = lax.axis_index("lat")
    count = lax.axis_size("lon")
    return lon, lat, lax.rem(lon + 1, count), lax.rem(lon + count - 1, count)


def meet(peers):
    barrier = pltpu.get_barrier_semaphore()
    for peer in peers:
        pl.semaphore_signal(barrier, inc=1, device_id=peer, device_id_type=pl.DeviceIdType.MESH)
    pl.semaphore_wait(barrier, len(peers))


def remote(source, target, sems, index, peer):
    return pltpu.make_async_remote_copy(
        src_ref=source,
        dst_ref=target,
        send_sem=sems.at[0, index],
        recv_sem=sems.at[1, index],
        device_id=peer,
        device_id_type=pl.DeviceIdType.MESH,
    )


def ramp(index):
    offset = index + 0.5
    return jnp.minimum(1.0, jnp.minimum(offset / (2.0 * MARGIN), (SIDE - offset) / (2.0 * MARGIN)))


def patch_kernel(
    count_ref, slots_ref, kernel_ref, x_ref, c_ref, gain_row, bias_row, up_bias_row, up_ref, down_ref,
    out_ref, total_ref, taps_out_ref,
    xf, conv, cbf, dcv, nk, cbk, xhat, rstd, dnorm, hid, dact, ahl, dhl, gup, gdn, weights, data,
    lines, xt, gain_ref, bias_ref, upk_ref, dnk_ref, upt_ref, wide, taps, taps_ref, taps_sem,
    edges, got, strips,
    rims_a, rows_a, near_a, corner_a, above_a, rims_b, rows_b, near_b, corner_b, above_b,
    sum_ref, first, second, chunk, ksum, kfirst, ksecond, kchunk, sems,
):
    lon, lat, east, west = place()
    other = 1 - lat
    half = lon // 32
    cell = lax.rem(lon, 32) // 2
    core = lax.rem(lon, 2)
    plane = [(half * 32 + lax.rem(cell + d, 16) * 2 + core, lat) for d in range(1, 16)]
    column = (half * 2 + core) * 2 + lat
    cross = []
    for d in range(1, 8):
        j = lax.rem(column + d, 8)
        cross.append(((j // 4) * 32 + cell * 2 + lax.rem(j // 2, 2), lax.rem(j, 2)))
    near_by = [(east, lat), (west, lat), (lon, other), (east, other), (west, other)]
    meet(near_by + plane + cross)
    mine = lat * 2
    theirs = (1 - lat) * 8

    give = (1 - lat) * 48
    halos = []
    for part, source in ((0, x_ref), (1, c_ref)):
        halo = [remote(source.at[pl.ds(give, 16)], got.at[part], sems, 5 * part, (lon, other))]
        halo[0].start()

        def pack(k, carry):
            lane = lax.broadcasted_iota(jnp.int32, (REAL, LANES), 1)
            acc = [jnp.zeros((REAL, LANES), F32)] * 2
            for i in range(8):
                v = source[k * 8 + i].astype(F32)
                here = jnp.logical_and(lane >= 16 * i, lane < 16 * i + 16)
                for side in range(2):
                    moved = pltpu.roll(v, (16 * i + 16 * side) % LANES, 1)
                    acc[side] = jnp.where(here, moved, acc[side])
            for side in range(2):
                edges[part, side, k] = acc[side].astype(BF16)
            return carry

        lax.fori_loop(0, 8, pack, 0)
        for side, peer in ((0, west), (1, east)):
            halo.append(
                remote(
                    edges.at[part, side], strips.at[part, 1 - side, pl.ds(mine, 8)], sems,
                    5 * part + 1 + side, (peer, lat),
                )
            )
            halo.append(
                remote(
                    edges.at[part, side, pl.ds((1 - lat) * 6, 2)],
                    strips.at[part, 1 - side, pl.ds(lat * 8, 2)],
                    sems, 5 * part + 3 + side, (peer, other),
                )
            )
        for copy in halo[1:]:
            copy.start()
        halos.append(halo)

    taps[...] = jnp.zeros(taps.shape, F32)
    taps[0:49, 0:REAL] = kernel_ref[...].astype(F32)
    taps_copy = pltpu.make_async_copy(taps, taps_ref, taps_sem)
    taps_copy.start()

    def spread(source, size, slots, base):
        return [
            remote(
                source.at[pl.ds(pl.multiple_of(lax.rem(cell + d, 16) * size, 8), size)],
                slots.at[d], sems, base + d, plane[d - 1],
            )
            for d in range(1, 16)
        ]

    def across(slots, base):
        return [remote(slots.at[0], slots.at[d], sems, base + d, cross[d - 1]) for d in range(1, 8)]

    def collect(source, target, size, base):
        here = pl.ds(pl.multiple_of(cell * size, 8), size)
        return [
            remote(source, target.at[here], sems, base + d, plane[d - 1]) for d in range(1, 16)
        ]

    def start(copies):
        for copy in copies:
            copy.start()

    def wait(copies):
        for copy in copies:
            copy.wait()

    def piece_sum(source, size, slots):
        part = source[pl.ds(pl.multiple_of(cell * size, 8), size), :]
        for d in range(1, 16):
            part = part + slots[d]
        return part

    def column_sum(slots, size):
        whole = jnp.zeros((size, LANES), F32)
        for j in range(8):
            whole = whole + slots[lax.rem(column - j + 8, 8)]
        return whole

    ksum[...] = jnp.zeros(ksum.shape, F32)
    gup[...] = jnp.zeros(gup.shape, F32)
    gdn[...] = jnp.zeros(gdn.shape, F32)
    for ref in (xf, dcv):
        for p in range(2):
            ref[p, 0 : 3 * PITCH] = jnp.zeros((3 * PITCH, LANES), F32)
            ref[p, (ROWS + 3) * PITCH :] = jnp.zeros((5 * PITCH, LANES), F32)
    weights[...] = jnp.zeros(weights.shape, BF16)
    nk[CH:LANES, :] = jnp.zeros((LANES - CH, CELLS), BF16)
    cbk[CH:LANES, :] = jnp.zeros((LANES - CH, CELLS), BF16)
    cbk[LANES + CH :, :] = jnp.zeros((LANES - CH, CELLS), BF16)
    ones = lax.broadcasted_iota(jnp.int32, (LANES - CH, CELLS), 0) == 0
    nk[LANES + CH :, :] = jnp.where(ones, 1.0, 0.0).astype(BF16)

    def lanes(n):
        return lax.broadcasted_iota(jnp.int32, (n, LANES), 1)

    hidden = up_bias_row.shape[1]
    wide[...] = jnp.zeros(wide.shape, F32)
    for source, ref in ((gain_row, gain_ref), (bias_row, bias_ref)):
        wide[0:1, 0:REAL] = source[...].astype(F32)
        ref[...] = jnp.broadcast_to(wide[0:1, 0:LANES], (LANES, LANES)).T[:CH]
    wide[0:1, 0:hidden] = up_bias_row[...].astype(F32)
    up_bias = jnp.broadcast_to(wide[0:1, :], (LANES, 3 * LANES)).T[:HP]
    wide[0:REAL, 0:hidden] = up_ref[...].astype(F32)
    upt = wide[0:CH, 0:HP]
    upt_ref[...] = jnp.concatenate([upt, upt], axis=1).astype(BF16)
    up = wide[0:LANES, :].T[:HP]
    upk_ref[:, 0:LANES] = up.astype(BF16)
    upk_ref[:, LANES:] = jnp.where(lanes(HP) == CH, up_bias, up).astype(BF16)
    wide[0:REAL, 0:hidden] = down_ref[...].astype(F32)
    down = wide[0:LANES, :].T[:HP].astype(BF16)
    dnk_ref[:, 0:LANES] = down
    dnk_ref[:, LANES:] = down

    def clear(r, carry):
        for s in range(2):
            cbf[s, pl.ds(pl.multiple_of(r * PITCH + CH - 8, 8), 8), :] = jnp.zeros((8, LANES), F32)
        return carry

    lax.fori_loop(0, ROWS, clear, 0)
    taps_copy.wait()

    def row(r):
        return pl.ds(pl.multiple_of(r * PITCH, 8), CH)

    def active(s):
        here = jnp.logical_and(count_ref[0] > 0, slots_ref[0] == s)
        return jnp.logical_or(here, jnp.logical_and(count_ref[0] > 1, slots_ref[1] == s))

    on = [jnp.where(active(s), 1.0, 0.0) for s in range(2)]

    def widen(part, source, q0, count):
        def group(k, carry):
            lane = lanes(REAL)
            q = q0 + k
            if part:
                col_ramp = ramp(lanes(8).astype(F32)[0:1])
                row_ramps = [
                    ramp(jnp.full((1, LANES), q * 8 + i + 16 - 16 * lat, jnp.int32).astype(F32))
                    for i in range(8)
                ]
            for s in range(2):
                low, turn, rim = ((16, 16, 0), (0, 80, 80))[s]
                in_own = jnp.logical_and(lane >= low, lane < low + 80)
                in_rim = jnp.logical_and(lane >= rim, lane < rim + 16)
                edge = strips[part, s, q].astype(F32)
                for i in range(8):
                    v = pltpu.roll(source(k * 8 + i).astype(F32), turn, 1)
                    e = pltpu.roll(edge, (rim + LANES - 16 * i) % LANES, 1)
                    v = jnp.where(in_own, v, jnp.where(in_rim, e, 0.0))
                    if part:
                        at = pl.ds(pl.multiple_of((q * 8 + i) * PITCH, 8), REAL)
                        cbf[s, at, :] = v * (row_ramps[i] * col_ramp * on[s])
                    else:
                        at = pl.ds(pl.multiple_of((q * 8 + i + 3) * PITCH, 8), REAL)
                        xf[s, at, :] = v
            return carry

        lax.fori_loop(0, count, group, 0)

    wait(halos[0])
    widen(0, lambda r: x_ref[r], mine, 8)
    widen(0, lambda r: got[0, r], theirs, 2)

    def band(c, slot, sign):
        i = lax.broadcasted_iota(jnp.int32, (16, LANES), 0)
        j = lanes(16)
        j = jnp.where(j >= 64, j - LANES, j)
        gap = (i - j) * sign + 3
        for a in range(7):
            base = jnp.zeros((16, LANES), F32)
            for b in range(7):
                base = jnp.where(gap == b, taps_ref[a * 7 + b, c], base)
            for m in range(6):
                tile = (base if m == 0 else pltpu.roll(base, 16 * m, 1)).astype(BF16)
                for q in range(2):
                    u = a + q if sign > 0 else q + 6 - a
                    weights[slot, u * LANES + 16 * m : u * LANES + 16 * (m + 1), q * LANES : (q + 1) * LANES] = tile

    def every_other(ref, p, parity, c):
        return ref[p, pl.ds(parity * PITCH + c, 44, stride=2 * PITCH), :]

    def moved_rows(slot, kind, u):
        near = u // 2
        return jnp.concatenate(
            [lines[slot, kind, 2 * p + u % 2, near : near + ROWS // 2] for p in range(2)], axis=0
        ).astype(BF16)

    def conv_channel(c, slot):
        band(c, slot, 1)
        for p in range(2):
            for parity in range(2):
                lines[slot, 0, 2 * p + parity, 0:44] = every_other(xf, p, parity, c)
        for u in range(8):
            data[slot, 0:ROWS, u * LANES : (u + 1) * LANES] = moved_rows(slot, 0, u)
        for q in range(2):
            near = (q + 3) // 2
            v = jnp.concatenate(
                [lines[slot, 0, 2 * p + (q + 3) % 2, near : near + ROWS // 2] for p in range(2)], axis=0
            )
            v = v.T[:SIDE].astype(BF16)
            xt[c, q * SIDE : (q + 1) * SIDE] = v
        out = jnp.dot(data[slot, 0:ROWS, :], weights[slot], preferred_element_type=F32)
        for p in range(2):
            for q in range(2):
                conv[p, pl.ds(q * PITCH + c, ROWS // 2, stride=2 * PITCH), :] = out[
                    p * (ROWS // 2) : (p + 1) * (ROWS // 2), q * LANES : (q + 1) * LANES
                ]

    def conv_channels(i, carry):
        for slot in range(UNROLL):
            conv_channel(i * UNROLL + slot, slot)
        return carry

    lax.fori_loop(0, REAL // UNROLL, conv_channels, 0)

    wait(halos[1])
    widen(1, lambda r: c_ref[r], mine, 8)
    widen(1, lambda r: got[1, r], theirs, 2)

    def pointwise(index, carry):
        p = index // (ROWS // RB)
        r0 = (index % (ROWS // RB)) * RB
        lane = lanes(CH)
        real = lax.broadcasted_iota(jnp.int32, (CH, LANES), 0) < 77
        gain = gain_ref[...]
        bias = bias_ref[...]
        for half in range(RB // 4):
            rows = [conv[p, row(r0 + half * 4 + i), :] for i in range(4)]
            for k, v in enumerate(pack_rows(rows, lane)):
                at = pl.ds((half * 3 + k) * LANES, LANES)
                mean = jnp.sum(jnp.where(real, v, 0.0), axis=0, keepdims=True) * (1.0 / 77.0)
                cen = jnp.where(real, v - mean, 0.0)
                var = jnp.sum(cen * cen, axis=0, keepdims=True) * (1.0 / 77.0)
                rs = lax.rsqrt(var + 1e-06)
                xh = cen * rs
                xhat[:, at] = xh
                rstd[:, at] = jnp.broadcast_to(rs, (8, LANES))
                hi, lo = halves(xh * gain + bias)
                nk[0:CH, at] = hi
                nk[LANES : LANES + CH, at] = lo
            rows = [cbf[p, row(r0 + half * 4 + i), :] for i in range(4)]
            for k, v in enumerate(pack_rows(rows, lane)):
                at = pl.ds((half * 3 + k) * LANES, LANES)
                hi, lo = halves(v)
                cbk[0:CH, at] = hi
                cbk[LANES : LANES + CH, at] = lo
        def ahead(t):
            at = pl.ds(t * TILE, TILE)
            hid[t % 2] = jnp.dot(upk_ref[...], nk[:, at], preferred_element_type=F32)
            dact[t % 2] = jnp.dot(dnk_ref[...], cbk[:, at], preferred_element_type=F32)

        tiles = CELLS // TILE
        def behind(t):
            at = pl.ds(t * TILE, TILE)
            dnorm[:, at] = jnp.dot(upt_ref[...], dhl[:, at], preferred_element_type=F32)
            if t % 2 == 1:
                two = pl.ds((t - 1) * TILE, 2 * TILE)
                gdn[...] += lax.dot_general(ahl[:, two], cbk[:, two], NT, preferred_element_type=F32)
                gup[...] += lax.dot_general(dhl[:, two], nk[:, two], NT, preferred_element_type=F32)

        ahead(0)
        for t in range(tiles):
            if t + 1 < tiles:
                ahead(t + 1)
            if t:
                behind(t - 1)
            at = pl.ds(t * TILE, TILE)
            for i in range(HP // 16):
                part = pl.ds(i * 16, 16)
                rest = pl.ds(HP + i * 16, 16)
                act, slope = gelu_parts(hid[t % 2, part, :])
                ahl[part, at], ahl[rest, at] = halves(act)
                dhl[part, at], dhl[rest, at] = halves(slope * dact[t % 2, part, :])
        behind(tiles - 1)
        for half in range(RB // 4):
            packed = []
            for k in range(3):
                first = (half * 3 + k) * LANES
                at = pl.ds(first, LANES)
                xh = xhat[:, at]
                dxh = dnorm[:, at] * gain
                m1 = jnp.sum(dxh, axis=0, keepdims=True) * (1.0 / 77.0)
                m2 = jnp.sum(dxh * xh, axis=0, keepdims=True) * (1.0 / 77.0)
                v = (dxh - m1 - xh * m2) * rstd[0:1, at]
                packed.append(jnp.where(real, v, 0.0))
            for i, v in enumerate(unpack_rows(packed, lane)):
                at = row(r0 + half * 4 + i + 3)
                dcv[p, at, :] = v
        return carry

    lax.fori_loop(0, 2 * (ROWS // RB), pointwise, 0)

    for place_at, ref in ((0, gup), (HP, gdn)):
        total = ref[0:HP, :] + ref[HP : 2 * HP, :]
        sum_ref[place_at : place_at + HP, :] = total[:, :LANES] + total[:, LANES:]
    start(spread(sum_ref, PIECE, first, 20))

    def back_channel(c, slot):
        band(c, slot, -1)
        for p in range(2):
            for parity in range(2):
                v = every_other(dcv, p, parity, c)
                hi = v.astype(BF16).astype(F32)
                lines[slot, 0, 2 * p + parity, 0:44] = hi
                lines[slot, 1, 2 * p + parity, 0:44] = v - hi
        for u in range(8):
            for k in range(2):
                data[slot, k * ROWS : (k + 1) * ROWS, u * LANES : (u + 1) * LANES] = moved_rows(slot, k, u)
        out = jnp.dot(data[slot], weights[slot], preferred_element_type=F32)
        out = out[:ROWS] + out[ROWS:]
        for p in range(2):
            for q in range(2):
                at = pl.ds(q * PITCH + c, ROWS // 2, stride=2 * PITCH)
                cbf[p, at, :] = cbf[p, at, :] + out[
                    p * (ROWS // 2) : (p + 1) * (ROWS // 2), q * LANES : (q + 1) * LANES
                ]
        total = None
        sub = lax.broadcasted_iota(jnp.int32, (8, LANES), 0)
        lane = lanes(8)
        line = jnp.zeros((8, LANES), F32)
        pair = jnp.concatenate([xt[c], xt[c]], axis=1)
        prods = jnp.dot(pair, data[slot], preferred_element_type=F32)
        for a in range(7):
            v = None
            for m in range(12):
                here = [
                    prods[q * SIDE + 8 * m : q * SIDE + 8 * (m + 1), u * LANES : (u + 1) * LANES]
                    for q, u in ((0, 6 - a), (1, 7 - a))
                ]
                t = here[0] + here[1]
                if m:
                    t = pltpu.roll(t, LANES - 8 * m, 1)
                v = t if v is None else v + t
            for bit in (1, 2, 4):
                v = jnp.where((sub // bit) % 2 == 1, pltpu.roll(v, LANES - bit, 1), v)
            v = pltpu.roll(v, 3 + 8 * a, 1)
            line = jnp.where(jnp.logical_and(lane >= 8 * a, lane < 8 * a + 7), v, line)
        ksum[pl.ds(c, 1), :] = jnp.sum(line, axis=0, keepdims=True)

    def fold_copies(bufs, base):
        rims, rows, near, corner, above = bufs
        margin = [remote(rows, above, sems, base, (lon, other))]
        sides = []
        for side, peer in ((0, west), (1, east)):
            margin.append(
                remote(
                    rims.at[side, pl.ds(theirs, 2)], corner.at[1 - side], sems, base + 1 + side,
                    (peer, other),
                )
            )
            sides.append(
                remote(rims.at[side, pl.ds(mine, 8)], near.at[1 - side], sems, base + 3 + side, (peer, lat))
            )
        return margin, sides

    def leave(c0, count, bufs, base):
        rims, rows, near, corner, above = bufs
        margin, sides = fold_copies(bufs, base)

        def some(r):
            return pl.ds(pl.multiple_of(r * PITCH + c0, 8), count)

        def assemble(k, carry):
            lane = lanes(count)
            edge = [jnp.zeros((count, LANES), F32)] * 2
            for i in range(8):
                d0 = cbf[0, some(k * 8 + i), :]
                d1 = cbf[1, some(k * 8 + i), :]
                west_part = jnp.where(lane < 80, pltpu.roll(d0, 112, 1), 0.0)
                east_part = jnp.where(lane >= 48, pltpu.roll(d1, 48, 1), 0.0)
                conv[0, some(k * 8 + i), :] = west_part + east_part
                here = jnp.logical_and(lane >= 16 * i, lane < 16 * i + 16)
                for s, d in ((0, d0), (1, d1)):
                    moved = pltpu.roll(d, (16 * i + LANES - 80 * s) % LANES, 1)
                    edge[s] = jnp.where(here, moved, edge[s])
            for s in range(2):
                rims[s, k] = edge[s].astype(BF16)
            return carry

        lax.fori_loop(theirs, theirs + 2, assemble, 0)

        def narrow_rows(r, carry):
            rows[r] = conv[0, some(theirs * 8 + r), :].astype(BF16)
            return carry

        lax.fori_loop(0, MARGIN, narrow_rows, 0)
        start(margin)
        lax.fori_loop(mine, mine + 8, assemble, 0)
        start(sides)

    def arrive(c0, count, bufs, base):
        rims, rows, near, corner, above = bufs
        margin, sides = fold_copies(bufs, base)

        def added(source, k, i, lane):
            w = pltpu.roll(source[0, k].astype(F32), (LANES - 16 * i) % LANES, 1)
            e = pltpu.roll(source[1, k].astype(F32), 112 - 16 * i, 1)
            return jnp.where(lane < 16, w, jnp.where(lane >= 112, e, 0.0))

        def finish(k, carry):
            lane = lanes(count)
            for i in range(8):
                at = pl.ds(pl.multiple_of(((mine + k) * 8 + i) * PITCH + c0, 8), count)
                out_ref[k * 8 + i, c0 : c0 + count] = conv[0, at, :] + added(near, k, i, lane)
            return carry

        def finish_corner(k, carry):
            lane = lanes(count)
            for i in range(8):
                add = added(corner, k, i, lane) + above[k * 8 + i].astype(F32)
                out_ref[((1 - lat) * 6 + k) * 8 + i, c0 : c0 + count] += add
            return carry

        wait(sides)
        lax.fori_loop(0, 8, finish, 0)
        wait(margin)
        lax.fori_loop(0, 2, finish_corner, 0)

    bufs_a = (rims_a, rows_a, near_a, corner_a, above_a)
    bufs_b = (rims_b, rows_b, near_b, corner_b, above_b)

    def back_channels(i, carry):
        for slot in range(UNROLL):
            back_channel(i * UNROLL + slot, slot)

        @pl.when(i == 14 // UNROLL)
        def _():
            wait(spread(sum_ref, PIECE, first, 20))
            second[0] = piece_sum(sum_ref, PIECE, first)
            start(across(second, 36))

        @pl.when(i == 33 // UNROLL)
        def _():
            wait(across(second, 36))
            chunk[...] = column_sum(second, PIECE)
            start(collect(chunk, total_ref, PIECE, 44))

        @pl.when(i == (CUT - 1) // UNROLL)
        def _():
            leave(0, CUT, bufs_a, 10)

        return carry

    lax.fori_loop(0, REAL // UNROLL, back_channels, 0)
    start(spread(ksum, 8, kfirst, 60))
    leave(CUT, CH - CUT, bufs_b, 15)
    total_ref[pl.ds(pl.multiple_of(cell * PIECE, 8), PIECE), :] = chunk[...]
    wait(spread(ksum, 8, kfirst, 60))
    ksecond[0] = piece_sum(ksum, 8, kfirst)
    start(across(ksecond, 76))
    arrive(0, CUT, bufs_a, 10)
    wait(across(ksecond, 76))
    kchunk[...] = column_sum(ksecond, 8)
    taps_out_ref[pl.ds(pl.multiple_of(cell * 8, 8), 8), :] = kchunk[...]
    start(collect(kchunk, taps_out_ref, 8, 84))
    arrive(CUT, CH - CUT, bufs_b, 15)
    wait(collect(chunk, total_ref, PIECE, 44))
    wait(collect(kchunk, taps_out_ref, 8, 84))


def patches(count, slots, *arrays):
    smem = pl.BlockSpec(memory_space=pltpu.SMEM)
    vmem = pl.BlockSpec(memory_space=pltpu.VMEM)
    return pl.pallas_call(
        patch_kernel,
        name="patches",
        out_shape=(
            jax.ShapeDtypeStruct((ROWS - MARGIN, CH, LANES), F32),
            jax.ShapeDtypeStruct((2 * HP, LANES), F32),
            jax.ShapeDtypeStruct((TAPS, LANES), F32),
        ),
        in_specs=[smem] * 2 + [vmem] * 8,
        out_specs=(vmem,) * 3,
        scratch_shapes=[
            pltpu.VMEM((2, (ROWS + 8) * PITCH, LANES), F32),
            pltpu.VMEM((2, ROWS * PITCH, LANES), F32),
            pltpu.VMEM((2, ROWS * PITCH, LANES), F32),
            pltpu.VMEM((2, (ROWS + 8) * PITCH, LANES), F32),
            pltpu.VMEM((2 * LANES, CELLS), BF16),
            pltpu.VMEM((2 * LANES, CELLS), BF16),
            pltpu.VMEM((CH, CELLS), F32),
            pltpu.VMEM((8, CELLS), F32),
            pltpu.VMEM((CH, CELLS), F32),
            pltpu.VMEM((2, HP, TILE), F32),
            pltpu.VMEM((2, HP, TILE), F32),
            pltpu.VMEM((2 * HP, CELLS), BF16),
            pltpu.VMEM((2 * HP, CELLS), BF16),
            pltpu.VMEM((2 * HP, 2 * LANES), F32),
            pltpu.VMEM((2 * HP, 2 * LANES), F32),
            pltpu.VMEM((UNROLL, 8 * LANES, 2 * LANES), BF16),
            pltpu.VMEM((UNROLL, 2 * ROWS, 8 * LANES), BF16),
            pltpu.VMEM((UNROLL, 2, 4, 48, LANES), F32),
            pltpu.VMEM((REAL, 2 * SIDE, ROWS), BF16),
            pltpu.VMEM((CH, LANES), F32),
            pltpu.VMEM((CH, LANES), F32),
            pltpu.VMEM((HP, 2 * LANES), BF16),
            pltpu.VMEM((HP, 2 * LANES), BF16),
            pltpu.VMEM((CH, 2 * HP), BF16),
            pltpu.VMEM((HP, 3 * LANES), F32),
            pltpu.VMEM((56, LANES), F32),
            pltpu.SMEM((56, LANES), F32),
            pltpu.SemaphoreType.DMA,
            pltpu.VMEM((2, 2, 8, REAL, LANES), BF16),
            pltpu.VMEM((2, MARGIN, REAL, LANES), BF16),
            pltpu.VMEM((2, 2, ROWS // 8, REAL, LANES), BF16),
            *(
                pltpu.VMEM((*lead, count, LANES), BF16)
                for count in (CUT, CH - CUT)
                for lead in ((2, ROWS // 8), (MARGIN,), (2, 8), (2, 2), (MARGIN,))
            ),
            pltpu.VMEM((2 * HP, LANES), F32),
            pltpu.VMEM((16, PIECE, LANES), F32),
            pltpu.VMEM((8, PIECE, LANES), F32),
            pltpu.VMEM((PIECE, LANES), F32),
            pltpu.VMEM((TAPS, LANES), F32),
            pltpu.VMEM((16, 8, LANES), F32),
            pltpu.VMEM((8, 8, LANES), F32),
            pltpu.VMEM((8, LANES), F32),
            pltpu.SemaphoreType.DMA((2, 100)),
        ],
        compiler_params=pltpu.CompilerParams(
            collective_id=0, has_side_effects=True, vmem_limit_bytes=63 * 1024 * 1024
        ),
    )(count, slots, *arrays)


def body(
    state_field, cotangent, land_mask, ocean_slots, ocean_count,
    kernel, norm_gain, norm_bias, up_weight, up_bias, down_weight,
):
    channels, height, breadth = state_field.shape
    hidden = up_weight.shape[0]
    masked = jnp.where(land_mask[None] > 0, cotangent, jnp.zeros_like(cotangent))
    out, total, taps = patches(
        ocean_count.reshape(1), ocean_slots.reshape(2), kernel.T,
        jnp.transpose(state_field, (1, 0, 2)), jnp.transpose(masked, (1, 0, 2)),
        norm_gain[None], norm_bias[None], up_bias[None], up_weight.T, down_weight,
    )
    scale = 1.0 / math.sqrt(height * lax.axis_size("lat") * breadth * lax.axis_size("lon"))
    total = total * scale
    field_grad = jnp.transpose(out, (1, 0, 2))[:channels]
    taps = (taps * scale)[:channels, :56].reshape(channels, 7, 8)
    kernel_grad = taps[:, :, 6::-1].reshape(channels, 49)
    up_grad = total[:hidden, :channels]
    down_grad = total[HP : HP + hidden, :channels].T
    return (field_grad, kernel_grad, up_grad, down_grad)


def solution(mesh):
    in_specs = (
        P(None, "lat", "lon"), P(None, "lat", "lon"), P("lat", "lon"), P("lat", "lon", None),
        P("lat", "lon"), P(), P(), P(), P(), P(), P(),
    )
    out_specs = (P(None, "lat", "lon"), P(), P(), P())
    return jax.shard_map(body, mesh=mesh, in_specs=in_specs, out_specs=out_specs, check_vma=False)
```

```python
import functools
import math

import jax
import jax.numpy as jnp
import numpy as np
from jax import lax
from jax.experimental import pallas as pl
from jax.experimental.pallas import tpu as pltpu
from jax.sharding import PartitionSpec as P

STRIDE = 64
MARGIN = 16
SIDE = 96
ROWS = 80
REAL = 77
CH = 80
PITCH = 88
HP = 320
LANES = 128
RB = 16
CELLS = RB * SIDE
TILE = 256
UNROLL = 11
PIECE = 2 * HP // 16
CUT = 48
TAPS = 128
F32 = jnp.float32
BF16 = jnp.bfloat16

NT = (((1,), (1,)), ((), ()))


def gelu_parts(h):
    cdf = 0.5 * lax.erf(h * math.sqrt(0.5)) + 0.5
    e = jnp.exp2(h * h * (-0.5 / math.log(2.0)))
    return h * cdf, cdf + h * (e * (1.0 / math.sqrt(2.0 * math.pi)))


def halves(v):
    hi = v.astype(BF16)
    lo = (v - hi.astype(F32)).astype(BF16)
    return hi, lo


def pack_rows(rows, lane):
    r1 = pltpu.roll(rows[1], 96, 1)
    r2 = pltpu.roll(rows[2], 64, 1)
    r3 = pltpu.roll(rows[3], 32, 1)
    return (
        jnp.where(lane < 96, rows[0], r1),
        jnp.where(lane < 64, r1, r2),
        jnp.where(lane < 32, r2, r3),
    )


def unpack_rows(packed, lane):
    live = lane < 96
    v0, v1, v2 = packed
    zero = jnp.zeros_like(v0)
    r1 = pltpu.roll(jnp.where(lane < 96, v1, v0), 32, 1)
    r2 = pltpu.roll(jnp.where(lane < 32, v2, v1), 64, 1)
    r3 = pltpu.roll(v2, 96, 1)
    return tuple(jnp.where(live, r, zero) for r in (v0, r1, r2, r3))


def place():
    lon = lax.axis_index("lon")
    lat = lax.axis_index("lat")
    count = lax.axis_size("lon")
    return lon, lat, lax.rem(lon + 1, count), lax.rem(lon + count - 1, count)


def meet(peers):
    barrier = pltpu.get_barrier_semaphore()
    for peer in peers:
        pl.semaphore_signal(barrier, inc=1, device_id=peer, device_id_type=pl.DeviceIdType.MESH)
    pl.semaphore_wait(barrier, len(peers))


def remote(source, target, sems, index, peer):
    return pltpu.make_async_remote_copy(
        src_ref=source,
        dst_ref=target,
        send_sem=sems.at[0, index],
        recv_sem=sems.at[1, index],
        device_id=peer,
        device_id_type=pl.DeviceIdType.MESH,
    )


def ramp(index):
    offset = index + 0.5
    return jnp.minimum(1.0, jnp.minimum(offset / (2.0 * MARGIN), (SIDE - offset) / (2.0 * MARGIN)))


def patch_kernel(
    count_ref, slots_ref, kernel_ref, x_ref, c_ref, gain_row, bias_row, up_bias_row, up_ref, down_ref,
    out_ref, total_ref, taps_out_ref,
    xf, conv, cbf, dcv, nk, cbk, xhat, rstd, dnorm, hid, dact, ahl, dhl, gup, gdn, weights, data,
    lines, xt, gain_ref, bias_ref, upk_ref, dnk_ref, upt_ref, wide, taps, taps_ref, taps_sem,
    edges, got, strips,
    rims_a, rows_a, near_a, corner_a, above_a, rims_b, rows_b, near_b, corner_b, above_b,
    sum_ref, first, second, chunk, ksum, kfirst, ksecond, kchunk, sems,
):
    lon, lat, east, west = place()
    other = 1 - lat
    half = lon // 32
    cell = lax.rem(lon, 32) // 2
    core = lax.rem(lon, 2)
    plane = [(half * 32 + lax.rem(cell + d, 16) * 2 + core, lat) for d in range(1, 16)]
    column = (half * 2 + core) * 2 + lat
    cross = []
    for d in range(1, 8):
        j = lax.rem(column + d, 8)
        cross.append(((j // 4) * 32 + cell * 2 + lax.rem(j // 2, 2), lax.rem(j, 2)))
    near_by = [(east, lat), (west, lat), (lon, other), (east, other), (west, other)]
    meet(near_by + plane + cross)
    mine = lat * 2
    theirs = (1 - lat) * 8

    give = (1 - lat) * 48
    halos = []
    for part, source in ((0, x_ref), (1, c_ref)):
        halo = [remote(source.at[pl.ds(give, 16)], got.at[part], sems, 5 * part, (lon, other))]
        halo[0].start()

        def pack(k, carry):
            lane = lax.broadcasted_iota(jnp.int32, (REAL, LANES), 1)
            acc = [jnp.zeros((REAL, LANES), F32)] * 2
            for i in range(8):
                v = source[k * 8 + i].astype(F32)
                here = jnp.logical_and(lane >= 16 * i, lane < 16 * i + 16)
                for side in range(2):
                    moved = pltpu.roll(v, (16 * i + 16 * side) % LANES, 1)
                    acc[side] = jnp.where(here, moved, acc[side])
            for side in range(2):
                edges[part, side, k] = acc[side].astype(BF16)
            return carry

        lax.fori_loop(0, 8, pack, 0)
        for side, peer in ((0, west), (1, east)):
            halo.append(
                remote(
                    edges.at[part, side], strips.at[part, 1 - side, pl.ds(mine, 8)], sems,
                    5 * part + 1 + side, (peer, lat),
                )
            )
            halo.append(
                remote(
                    edges.at[part, side, pl.ds((1 - lat) * 6, 2)],
                    strips.at[part, 1 - side, pl.ds(lat * 8, 2)],
                    sems, 5 * part + 3 + side, (peer, other),
                )
            )
        for copy in halo[1:]:
            copy.start()
        halos.append(halo)

    taps[...] = jnp.zeros(taps.shape, F32)
    taps[0:49, 0:REAL] = kernel_ref[...].astype(F32)
    taps_copy = pltpu.make_async_copy(taps, taps_ref, taps_sem)
    taps_copy.start()

    def spread(source, size, slots, base):
        return [
            remote(
                source.at[pl.ds(pl.multiple_of(lax.rem(cell + d, 16) * size, 8), size)],
                slots.at[d], sems, base + d, plane[d - 1],
            )
            for d in range(1, 16)
        ]

    def across(slots, base):
        return [remote(slots.at[0], slots.at[d], sems, base + d, cross[d - 1]) for d in range(1, 8)]

    def collect(source, target, size, base):
        here = pl.ds(pl.multiple_of(cell * size, 8), size)
        return [
            remote(source, target.at[here], sems, base + d, plane[d - 1]) for d in range(1, 16)
        ]

    def start(copies):
        for copy in copies:
            copy.start()

    def wait(copies):
        for copy in copies:
            copy.wait()

    def piece_sum(source, size, slots):
        part = source[pl.ds(pl.multiple_of(cell * size, 8), size), :]
        for d in range(1, 16):
            part = part + slots[d]
        return part

    def column_sum(slots, size):
        whole = jnp.zeros((size, LANES), F32)
        for j in range(8):
            whole = whole + slots[lax.rem(column - j + 8, 8)]
        return whole

    ksum[...] = jnp.zeros(ksum.shape, F32)
    gup[...] = jnp.zeros(gup.shape, F32)
    gdn[...] = jnp.zeros(gdn.shape, F32)
    for ref in (xf, dcv):
        for p in range(2):
            ref[p, 0 : 3 * PITCH] = jnp.zeros((3 * PITCH, LANES), F32)
            ref[p, (ROWS + 3) * PITCH :] = jnp.zeros((5 * PITCH, LANES), F32)
    weights[...] = jnp.zeros(weights.shape, BF16)
    nk[CH:LANES, :] = jnp.zeros((LANES - CH, CELLS), BF16)
    cbk[CH:LANES, :] = jnp.zeros((LANES - CH, CELLS), BF16)
    cbk[LANES + CH :, :] = jnp.zeros((LANES - CH, CELLS), BF16)
    ones = lax.broadcasted_iota(jnp.int32, (LANES - CH, CELLS), 0) == 0
    nk[LANES + CH :, :] = jnp.where(ones, 1.0, 0.0).astype(BF16)

    def lanes(n):
        return lax.broadcasted_iota(jnp.int32, (n, LANES), 1)

    hidden = up_bias_row.shape[1]
    wide[...] = jnp.zeros(wide.shape, F32)
    for source, ref in ((gain_row, gain_ref), (bias_row, bias_ref)):
        wide[0:1, 0:REAL] = source[...].astype(F32)
        ref[...] = jnp.broadcast_to(wide[0:1, 0:LANES], (LANES, LANES)).T[:CH]
    wide[0:1, 0:hidden] = up_bias_row[...].astype(F32)
    up_bias = jnp.broadcast_to(wide[0:1, :], (LANES, 3 * LANES)).T[:HP]
    wide[0:REAL, 0:hidden] = up_ref[...].astype(F32)
    upt = wide[0:CH, 0:HP]
    upt_ref[...] = jnp.concatenate([upt, upt], axis=1).astype(BF16)
    up = wide[0:LANES, :].T[:HP]
    upk_ref[:, 0:LANES] = up.astype(BF16)
    upk_ref[:, LANES:] = jnp.where(lanes(HP) == CH, up_bias, up).astype(BF16)
    wide[0:REAL, 0:hidden] = down_ref[...].astype(F32)
    down = wide[0:LANES, :].T[:HP].astype(BF16)
    dnk_ref[:, 0:LANES] = down
    dnk_ref[:, LANES:] = down

    def clear(r, carry):
        for s in range(2):
            cbf[s, pl.ds(pl.multiple_of(r * PITCH + CH - 8, 8), 8), :] = jnp.zeros((8, LANES), F32)
        return carry

    lax.fori_loop(0, ROWS, clear, 0)
    taps_copy.wait()

    def row(r):
        return pl.ds(pl.multiple_of(r * PITCH, 8), CH)

    def active(s):
        here = jnp.logical_and(count_ref[0] > 0, slots_ref[0] == s)
        return jnp.logical_or(here, jnp.logical_and(count_ref[0] > 1, slots_ref[1] == s))

    on = [jnp.where(active(s), 1.0, 0.0) for s in range(2)]

    def widen(part, source, q0, count):
        def group(k, carry):
            lane = lanes(REAL)
            q = q0 + k
            if part:
                col_ramp = ramp(lanes(8).astype(F32)[0:1])
                row_ramps = [
                    ramp(jnp.full((1, LANES), q * 8 + i + 16 - 16 * lat, jnp.int32).astype(F32))
                    for i in range(8)
                ]
            for s in range(2):
                low, turn, rim = ((16, 16, 0), (0, 80, 80))[s]
                in_own = jnp.logical_and(lane >= low, lane < low + 80)
                in_rim = jnp.logical_and(lane >= rim, lane < rim + 16)
                edge = strips[part, s, q].astype(F32)
                for i in range(8):
                    v = pltpu.roll(source(k * 8 + i).astype(F32), turn, 1)
                    e = pltpu.roll(edge, (rim + LANES - 16 * i) % LANES, 1)
                    v = jnp.where(in_own, v, jnp.where(in_rim, e, 0.0))
                    if part:
                        at = pl.ds(pl.multiple_of((q * 8 + i) * PITCH, 8), REAL)
                        cbf[s, at, :] = v * (row_ramps[i] * col_ramp * on[s])
                    else:
                        at = pl.ds(pl.multiple_of((q * 8 + i + 3) * PITCH, 8), REAL)
                        xf[s, at, :] = v
            return carry

        lax.fori_loop(0, count, group, 0)

    wait(halos[0])
    widen(0, lambda r: x_ref[r], mine, 8)
    widen(0, lambda r: got[0, r], theirs, 2)

    def band(c, slot, sign):
        i = lax.broadcasted_iota(jnp.int32, (16, LANES), 0)
        j = lanes(16)
        j = jnp.where(j >= 64, j - LANES, j)
        gap = (i - j) * sign + 3
        for a in range(7):
            base = jnp.zeros((16, LANES), F32)
            for b in range(7):
                base = jnp.where(gap == b, taps_ref[a * 7 + b, c], base)
            for m in range(6):
                tile = (base if m == 0 else pltpu.roll(base, 16 * m, 1)).astype(BF16)
                for q in range(2):
                    u = a + q if sign > 0 else q + 6 - a
                    weights[slot, u * LANES + 16 * m : u * LANES + 16 * (m + 1), q * LANES : (q + 1) * LANES] = tile

    def every_other(ref, p, parity, c):
        return ref[p, pl.ds(parity * PITCH + c, 44, stride=2 * PITCH), :]

    def moved_rows(slot, kind, u):
        near = u // 2
        return jnp.concatenate(
            [lines[slot, kind, 2 * p + u % 2, near : near + ROWS // 2] for p in range(2)], axis=0
        ).astype(BF16)

    def conv_channel(c, slot):
        band(c, slot, 1)
        for p in range(2):
            for parity in range(2):
                lines[slot, 0, 2 * p + parity, 0:44] = every_other(xf, p, parity, c)
        for u in range(8):
            data[slot, 0:ROWS, u * LANES : (u + 1) * LANES] = moved_rows(slot, 0, u)
        for q in range(2):
            near = (q + 3) // 2
            v = jnp.concatenate(
                [lines[slot, 0, 2 * p + (q + 3) % 2, near : near + ROWS // 2] for p in range(2)], axis=0
            )
            v = v.T[:SIDE].astype(BF16)
            xt[c, q * SIDE : (q + 1) * SIDE] = v
        out = jnp.dot(data[slot, 0:ROWS, :], weights[slot], preferred_element_type=F32)
        for p in range(2):
            for q in range(2):
                conv[p, pl.ds(q * PITCH + c, ROWS // 2, stride=2 * PITCH), :] = out[
                    p * (ROWS // 2) : (p + 1) * (ROWS // 2), q * LANES : (q + 1) * LANES
                ]

    def conv_channels(i, carry):
        for slot in range(UNROLL):
            conv_channel(i * UNROLL + slot, slot)
        return carry

    lax.fori_loop(0, REAL // UNROLL, conv_channels, 0)

    wait(halos[1])
    widen(1, lambda r: c_ref[r], mine, 8)
    widen(1, lambda r: got[1, r], theirs, 2)

    def pointwise(index, carry):
        p = index // (ROWS // RB)
        r0 = (index % (ROWS // RB)) * RB
        lane = lanes(CH)
        real = lax.broadcasted_iota(jnp.int32, (CH, LANES), 0) < 77
        gain = gain_ref[...]
        bias = bias_ref[...]
        for half in range(RB // 4):
            rows = [conv[p, row(r0 + half * 4 + i), :] for i in range(4)]
            for k, v in enumerate(pack_rows(rows, lane)):
                at = pl.ds((half * 3 + k) * LANES, LANES)
                mean = jnp.sum(jnp.where(real, v, 0.0), axis=0, keepdims=True) * (1.0 / 77.0)
                cen = jnp.where(real, v - mean, 0.0)
                var = jnp.sum(cen * cen, axis=0, keepdims=True) * (1.0 / 77.0)
                rs = lax.rsqrt(var + 1e-06)
                xh = cen * rs
                xhat[:, at] = xh
                rstd[:, at] = jnp.broadcast_to(rs, (8, LANES))
                hi, lo = halves(xh * gain + bias)
                nk[0:CH, at] = hi
                nk[LANES : LANES + CH, at] = lo
            rows = [cbf[p, row(r0 + half * 4 + i), :] for i in range(4)]
            for k, v in enumerate(pack_rows(rows, lane)):
                at = pl.ds((half * 3 + k) * LANES, LANES)
                hi, lo = halves(v)
                cbk[0:CH, at] = hi
                cbk[LANES : LANES + CH, at] = lo
        def ahead(t):
            at = pl.ds(t * TILE, TILE)
            hid[t % 2] = jnp.dot(upk_ref[...], nk[:, at], preferred_element_type=F32)
            dact[t % 2] = jnp.dot(dnk_ref[...], cbk[:, at], preferred_element_type=F32)

        tiles = CELLS // TILE
        def behind(t):
            at = pl.ds(t * TILE, TILE)
            dnorm[:, at] = jnp.dot(upt_ref[...], dhl[:, at], preferred_element_type=F32)
            if t % 2 == 1:
                two = pl.ds((t - 1) * TILE, 2 * TILE)
                gdn[...] += lax.dot_general(ahl[:, two], cbk[:, two], NT, preferred_element_type=F32)
                gup[...] += lax.dot_general(dhl[:, two], nk[:, two], NT, preferred_element_type=F32)

        ahead(0)
        for t in range(tiles):
            if t + 1 < tiles:
                ahead(t + 1)
            if t:
                behind(t - 1)
            at = pl.ds(t * TILE, TILE)
            for i in range(HP // 16):
                part = pl.ds(i * 16, 16)
                rest = pl.ds(HP + i * 16, 16)
                act, slope = gelu_parts(hid[t % 2, part, :])
                ahl[part, at], ahl[rest, at] = halves(act)
                dhl[part, at], dhl[rest, at] = halves(slope * dact[t % 2, part, :])
        behind(tiles - 1)
        for half in range(RB // 4):
            packed = []
            for k in range(3):
                first = (half * 3 + k) * LANES
                at = pl.ds(first, LANES)
                xh = xhat[:, at]
                dxh = dnorm[:, at] * gain
                m1 = jnp.sum(dxh, axis=0, keepdims=True) * (1.0 / 77.0)
                m2 = jnp.sum(dxh * xh, axis=0, keepdims=True) * (1.0 / 77.0)
                v = (dxh - m1 - xh * m2) * rstd[0:1, at]
                packed.append(jnp.where(real, v, 0.0))
            for i, v in enumerate(unpack_rows(packed, lane)):
                at = row(r0 + half * 4 + i + 3)
                dcv[p, at, :] = v
        return carry

    lax.fori_loop(0, 2 * (ROWS // RB), pointwise, 0)

    for place_at, ref in ((0, gup), (HP, gdn)):
        total = ref[0:HP, :] + ref[HP : 2 * HP, :]
        sum_ref[place_at : place_at + HP, :] = total[:, :LANES] + total[:, LANES:]
    start(spread(sum_ref, PIECE, first, 20))

    def back_channel(c, slot):
        band(c, slot, -1)
        for p in range(2):
            for parity in range(2):
                v = every_other(dcv, p, parity, c)
                hi = v.astype(BF16).astype(F32)
                lines[slot, 0, 2 * p + parity, 0:44] = hi
                lines[slot, 1, 2 * p + parity, 0:44] = v - hi
        for u in range(8):
            for k in range(2):
                data[slot, k * ROWS : (k + 1) * ROWS, u * LANES : (u + 1) * LANES] = moved_rows(slot, k, u)
        out = jnp.dot(data[slot], weights[slot], preferred_element_type=F32)
        out = out[:ROWS] + out[ROWS:]
        for p in range(2):
            for q in range(2):
                at = pl.ds(q * PITCH + c, ROWS // 2, stride=2 * PITCH)
                conv[p, at, :] = out[
                    p * (ROWS // 2) : (p + 1) * (ROWS // 2), q * LANES : (q + 1) * LANES
                ]
        total = None
        sub = lax.broadcasted_iota(jnp.int32, (8, LANES), 0)
        lane = lanes(8)
        line = jnp.zeros((8, LANES), F32)
        pair = jnp.concatenate([xt[c], xt[c]], axis=1)
        prods = jnp.dot(pair, data[slot], preferred_element_type=F32)
        for a in range(7):
            v = None
            for m in range(12):
                here = [
                    prods[q * SIDE + 8 * m : q * SIDE + 8 * (m + 1), u * LANES : (u + 1) * LANES]
                    for q, u in ((0, 6 - a), (1, 7 - a))
                ]
                t = here[0] + here[1]
                if m:
                    t = pltpu.roll(t, LANES - 8 * m, 1)
                v = t if v is None else v + t
            for bit in (1, 2, 4):
                v = jnp.where((sub // bit) % 2 == 1, pltpu.roll(v, LANES - bit, 1), v)
            v = pltpu.roll(v, 3 + 8 * a, 1)
            line = jnp.where(jnp.logical_and(lane >= 8 * a, lane < 8 * a + 7), v, line)
        ksum[pl.ds(c, 1), :] = jnp.sum(line, axis=0, keepdims=True)

    def fold_copies(bufs, base):
        rims, rows, near, corner, above = bufs
        margin = [remote(rows, above, sems, base, (lon, other))]
        sides = []
        for side, peer in ((0, west), (1, east)):
            margin.append(
                remote(
                    rims.at[side, pl.ds(theirs, 2)], corner.at[1 - side], sems, base + 1 + side,
                    (peer, other),
                )
            )
            sides.append(
                remote(rims.at[side, pl.ds(mine, 8)], near.at[1 - side], sems, base + 3 + side, (peer, lat))
            )
        return margin, sides

    def leave(c0, count, bufs, base):
        rims, rows, near, corner, above = bufs
        margin, sides = fold_copies(bufs, base)

        def some(r):
            return pl.ds(pl.multiple_of(r * PITCH + c0, 8), count)

        def assemble(k, carry):
            lane = lanes(count)
            edge = [jnp.zeros((count, LANES), F32)] * 2
            for i in range(8):
                d0 = cbf[0, some(k * 8 + i), :] + conv[0, some(k * 8 + i), :]
                d1 = cbf[1, some(k * 8 + i), :] + conv[1, some(k * 8 + i), :]
                west_part = jnp.where(lane < 80, pltpu.roll(d0, 112, 1), 0.0)
                east_part = jnp.where(lane >= 48, pltpu.roll(d1, 48, 1), 0.0)
                conv[0, some(k * 8 + i), :] = west_part + east_part
                here = jnp.logical_and(lane >= 16 * i, lane < 16 * i + 16)
                for s, d in ((0, d0), (1, d1)):
                    moved = pltpu.roll(d, (16 * i + LANES - 80 * s) % LANES, 1)
                    edge[s] = jnp.where(here, moved, edge[s])
            for s in range(2):
                rims[s, k] = edge[s].astype(BF16)
            return carry

        lax.fori_loop(theirs, theirs + 2, assemble, 0)

        def narrow_rows(r, carry):
            rows[r] = conv[0, some(theirs * 8 + r), :].astype(BF16)
            return carry

        lax.fori_loop(0, MARGIN, narrow_rows, 0)
        start(margin)
        lax.fori_loop(mine, mine + 8, assemble, 0)
        start(sides)

    def arrive(c0, count, bufs, base):
        rims, rows, near, corner, above = bufs
        margin, sides = fold_copies(bufs, base)

        def added(source, k, i, lane):
            w = pltpu.roll(source[0, k].astype(F32), (LANES - 16 * i) % LANES, 1)
            e = pltpu.roll(source[1, k].astype(F32), 112 - 16 * i, 1)
            return jnp.where(lane < 16, w, jnp.where(lane >= 112, e, 0.0))

        def finish(k, carry):
            lane = lanes(count)
            for i in range(8):
                at = pl.ds(pl.multiple_of(((mine + k) * 8 + i) * PITCH + c0, 8), count)
                out_ref[k * 8 + i, c0 : c0 + count] = conv[0, at, :] + added(near, k, i, lane)
            return carry

        def finish_corner(k, carry):
            lane = lanes(count)
            for i in range(8):
                add = added(corner, k, i, lane) + above[k * 8 + i].astype(F32)
                out_ref[((1 - lat) * 6 + k) * 8 + i, c0 : c0 + count] += add
            return carry

        wait(sides)
        lax.fori_loop(0, 8, finish, 0)
        wait(margin)
        lax.fori_loop(0, 2, finish_corner, 0)

    bufs_a = (rims_a, rows_a, near_a, corner_a, above_a)
    bufs_b = (rims_b, rows_b, near_b, corner_b, above_b)

    def back_channels(i, carry):
        for slot in range(UNROLL):
            back_channel(i * UNROLL + slot, slot)

        @pl.when(i == 14 // UNROLL)
        def _():
            wait(spread(sum_ref, PIECE, first, 20))
            second[0] = piece_sum(sum_ref, PIECE, first)
            start(across(second, 36))

        @pl.when(i == 33 // UNROLL)
        def _():
            wait(across(second, 36))
            chunk[...] = column_sum(second, PIECE)
            start(collect(chunk, total_ref, PIECE, 44))

        @pl.when(i == (CUT - 1) // UNROLL)
        def _():
            leave(0, CUT, bufs_a, 10)

        return carry

    lax.fori_loop(0, REAL // UNROLL, back_channels, 0)
    start(spread(ksum, 8, kfirst, 60))
    leave(CUT, CH - CUT, bufs_b, 15)
    total_ref[pl.ds(pl.multiple_of(cell * PIECE, 8), PIECE), :] = chunk[...]
    wait(spread(ksum, 8, kfirst, 60))
    ksecond[0] = piece_sum(ksum, 8, kfirst)
    start(across(ksecond, 76))
    arrive(0, CUT, bufs_a, 10)
    wait(across(ksecond, 76))
    kchunk[...] = column_sum(ksecond, 8)
    taps_out_ref[pl.ds(pl.multiple_of(cell * 8, 8), 8), :] = kchunk[...]
    start(collect(kchunk, taps_out_ref, 8, 84))
    arrive(CUT, CH - CUT, bufs_b, 15)
    wait(collect(chunk, total_ref, PIECE, 44))
    wait(collect(kchunk, taps_out_ref, 8, 84))


def patches(count, slots, *arrays):
    smem = pl.BlockSpec(memory_space=pltpu.SMEM)
    vmem = pl.BlockSpec(memory_space=pltpu.VMEM)
    return pl.pallas_call(
        patch_kernel,
        name="patches",
        out_shape=(
            jax.ShapeDtypeStruct((ROWS - MARGIN, CH, LANES), F32),
            jax.ShapeDtypeStruct((2 * HP, LANES), F32),
            jax.ShapeDtypeStruct((TAPS, LANES), F32),
        ),
        in_specs=[smem] * 2 + [vmem] * 8,
        out_specs=(vmem,) * 3,
        scratch_shapes=[
            pltpu.VMEM((2, (ROWS + 8) * PITCH, LANES), F32),
            pltpu.VMEM((2, ROWS * PITCH, LANES), F32),
            pltpu.VMEM((2, ROWS * PITCH, LANES), F32),
            pltpu.VMEM((2, (ROWS + 8) * PITCH, LANES), F32),
            pltpu.VMEM((2 * LANES, CELLS), BF16),
            pltpu.VMEM((2 * LANES, CELLS), BF16),
            pltpu.VMEM((CH, CELLS), F32),
            pltpu.VMEM((8, CELLS), F32),
            pltpu.VMEM((CH, CELLS), F32),
            pltpu.VMEM((2, HP, TILE), F32),
            pltpu.VMEM((2, HP, TILE), F32),
            pltpu.VMEM((2 * HP, CELLS), BF16),
            pltpu.VMEM((2 * HP, CELLS), BF16),
            pltpu.VMEM((2 * HP, 2 * LANES), F32),
            pltpu.VMEM((2 * HP, 2 * LANES), F32),
            pltpu.VMEM((UNROLL, 8 * LANES, 2 * LANES), BF16),
            pltpu.VMEM((UNROLL, 2 * ROWS, 8 * LANES), BF16),
            pltpu.VMEM((UNROLL, 2, 4, 48, LANES), F32),
            pltpu.VMEM((REAL, 2 * SIDE, ROWS), BF16),
            pltpu.VMEM((CH, LANES), F32),
            pltpu.VMEM((CH, LANES), F32),
            pltpu.VMEM((HP, 2 * LANES), BF16),
            pltpu.VMEM((HP, 2 * LANES), BF16),
            pltpu.VMEM((CH, 2 * HP), BF16),
            pltpu.VMEM((HP, 3 * LANES), F32),
            pltpu.VMEM((56, LANES), F32),
            pltpu.SMEM((56, LANES), F32),
            pltpu.SemaphoreType.DMA,
            pltpu.VMEM((2, 2, 8, REAL, LANES), BF16),
            pltpu.VMEM((2, MARGIN, REAL, LANES), BF16),
            pltpu.VMEM((2, 2, ROWS // 8, REAL, LANES), BF16),
            *(
                pltpu.VMEM((*lead, count, LANES), BF16)
                for count in (CUT, CH - CUT)
                for lead in ((2, ROWS // 8), (MARGIN,), (2, 8), (2, 2), (MARGIN,))
            ),
            pltpu.VMEM((2 * HP, LANES), F32),
            pltpu.VMEM((16, PIECE, LANES), F32),
            pltpu.VMEM((8, PIECE, LANES), F32),
            pltpu.VMEM((PIECE, LANES), F32),
            pltpu.VMEM((TAPS, LANES), F32),
            pltpu.VMEM((16, 8, LANES), F32),
            pltpu.VMEM((8, 8, LANES), F32),
            pltpu.VMEM((8, LANES), F32),
            pltpu.SemaphoreType.DMA((2, 100)),
        ],
        compiler_params=pltpu.CompilerParams(
            collective_id=0, has_side_effects=True, vmem_limit_bytes=63 * 1024 * 1024
        ),
    )(count, slots, *arrays)


def body(
    state_field, cotangent, land_mask, ocean_slots, ocean_count,
    kernel, norm_gain, norm_bias, up_weight, up_bias, down_weight,
):
    channels, height, breadth = state_field.shape
    hidden = up_weight.shape[0]
    masked = jnp.where(land_mask[None] > 0, cotangent, jnp.zeros_like(cotangent))
    out, total, taps = patches(
        ocean_count.reshape(1), ocean_slots.reshape(2), kernel.T,
        jnp.transpose(state_field, (1, 0, 2)), jnp.transpose(masked, (1, 0, 2)),
        norm_gain[None], norm_bias[None], up_bias[None], up_weight.T, down_weight,
    )
    scale = 1.0 / math.sqrt(height * lax.axis_size("lat") * breadth * lax.axis_size("lon"))
    total = total * scale
    field_grad = jnp.transpose(out, (1, 0, 2))[:channels]
    taps = (taps * scale)[:channels, :56].reshape(channels, 7, 8)
    kernel_grad = taps[:, :, 6::-1].reshape(channels, 49)
    up_grad = total[:hidden, :channels]
    down_grad = total[HP : HP + hidden, :channels].T
    return (field_grad, kernel_grad, up_grad, down_grad)


def solution(mesh):
    in_specs = (
        P(None, "lat", "lon"), P(None, "lat", "lon"), P("lat", "lon"), P("lat", "lon", None),
        P("lat", "lon"), P(), P(), P(), P(), P(), P(),
    )
    out_specs = (P(None, "lat", "lon"), P(), P(), P())
    return jax.shard_map(body, mesh=mesh, in_specs=in_specs, out_specs=out_specs, check_vma=False)
```
